32 devices in a mesh: expert: 8 (over y, x, core), tensor: 4 (over z).
Axes of the slice: x: 2, y: 2, z: 4, core: 2. Of those that a mesh axis runs over, the one named last changes fastest.
Arguments:
- patches: bfloat16 [3152, 768], P('expert'), may hold values from -6 to 6
- first_gain: float32 [768], replicated, may hold values from 0.5 to 1.5
- first_bias: float32 [768], replicated, may hold values from -1.5 to 1.5
- qkv_weight: bfloat16 [768, 3, 768], P(None, None, 'tensor'), may hold values from -0.3125 to 0.3125
- out_weight: bfloat16 [768, 768], P('tensor'), may hold values from -0.875 to 0.875
- second_gain: float32 [768], replicated, may hold values from 0.5 to 1.5
- second_bias: float32 [768], replicated, may hold values from -1.5 to 1.5
- router_weight: bfloat16 [768, 8], replicated, may hold values from -0.15625 to 0.15625
- up_weight: bfloat16 [8, 768, 3072], P('expert', None, 'tensor'), may hold values from -0.21875 to 0.21875
- down_weight: bfloat16 [8, 3072, 768], P('expert', 'tensor'), may hold values from -0.109375 to 0.109375
- expert_ids: int32 [3152, 2], P('expert'), may hold values from 0 to 7, all different within a row; in each aligned block of 394 rows (0 to 393, 394 to 787, ...) at most 148 rows name the same one
- router_noise: float32 [3152, 2], P('expert'), may hold values from -1.5 to 1.5
- images_live: int32 [8], P('expert'), may hold values from 1 to 2, as said below
- out_grad: bfloat16 [3152, 768], P('expert'), may hold values from -5 to 5
Outputs:
- block_out: bfloat16 [3152, 768], P('expert')
- patches_grad: float32 [3152, 768], P('expert')
- first_gain_grad: float32 [768], P('expert')
- first_bias_grad: float32 [768], P('expert')
- qkv_weight_grad: float32 [768, 3, 768], P('expert', None, 'tensor')
- out_weight_grad: float32 [768, 768], P('tensor', 'expert')
- second_gain_grad: float32 [768], P('expert')
- second_bias_grad: float32 [768], P('expert')
- router_weight_grad: float32 [768, 8], P('expert')
- up_weight_grad: float32 [8, 768, 3072], P('expert', None, 'tensor')
- down_weight_grad: float32 [8, 3072, 768], P('expert', 'tensor')
The draws below stay inside these ranges and needn't reach their ends.
Inputs may be any that keep to these rules, and one draw needn't show every extreme that they name: `expert_ids`: the two experts of a row differ. Among the rows of one group no expert is named more than 148 times, and in every draw some expert is named exactly 148 times by the rows of some group. The first images_live[g] images of group g are in use, the rest are padding; every draw has a group with all 2 images in use and a group with the fewest.
All inputs are finite; a program needn't handle non-finite values.
Results may differ from the reference program's by a relative error of at most 0.015.
Values may be sent and summed in bfloat16 or wider, within the bound.
A program may use at most 128 MiB of HBM per device.

```python
import math
import jax
import jax.numpy as jnp
import numpy as np
from jax import lax

D = 768
HEADS = 12
HEAD_DIM = 64
FF = 3072
TOK_IMG = 197
IMG_DEV = 2
EXPERTS = 8
GROUPS = 8
ROWS_DEV = 394
TOKENS = 3152
CAP = 148


def draw_images_live(key, part):
    key = jax.random.fold_in(key, 7)
    fewest = IMG_DEV - IMG_DEV // 2
    counts = jax.random.randint(jax.random.fold_in(key, 1), (GROUPS,), fewest, IMG_DEV + 1)
    order = jax.random.permutation(jax.random.fold_in(key, 2), GROUPS)
    full_count = jax.random.randint(jax.random.fold_in(key, 3), (), 1, GROUPS)
    rank = jnp.zeros((GROUPS,), jnp.int32).at[order].set(jnp.arange(GROUPS, dtype=jnp.int32))
    counts = jnp.where(rank < full_count, IMG_DEV, counts)
    counts = jnp.where(rank == GROUPS - 1, fewest, counts)
    return counts.astype(jnp.int32)


def with_spikes(values, own_key, source, target, blocks, factor):
    def block_of(dim):
        return (jnp.arange(values.shape[dim]) // (values.shape[dim] // blocks)).reshape((-1,) + (1,) * (values.ndim - 1 - dim))

    first = jax.random.permutation(own_key, blocks)[block_of(target)]
    far = (block_of(target) + blocks // 2) % blocks
    return jnp.where((block_of(source) == first) | (block_of(source) == far), factor * values, values)


def block_scale(stream_key, shape, shards, low, largest):
    factor_of = 1.0
    for axis_at, blocks in shards:
        draws = jax.random.uniform(jax.random.fold_in(jax.random.fold_in(stream_key, 6), axis_at), (blocks,), jnp.float32, low / len(shards), largest / len(shards))
        factor_of = factor_of * jnp.repeat(jnp.exp(draws), shape[axis_at] // blocks).reshape((-1,) + (1,) * (len(shape) - 1 - axis_at))
    return factor_of


def shared_out(own_key, own, number, rows, count, top, reach, lean):
    order = jax.random.permutation(own_key, count)
    heavy_load, common = shares(count, rows * top, reach, lean, True), shares(count, rows * top, reach, lean, False)
    places = jnp.arange(count)

    def named(lengths, turn):
        used = int((lengths > 0).sum())
        fixed = max(1, used // 4)
        passed = fixed + (places - fixed + turn * (used - fixed)) % max(1, count - fixed)
        return jnp.zeros((count,), jnp.int32).at[order[jnp.where(places < fixed, places, passed)]].set(jnp.asarray(lengths, jnp.int32))

    lengths = jnp.where(number % 4 == 0, named(heavy_load, number // 4), named(common, number - number // 4 - 1))
    mixed = jax.random.permutation(jax.random.fold_in(own, 3), count)
    source_of, taker = mixed[0:count // 2 * 2:2], mixed[1:count // 2 * 2:2]
    margin = jnp.minimum(lengths[source_of] - 1, reach - lengths[taker]) // 2
    margin = jnp.where((source_of == order[0]) | (taker == order[0]) | (lengths[taker] == 0), 0, jnp.maximum(margin, 0))
    passed = jax.random.randint(jax.random.fold_in(own, 4), (count // 2,), 0, 1 << 20) % (margin + 1)
    lengths = lengths.at[source_of].add(-passed).at[taker].add(passed)
    members = jnp.searchsorted(jnp.cumsum(lengths), jnp.arange(rows * top), side="right").astype(jnp.int32)
    table = members.reshape(top, rows).T
    table = table[jax.random.permutation(jax.random.fold_in(own, 1), rows)]
    turn = jax.random.randint(jax.random.fold_in(own, 2), (rows, 1), 0, top)
    return jnp.take_along_axis(table, (jnp.arange(top)[None, :] + turn) % top, axis=1)


def shares(number_of, total, reach, skew, full):
    portions = [(1 << 20) // math.isqrt(standing ** skew) + 1 for standing in range(1, number_of + 1)]
    largest = reach if full else min(reach, max(-(-total // number_of), total * portions[0] // sum(portions)))
    least = 1 if total - largest >= number_of - 1 else 0
    given, rest = [largest] + [least] * (number_of - 1), total - largest - least * (number_of - 1)
    while rest > 0:
        candidates = [i for i in range(1, number_of) if given[i] < largest] or [i for i in range(1, number_of) if given[i] < reach]
        mass, budget = sum([portions[i] for i in candidates]), rest
        for i in candidates:
            extra = min(reach - given[i], max(1, budget * portions[i] // mass), rest)
            given[i] = given[i] + extra
            rest = rest - extra
    return np.array(given)


def normal_values(stream_key, shape, spread, reach, shards=(), held_as=jnp.bfloat16):
    array = spread * jax.random.normal(stream_key, shape, jnp.float32)
    if shards:
        array = array * block_scale(stream_key, shape, shards, -0.22, 0.18)
    return jnp.clip(array, -reach, reach).astype(held_as)


def bell_draw_with(key, shape, deviation, bound, shards, heavy, kind=jnp.bfloat16):
    values = deviation * jax.random.normal(key, shape, jnp.float32)
    if shards:
        values = values * block_scale(key, shape, shards, -0.22, 0.18)
    return jnp.clip(with_spikes(values, jax.random.fold_in(key, 3), *heavy), -bound, bound).astype(kind)


def setup_inputs(seed: int = 0) -> dict:
    seeds = jax.random.split(jax.random.key(seed), 15)
    patches = normal_values(seeds[0], (TOKENS, D), 1.0, 6.0, ((0, 8),))
    first_gain = jnp.clip(1.0 + 0.1 * jax.random.normal(seeds[1], (D,), jnp.float32), 0.5, 1.5)
    first_bias = normal_values(seeds[2], (D,), 0.3, 1.5, (), jnp.float32)
    qkv_weight = normal_values(seeds[3], (D, 3, D), (D // 2) ** -0.5, 0.3125, ((2, 4),))
    out_weight = normal_values(seeds[4], (D, D), (D // 16) ** -0.5, 0.875, ((0, 4),))
    second_gain = jnp.clip(1.0 + 0.1 * jax.random.normal(seeds[5], (D,), jnp.float32), 0.5, 1.5)
    second_bias = normal_values(seeds[6], (D,), 0.3, 1.5, (), jnp.float32)
    router_weight = normal_values(seeds[7], (D, EXPERTS), (2 * D) ** -0.5, 0.15625)
    up_weight = normal_values(seeds[8], (EXPERTS, D, FF), D ** -0.5, 0.21875, ((0, 8), (2, 4)))
    down_weight = normal_values(seeds[9], (EXPERTS, FF, D), FF ** -0.5, 0.109375, ((0, 8), (1, 4)))
    expert_ids_keys = jax.random.split(jax.random.fold_in(seeds[10], 1), TOKENS // ROWS_DEV)
    expert_ids_turns = jax.random.permutation(jax.random.fold_in(seeds[10], 3), TOKENS // ROWS_DEV)
    expert_ids = jax.vmap(lambda own, number: shared_out(jax.random.fold_in(seeds[10], 2), own, number, ROWS_DEV, EXPERTS, 2, CAP, 2))(expert_ids_keys, expert_ids_turns).reshape((TOKENS, 2))
    router_noise = normal_values(seeds[11], (TOKENS, 2), 0.3, 1.5, ((0, 8),), jnp.float32)
    images_live = draw_images_live(jax.random.fold_in(seeds[14], 71), 0)
    out_grad = bell_draw_with(seeds[13], (TOKENS, D), 1.0, 5.0, ((0, 8),), (0, 1, 8, 2.0))
    return {"patches": patches, "first_gain": first_gain, "first_bias": first_bias, "qkv_weight": qkv_weight, "out_weight": out_weight, "second_gain": second_gain, "second_bias": second_bias, "router_weight": router_weight, "up_weight": up_weight, "down_weight": down_weight, "expert_ids": expert_ids, "router_noise": router_noise, "images_live": images_live, "out_grad": out_grad}


epsilon = 1e-06
highest = lax.Precision.HIGHEST

@jax.custom_vjp
def low(v):
    return lax.optimization_barrier(v.astype(jnp.bfloat16)).astype(jnp.float32)

@jax.custom_vjp
def low_back(v):
    return v

def low_keep(v):
    return (low(v), None)

def low_pass(kept, grad):
    return (grad,)

def back_keep(v):
    return (v, None)

def back_low(kept, grad):
    return (low(grad),)
low.defvjp(low_keep, low_pass)
low_back.defvjp(back_keep, back_low)

def layer_norm(values, norm_gain, norm_bias):
    center = values - lax.optimization_barrier(jnp.mean(values, axis=-1, keepdims=True))
    variance = lax.optimization_barrier(jnp.mean(center * center, axis=-1, keepdims=True))
    return center * lax.rsqrt(variance + epsilon) * norm_gain + norm_bias

def reference(patches, first_gain, first_bias, qkv_weight, out_weight, second_gain, second_bias, router_weight, up_weight, down_weight, expert_ids, router_noise, images_live, out_grad):
    span = GROUPS * CAP
    token_index = jnp.arange(TOKENS, dtype=jnp.int32)
    token_group = token_index // ROWS_DEV
    token_image = token_index % ROWS_DEV // TOK_IMG
    live_token = (token_image < images_live[token_group]).astype(jnp.int32)
    live_group = live_token.reshape(GROUPS, ROWS_DEV)
    ids_group = expert_ids.reshape(GROUPS, ROWS_DEV, 2)
    ordered = jnp.concatenate([ids_group[:, :, 0], ids_group[:, :, 1]], axis=1)
    live_pairs = jnp.concatenate([live_group, live_group], axis=1)
    expert_range = jnp.arange(EXPERTS, dtype=jnp.int32)
    onehot = (ordered[:, :, None] == expert_range[None, None, :]).astype(jnp.int32) * live_pairs[:, :, None]
    earlier = (jnp.cumsum(onehot, axis=1) - onehot).astype(jnp.int32)
    slot_index = lax.optimization_barrier(jnp.sum(earlier * onehot, axis=2)).astype(jnp.int32).reshape(GROUPS, 2, ROWS_DEV)
    slot_index = jnp.transpose(slot_index, (0, 2, 1)).reshape(TOKENS, 2)
    live_both = jnp.broadcast_to(live_token[:, None], (TOKENS, 2))
    target = jnp.where(live_both > 0, expert_ids * span + token_group[:, None] * CAP + slot_index, EXPERTS * span).astype(jnp.int32)
    owners = jnp.broadcast_to(token_index[:, None], (TOKENS, 2)).reshape(-1).astype(jnp.int32)
    source = jnp.full((EXPERTS * span,), TOKENS, jnp.int32).at[target.reshape(-1)].set(owners, mode='drop')
    selector = (expert_ids[:, :, None] == expert_range[None, None, :]).astype(jnp.float32)
    live_column = live_token.astype(jnp.float32)[:, None]
    noise = router_noise.astype(jnp.float32)

    def forward(inputs, gain_one, bias_one, qkv_full, out_full, gain_two, bias_two, router_full, up_full, down_full):
        first = low(layer_norm(inputs, gain_one, bias_one))

        def attend(group_rows):
            projected = low_back(low(jnp.dot(group_rows, qkv_full.reshape(D, 3 * D), precision=highest)))
            projected = projected.reshape(IMG_DEV, TOK_IMG, 3, HEADS, HEAD_DIM)
            scores = low_back(jnp.einsum('ilhd,imhd->ihlm', projected[:, :, 0], projected[:, :, 1], precision=highest) * HEAD_DIM ** (-0.5))
            probs = low(jax.nn.softmax(scores, axis=-1))
            mixed = low_back(low(jnp.einsum('ihlm,imhd->ilhd', probs, projected[:, :, 2], precision=highest)))
            return jnp.dot(mixed.reshape(ROWS_DEV, D), out_full, precision=highest)
        attended = lax.map(jax.checkpoint(attend), first.reshape(GROUPS, ROWS_DEV, D)).reshape(TOKENS, D)
        resid = inputs + low_back(attended)
        second = low(layer_norm(resid, gain_two, bias_two))
        logits = jnp.dot(second, router_full, precision=highest)
        chosen = lax.optimization_barrier(jnp.sum(selector * logits[:, None, :], axis=2)) + noise
        gates = jax.nn.softmax(chosen, axis=-1)
        padded = jnp.concatenate([second, jnp.zeros((1, D), second.dtype)], axis=0)
        expert_in = low_back(padded[source]).reshape(EXPERTS, span, D)

        def expert_run(operands):
            rows_in, up_one, down_one = operands
            hidden_pre = low_back(jnp.dot(rows_in, up_one, precision=highest))
            activated = low(jax.nn.gelu(hidden_pre, approximate=False))
            return low_back(low(jnp.dot(activated, down_one, precision=highest)))
        expert_out = lax.map(jax.checkpoint(expert_run), (expert_in, up_full, down_full))
        flat = jnp.concatenate([expert_out.reshape(EXPERTS * span, D), jnp.zeros((1, D), expert_out.dtype)], axis=0)
        picked = flat[target]
        mixture = lax.optimization_barrier(jnp.sum(gates[:, :, None] * picked, axis=1))
        return live_column * (resid + mixture)
    floats = [patches, first_gain, first_bias, qkv_weight, out_weight, second_gain, second_bias, router_weight, up_weight, down_weight]
    floats = [argument.astype(jnp.float32) for argument in floats]
    result, pullback = jax.vjp(forward, *floats)
    grads = pullback(out_grad.astype(jnp.float32))
    return (result.astype(jnp.bfloat16), grads[0], grads[1], grads[2], grads[3], grads[4], grads[5], grads[6], grads[7], grads[8], grads[9])
```

```python
import functools

import jax
import jax.numpy as jnp
from jax import lax
from jax.experimental import pallas as pl
from jax.experimental.pallas import tpu as pltpu
from jax.sharding import PartitionSpec as P

HEAD_DIM = 64
TOK_IMG = 197
TILE = 16
EPSILON = 1e-06
MESH = pl.DeviceIdType.MESH
F32 = jnp.float32
BF16 = jnp.bfloat16


def round_up(value, unit):
    return (value + unit - 1) // unit * unit


def nn(a, b):
    return lax.dot_general(a, b, (((1,), (0,)), ((), ())), preferred_element_type=F32)


def nt(a, b):
    return lax.dot_general(a, b, (((1,), (1,)), ((), ())), preferred_element_type=F32)


def tn(a, b):
    return lax.dot_general(a, b, (((0,), (0,)), ((), ())), preferred_element_type=F32)


def in_three(values):
    high = values.astype(BF16)
    rest = values - high.astype(F32)
    middle = rest.astype(BF16)
    return high, middle, (rest - middle.astype(F32)).astype(BF16)


def normalize(values):
    center = values - jnp.mean(values, axis=-1, keepdims=True)
    scale = lax.rsqrt(jnp.mean(center * center, axis=-1, keepdims=True) + EPSILON)
    return center * scale, scale


def norm_back(normal, scale, grad_normal):
    return scale * (
        grad_normal
        - jnp.mean(grad_normal, axis=-1, keepdims=True)
        - normal * jnp.mean(grad_normal * normal, axis=-1, keepdims=True)
    )


class Shapes:
    def __init__(self, mesh, row_count, model_width, local_width):
        self.experts = mesh.shape["expert"]
        self.depth = mesh.shape["tensor"]
        self.rows = row_count
        self.width = model_width
        self.local = local_width
        self.heads = local_width // HEAD_DIM
        self.padded = round_up(row_count, TILE)
        self.capacity = (3 * row_count + self.experts - 1) // self.experts
        self.slots = round_up(self.capacity, TILE)
        self.slot_lanes = round_up(self.slots, 128)
        self.step = (self.padded - TILE) // self.depth
        self.window = self.step + TILE
        self.share = model_width // self.experts
        self.share_rows = round_up(self.share, TILE)
        self.small = round_up(self.experts + 4, 8)


def whole_kernel(
    sh,
    patches,
    gain1,
    bias1,
    wqkv,
    wout,
    gain2,
    bias2,
    router_t,
    ids_row,
    noise_row,
    images_live,
    out_grad,
    up_hbm,
    down_hbm,
    block_out,
    patches_grad,
    qkv_out,
    wout_out,
    small_out,
    up_out,
    down_out,
    up,
    down,
    wfull,
    pt,
    og,
    first_low,
    q_s,
    k_s,
    v_s,
    probs_s,
    mixed_all,
    resid,
    second_low,
    place,
    x_send,
    x_recv,
    c_send,
    c_recv,
    g_send,
    g_recv,
    act,
    slope,
    delta,
    hid,
    eo_send,
    eo_home,
    ei_home,
    gg_send,
    gg_home,
    acc,
    mix_part,
    mix_recv,
    in_part,
    in_recv,
    first_recv,
    rterm,
    resid_win,
    bo_all,
    ag_all,
    pg_all,
    at_grad,
    gz_send,
    gz_recv,
    qg_send,
    qg_recv,
    og_wsend,
    og_wrecv,
    sz_send,
    sz_recv,
    sp_send,
    sp_recv,
    fz_send,
    fz_recv,
    fp_send,
    fp_recv,
    local_sem,
    e_sem,
    z_sem,
    z_extra,
    w_sem,
):
    E, Z = sh.experts, sh.depth
    R, RP, D = sh.rows, sh.padded, sh.width
    CP, CL = sh.slots, sh.slot_lanes
    me = lax.axis_index("expert")
    mz = lax.axis_index("tensor")

    def plane(step):
        return lax.rem(me + step, E)

    def before(step):
        return lax.rem(me - step + E, E)

    def above(step):
        return lax.rem(mz + step, Z)

    def below(step):
        return lax.rem(mz - step + Z, Z)

    def to_plane(src, dst, kind, step):
        return pltpu.make_async_remote_copy(
            src_ref=src,
            dst_ref=dst,
            send_sem=e_sem.at[kind, 0, step],
            recv_sem=e_sem.at[kind, 1, step],
            device_id=(plane(step), mz),
            device_id_type=MESH,
        )

    def to_depth(src, dst, kind, step, sems=None):
        sems = z_sem if sems is None else sems
        return pltpu.make_async_remote_copy(
            src_ref=src,
            dst_ref=dst,
            send_sem=sems.at[kind, 0, step],
            recv_sem=sems.at[kind, 1, step],
            device_id=(me, above(step)),
            device_id_type=MESH,
        )

    barrier = pltpu.get_barrier_semaphore()
    for step in range(1, E):
        pl.semaphore_signal(barrier, inc=1, device_id=(plane(step), mz), device_id_type=MESH)
    for step in range(1, Z):
        pl.semaphore_signal(barrier, inc=1, device_id=(me, above(step)), device_id_type=MESH)

    load_up = pltpu.make_async_copy(up_hbm, up, local_sem.at[0])
    load_down = pltpu.make_async_copy(down_hbm, down, local_sem.at[1])
    load_up.start()
    load_down.start()

    live_rows = images_live[0] * TOK_IMG
    lane = lax.broadcasted_iota(jnp.int32, (1, RP), 1)
    live = (lane < live_rows).astype(F32)
    expert_of = lax.broadcasted_iota(jnp.int32, (E, RP), 0)
    ids = ids_row[...]
    hot = [(expert_of == ids[k : k + 1]).astype(F32) * live for k in range(2)]
    earlier = (
        lax.broadcasted_iota(jnp.int32, (RP, RP), 0) < lax.broadcasted_iota(jnp.int32, (RP, RP), 1)
    ).astype(BF16)
    counts = [nn(h.astype(BF16), earlier) for h in hot]
    counts[1] = counts[1] + jnp.sum(hot[0], axis=1, keepdims=True)
    start = expert_of.astype(F32) * CP
    spot_row = [
        jnp.where(live > 0, jnp.sum(hot[k] * (counts[k] + start), axis=0, keepdims=True), -1.0)
        for k in range(2)
    ]
    spot_row = [s.astype(jnp.int32) for s in spot_row]
    eye_rows = lax.broadcasted_iota(jnp.int32, (RP, RP), 0) == lax.broadcasted_iota(
        jnp.int32, (RP, RP), 1
    )
    spot_col = [
        jnp.sum(jnp.where(eye_rows, s.astype(F32), 0.0), axis=1, keepdims=True).astype(jnp.int32)
        for s in spot_row
    ]
    slot_lane = lax.broadcasted_iota(jnp.int32, (RP, E * CP), 1)
    place[...] = ((slot_lane == spot_col[0]) | (slot_lane == spot_col[1])).astype(BF16)

    def spread(e):
        slot = lax.broadcasted_iota(jnp.int32, (CP, RP), 0) + e * CP
        return slot == spot_row[0], slot == spot_row[1]

    eye_slots = lax.broadcasted_iota(jnp.int32, (CP, CL), 0) == lax.broadcasted_iota(
        jnp.int32, (CP, CL), 1
    )

    def as_row(column):
        return jnp.sum(jnp.where(eye_slots, column, 0.0), axis=0, keepdims=True)

    def as_column(row):
        return jnp.sum(jnp.where(eye_slots, row, 0.0), axis=1, keepdims=True)

    row_of = lax.broadcasted_iota(jnp.int32, (R, 1), 0)
    og[pl.ds(RP - TILE, TILE)] = jnp.zeros((TILE, D), BF16)
    og[0:R] = jnp.where(row_of < live_rows, out_grad[...], jnp.zeros((), BF16))
    pt[pl.ds(RP - TILE, TILE)] = jnp.zeros((TILE, D), BF16)
    pt[0:R] = patches[...]

    def pack_cotangent(e, carry):
        s0, s1 = spread(e)
        c_send[e] = nn((s0 | s1).astype(BF16), og[...]).astype(BF16)
        return carry

    lax.fori_loop(0, E, pack_cotangent, 0)

    pl.semaphore_wait(barrier, E - 1 + Z - 1)

    half = D // 2
    core = lax.rem(me, 2)
    sibling = me + 1 - 2 * core
    columns = pl.ds(pl.multiple_of(core * half, 128), half)
    wfull[mz] = wout[...]
    w_out_copies = []
    for step in range(1, Z):
        copy = to_depth(wout.at[:, columns], wfull.at[mz, :, columns], 0, step)
        copy.start()
        w_out_copies.append(copy)
    c_copies = []
    for step in range(1, E):
        copy = to_plane(c_send.at[plane(step)], c_recv.at[me], 0, step)
        copy.start()
        c_copies.append(copy)
    c_recv[me] = c_send[me]

    normal, _ = normalize(pt[...].astype(F32))
    first_low[...] = (normal * gain1[...].reshape(1, D) + bias1[...].reshape(1, D)).astype(BF16)
    projected = nn(first_low[...], wqkv[...]).astype(BF16)
    for h in range(sh.heads):
        for part, dest in enumerate((q_s, k_s, v_s)):
            begin = part * sh.local + h * HEAD_DIM
            dest[h] = projected[:, begin : begin + HEAD_DIM]
    row2 = lax.broadcasted_iota(jnp.int32, (RP, RP), 0)
    col2 = lax.broadcasted_iota(jnp.int32, (RP, RP), 1)
    same = ((row2 >= TOK_IMG) == (col2 >= TOK_IMG)) & (col2 < R)
    scale = HEAD_DIM ** (-0.5)
    heads = []
    for h in range(sh.heads):
        scores = jnp.where(same, nt(q_s[h], k_s[h]) * scale, -1e30)
        exponent = jnp.exp(scores - jnp.max(scores, axis=1, keepdims=True))
        probs = exponent / jnp.sum(exponent, axis=1, keepdims=True)
        probs_s[h] = probs
        heads.append(nn(probs.astype(BF16), v_s[h]).astype(BF16))
    mixed_all[mz] = jnp.concatenate(heads, axis=1)
    m_copies = []
    for step in range(1, Z):
        copy = to_depth(mixed_all.at[mz], mixed_all.at[mz], 1, step)
        copy.start()
        m_copies.append(copy)

    w_passed = []
    for step in range(1, Z):
        origin = below(step)
        w_out_copies[step - 1].wait_recv()
        copy = pltpu.make_async_remote_copy(
            src_ref=wfull.at[origin, :, columns],
            dst_ref=wfull.at[origin, :, columns],
            send_sem=w_sem.at[0, step],
            recv_sem=w_sem.at[1, step],
            device_id=(sibling, mz),
            device_id_type=MESH,
        )
        copy.start()
        w_passed.append(copy)
    for copy in w_passed:
        copy.wait_recv()

    resid[...] = pt[...].astype(F32) + nn(mixed_all[mz], wfull[mz])
    for step in range(1, Z):
        m_copies[step - 1].wait_recv()
        resid[...] += nn(mixed_all[below(step)], wfull[below(step)])

    normal, _ = normalize(resid[...])
    second_low[...] = (normal * gain2[...].reshape(1, D) + bias2[...].reshape(1, D)).astype(BF16)
    logits = nt(router_t[...], second_low[...])
    chosen = [
        jnp.sum(hot[k] * logits, axis=0, keepdims=True) + noise_row[k : k + 1, :] for k in range(2)
    ]
    top = jnp.maximum(chosen[0], chosen[1])
    powers = [jnp.exp(c - top) for c in chosen]
    gates = [p / (powers[0] + powers[1]) for p in powers]

    def pack_rows(e, carry):
        s0, s1 = spread(e)
        x_send[e] = nn((s0 | s1).astype(BF16), second_low[...]).astype(BF16)
        gate = jnp.sum(
            jnp.where(s0, gates[0], 0.0) + jnp.where(s1, gates[1], 0.0), axis=1, keepdims=True
        )
        g_send[e] = jnp.broadcast_to(as_row(gate), (8, CL))
        return carry

    lax.fori_loop(0, E, pack_rows, 0)
    for step in range(1, E):
        to_plane(g_send.at[plane(step)], g_recv.at[me], 1, step).start()
        to_plane(x_send.at[plane(step)], x_recv.at[me], 2, step).start()
    g_recv[me] = g_send[me]
    x_recv[me] = x_send[me]

    load_up.wait()
    load_down.wait()

    def forward(step, carry):
        group = before(step)

        @pl.when(step > 0)
        def _():
            to_plane(g_send.at[0], g_recv.at[group], 1, step).wait_recv()
            to_plane(x_send.at[0], x_recv.at[group], 2, step).wait_recv()
            to_plane(c_send.at[0], c_recv.at[group], 0, step).wait_recv()

        hidden = nn(x_recv[group], up[...])
        below_it = 0.5 * (1.0 + lax.erf(hidden * (0.5**0.5)))
        bell = jnp.exp(-0.5 * hidden * hidden) * 0.3989422804014327
        act[group] = (hidden * below_it).astype(BF16)
        slope[group] = (below_it + hidden * bell).astype(BF16)
        result = nn(act[group], down[...])
        gate = as_column(g_recv[group][0:1])
        given = c_recv[group].astype(F32)
        dots = jnp.sum(given * result, axis=1, keepdims=True)
        gg_send[group] = jnp.broadcast_to(as_row(dots), (8, CL))
        eo_send[group] = (gate * result).astype(BF16)
        delta[group] = (gate * given).astype(BF16)

        @pl.when(step > 0)
        def _():
            back_to(gg_send.at[group], gg_home.at[me], 3, step).start()
            back_to(eo_send.at[group], eo_home.at[me], 4, step).start()

        return carry

    def back_to(src, dst, kind, step):
        return pltpu.make_async_remote_copy(
            src_ref=src,
            dst_ref=dst,
            send_sem=e_sem.at[kind, 0, step],
            recv_sem=e_sem.at[kind, 1, step],
            device_id=(before(step), mz),
            device_id_type=MESH,
        )

    lax.fori_loop(0, E, forward, 0)
    gg_home[me] = gg_send[me]
    eo_home[me] = eo_send[me]

    for copy in c_copies:
        copy.wait_send()
    ei_send = c_send

    def backward(step, carry):
        group = before(step)
        hid[group] = (nt(delta[group], down[...]) * slope[group]).astype(BF16)
        ei_send[group] = nt(hid[group], up[...]).astype(BF16)

        @pl.when(step > 0)
        def _():
            back_to(ei_send.at[group], ei_home.at[me], 5, step).start()

        return carry

    lax.fori_loop(0, E, backward, 0)
    ei_home[me] = ei_send[me]

    strip = 128
    F = up.shape[1]

    def flat(ref, first, size):
        return ref[:, :, pl.ds(pl.multiple_of(first, 128), size)].reshape(E * CP, size)

    def strip_copy(i, out, slot):
        return pltpu.make_async_copy(
            acc.at[slot], out.at[pl.ds(pl.multiple_of(i * strip, strip), strip)], local_sem.at[slot]
        )

    def strips(out, lhs, rhs, count, slot):
        def one(i, carry):
            at = slot + lax.rem(i, 2)

            @pl.when(i >= 2)
            def _():
                strip_copy(i - 2, out, at).wait()

            acc[at] = tn(flat(lhs, i * strip, strip), flat(rhs, 0, rhs.shape[2]))
            strip_copy(i, out, at).start()
            return carry

        lax.fori_loop(0, count, one, 0)

    strips(up_out, x_recv, hid, D // strip, 0)
    strips(down_out, act, delta, F // strip, 2)

    S, W = sh.step, sh.window

    def tail_of(position):
        return pl.ds(pl.multiple_of(position * S + TILE, TILE), S)

    def window_of(position):
        return pl.ds(pl.multiple_of(position * S, TILE), W)

    def scatter_windows(part, recv, kind):
        for step in range(1, Z):
            target = above(step)
            to_depth(
                part.at[tail_of(target)], recv.at[mz, pl.ds(TILE, S)], kind, step
            ).start()

            @pl.when(target == 0)
            def _():
                to_depth(
                    part.at[pl.ds(0, TILE)], recv.at[mz, pl.ds(0, TILE)], kind, step, z_extra
                ).start()

    def wait_scatter(part, recv, kind, total):
        for step in range(1, Z):
            source = below(step)
            to_depth(
                part.at[tail_of(0)], recv.at[source, pl.ds(TILE, S)], kind, step
            ).wait_recv()

            @pl.when(mz == 0)
            def _():
                to_depth(
                    part.at[pl.ds(0, TILE)], recv.at[source, pl.ds(0, TILE)], kind, step, z_extra
                ).wait_recv()

            total = total + recv[source].astype(F32)
        return total

    def finish_scatter(part, recv, kind):
        for step in range(1, Z):
            to_depth(
                part.at[tail_of(0)], recv.at[mz, pl.ds(TILE, S)], kind, step
            ).wait_send()

            @pl.when(above(step) == 0)
            def _():
                to_depth(
                    part.at[pl.ds(0, TILE)], recv.at[mz, pl.ds(0, TILE)], kind, step, z_extra
                ).wait_send()

    def gather_windows(every, kind):
        for step in range(1, Z):
            tail = every.at[mz, pl.ds(TILE, S)]
            to_depth(tail, tail, kind, step).start()

            @pl.when(mz == 0)
            def _():
                head = every.at[mz, pl.ds(0, TILE)]
                to_depth(head, head, kind, step, z_extra).start()

    def wait_gather(every, kind):
        for step in range(1, Z):
            source = below(step)
            tail = every.at[source, pl.ds(TILE, S)]
            to_depth(tail, tail, kind, step).wait_recv()

            @pl.when(source == 0)
            def _():
                head = every.at[source, pl.ds(0, TILE)]
                to_depth(head, head, kind, step, z_extra).wait_recv()

    def finish_gather(every, kind):
        for step in range(1, Z):
            tail = every.at[mz, pl.ds(TILE, S)]
            to_depth(tail, tail, kind, step).wait_send()

            @pl.when(mz == 0)
            def _():
                head = every.at[mz, pl.ds(0, TILE)]
                to_depth(head, head, kind, step, z_extra).wait_send()

    def put_together(every, dest):
        dest[0:TILE] = every[0, 0:TILE]
        for position in range(Z):
            dest[TILE + S * position : TILE + S * (position + 1)] = every[position, TILE:W]

    window = window_of(mz)
    own = (lax.broadcasted_iota(jnp.int32, (W, 1), 0) >= TILE) | (mz == 0)

    for step in range(1, E):
        to_plane(eo_send.at[0], eo_home.at[plane(step)], 4, step).wait_recv()
    mix_part[...] = nn(place[...], eo_home[...].reshape(E * CP, D)).astype(BF16)
    scatter_windows(mix_part, mix_recv, 2)
    for step in range(1, E):
        to_plane(gg_send.at[0], gg_home.at[plane(step)], 3, step).wait_recv()

    def pick_dots(e, totals):
        s0, s1 = spread(e)
        column = as_column(gg_home[e][0:1])
        return (
            totals[0] + jnp.sum(jnp.where(s0, column, 0.0), axis=0, keepdims=True),
            totals[1] + jnp.sum(jnp.where(s1, column, 0.0), axis=0, keepdims=True),
        )

    nothing = jnp.zeros((1, RP), F32)
    dots0, dots1 = lax.fori_loop(0, E, pick_dots, (nothing, nothing))
    gz_send[...] = jnp.zeros((8, RP), F32)
    gz_send[0:1] = dots0
    gz_send[1:2] = dots1
    for step in range(1, Z):
        to_depth(gz_send, gz_recv.at[mz], 3, step).start()
    gate_grad = gz_send[...]
    for step in range(1, Z):
        to_depth(gz_send, gz_recv.at[below(step)], 3, step).wait_recv()
        gate_grad = gate_grad + gz_recv[below(step)]
    both = gates[0] * gate_grad[0:1] + gates[1] * gate_grad[1:2]
    logit_grad = sum(hot[k] * (gates[k] * (gate_grad[k : k + 1] - both)) for k in range(2))
    parts = in_three(logit_grad)
    router_grad = sum(nn(p, second_low[...]) for p in parts)
    rterm[...] = sum(tn(p, router_t[...]) for p in parts)

    mixture = wait_scatter(mix_part, mix_recv, 2, mix_part[window].astype(F32))
    at = lax.broadcasted_iota(jnp.int32, (W, 1), 0) + mz * S
    bo_all[mz] = jnp.where(at < live_rows, resid[window] + mixture, 0.0).astype(BF16)
    gather_windows(bo_all, 4)

    for step in range(1, E):
        to_plane(ei_send.at[0], ei_home.at[plane(step)], 5, step).wait_recv()
    in_part[...] = nn(place[...], ei_home[...].reshape(E * CP, D)).astype(BF16)
    scatter_windows(in_part, in_recv, 5)
    cot = og[window].astype(F32)
    normal, spread_scale = normalize(resid[window])
    second_grad = wait_scatter(in_part, in_recv, 5, in_part[window].astype(F32)) + rterm[window]
    resid_grad = cot + norm_back(normal, spread_scale, second_grad * gain2[...].reshape(1, D))
    resid_win[...] = resid_grad
    ag_all[mz] = resid_grad.astype(BF16)
    gather_windows(ag_all, 6)
    sz_send[...] = jnp.zeros((8, D), F32)
    sz_send[0:1] = jnp.sum(jnp.where(own, second_grad * normal, 0.0), axis=0, keepdims=True)
    sz_send[1:2] = jnp.sum(jnp.where(own, second_grad, 0.0), axis=0, keepdims=True)
    for step in range(1, Z):
        to_depth(sz_send, sz_recv.at[mz], 7, step).start()
    wait_gather(ag_all, 6)
    put_together(ag_all, at_grad)

    mixed_grad = nt(at_grad[...], wout[...]).astype(BF16)
    grads = [[], [], []]
    for h in range(sh.heads):
        mg = mixed_grad[:, h * HEAD_DIM : (h + 1) * HEAD_DIM]
        probs = probs_s[h]
        prob_grad = nt(mg, v_s[h])
        score_grad = (
            probs * (prob_grad - jnp.sum(prob_grad * probs, axis=1, keepdims=True))
        ).astype(BF16)
        grads[0].append((nn(score_grad, k_s[h]) * scale).astype(BF16))
        grads[1].append((tn(score_grad, q_s[h]) * scale).astype(BF16))
        grads[2].append(tn(probs.astype(BF16), mg).astype(BF16))
    projected_grad = jnp.concatenate(grads[0] + grads[1] + grads[2], axis=1)
    finish_scatter(mix_part, mix_recv, 2)
    first_part = mix_part
    first_part[...] = nt(projected_grad, wqkv[...]).astype(BF16)
    scatter_windows(first_part, first_recv, 8)

    B, BP = sh.share, sh.share_rows
    qkv_grad = tn(first_low[...], projected_grad)
    for e in range(E):
        qg_send[e, 0:B] = qkv_grad[e * B : (e + 1) * B].astype(BF16)
    for step in range(1, E):
        to_plane(qg_send.at[plane(step)], qg_recv.at[me], 6, step).start()
    wout_grad = tn(at_grad[...], mixed_all[mz])
    for e in range(E):
        og_wsend[e, 0:B] = wout_grad[e * B : (e + 1) * B].astype(BF16)
    for step in range(1, E):
        to_plane(og_wsend.at[plane(step)], og_wrecv.at[me], 7, step).start()

    sums = sz_send[...]
    for step in range(1, Z):
        to_depth(sz_send, sz_recv.at[below(step)], 7, step).wait_recv()
        sums = sums + sz_recv[below(step)]
    sp_send[0:E] = router_grad
    sp_send[E : E + 4] = sums[0:4]
    for step in range(1, E):
        to_plane(sp_send, sp_recv.at[me], 8, step).start()

    normal, spread_scale = normalize(pt[window].astype(F32))
    first_grad = wait_scatter(first_part, first_recv, 8, first_part[window].astype(F32))
    patch_grad = resid_win[...] + norm_back(normal, spread_scale, first_grad * gain1[...].reshape(1, D))
    pg_all[mz] = patch_grad.astype(BF16)
    gather_windows(pg_all, 9)
    fz_send[...] = jnp.zeros((8, D), F32)
    fz_send[0:1] = jnp.sum(jnp.where(own, first_grad * normal, 0.0), axis=0, keepdims=True)
    fz_send[1:2] = jnp.sum(jnp.where(own, first_grad, 0.0), axis=0, keepdims=True)
    for step in range(1, Z):
        to_depth(fz_send, fz_recv.at[mz], 10, step).start()
    sums = fz_send[...]
    for step in range(1, Z):
        to_depth(fz_send, fz_recv.at[below(step)], 10, step).wait_recv()
        sums = sums + fz_recv[below(step)]
    fp_send[...] = sums
    for step in range(1, E):
        to_plane(fp_send, fp_recv.at[me], 9, step).start()

    wait_gather(bo_all, 4)
    put_together(bo_all, block_out)
    total = qg_send[me].astype(F32)
    total_w = og_wsend[me].astype(F32)
    total_s = sp_send[...]
    total_f = fp_send[...]
    for step in range(1, E):
        source = before(step)
        to_plane(qg_send.at[0], qg_recv.at[source], 6, step).wait_recv()
        total = total + qg_recv[source].astype(F32)
        to_plane(og_wsend.at[0], og_wrecv.at[source], 7, step).wait_recv()
        total_w = total_w + og_wrecv[source].astype(F32)
        to_plane(sp_send, sp_recv.at[source], 8, step).wait_recv()
        total_s = total_s + sp_recv[source]
        to_plane(fp_send, fp_recv.at[source], 9, step).wait_recv()
        total_f = total_f + fp_recv[source]
    qkv_out[...] = total[0:B]
    wout_out[...] = total_w[0:B]
    small_out[0:E] = total_s[0:E]
    small_out[E : E + 2] = total_s[E : E + 2]
    small_out[E + 2 : E + 4] = total_f[0:2]
    wait_gather(pg_all, 9)
    put_together(pg_all, patches_grad)

    for copy in w_out_copies + m_copies + w_passed:
        copy.wait_send()

    def sent(step, carry):
        to_plane(g_send.at[0], g_recv.at[0], 1, step).wait_send()
        to_plane(x_send.at[0], x_recv.at[0], 2, step).wait_send()
        to_plane(gg_send.at[0], gg_home.at[0], 3, step).wait_send()
        to_plane(eo_send.at[0], eo_home.at[0], 4, step).wait_send()
        to_plane(ei_send.at[0], ei_home.at[0], 5, step).wait_send()
        to_plane(qg_send.at[0], qg_recv.at[0], 6, step).wait_send()
        to_plane(og_wsend.at[0], og_wrecv.at[0], 7, step).wait_send()
        to_plane(sp_send, sp_recv.at[0], 8, step).wait_send()
        to_plane(fp_send, fp_recv.at[0], 9, step).wait_send()
        return carry

    lax.fori_loop(1, E, sent, 0)
    finish_scatter(in_part, in_recv, 5)
    finish_scatter(first_part, first_recv, 8)
    finish_gather(bo_all, 4)
    finish_gather(ag_all, 6)
    finish_gather(pg_all, 9)
    for step in range(1, Z):
        to_depth(gz_send, gz_recv.at[0], 3, step).wait_send()
        to_depth(sz_send, sz_recv.at[0], 7, step).wait_send()
        to_depth(fz_send, fz_recv.at[0], 10, step).wait_send()
    for last in (2, 1):
        strip_copy(D // strip - last, up_out, (D // strip - last) % 2).wait()
        strip_copy(F // strip - last, down_out, 2 + (F // strip - last) % 2).wait()


def scratch_of(sh, F):
    E, Z, RP, D = sh.experts, sh.depth, sh.padded, sh.width
    CP, CL, W = sh.slots, sh.slot_lanes, sh.window
    B, BP = sh.share, sh.share_rows
    L, H = sh.local, sh.heads
    blocks = (E, CP, D)

    def vm(shape, kind):
        return pltpu.VMEM(shape, kind)

    return [
        vm((D, F), BF16),
        vm((F, D), BF16),
        vm((Z, L, D), BF16),
        vm((RP, D), BF16),
        vm((RP, D), BF16),
        vm((RP, D), BF16),
        vm((H, RP, HEAD_DIM), BF16),
        vm((H, RP, HEAD_DIM), BF16),
        vm((H, RP, HEAD_DIM), BF16),
        vm((H, RP, RP), F32),
        vm((Z, RP, L), BF16),
        vm((RP, D), F32),
        vm((RP, D), BF16),
        vm((RP, E * CP), BF16),
        vm(blocks, BF16),
        vm(blocks, BF16),
        vm(blocks, BF16),
        vm(blocks, BF16),
        vm((E, 8, CL), F32),
        vm((E, 8, CL), F32),
        vm((E, CP, F), BF16),
        vm((E, CP, F), BF16),
        vm(blocks, BF16),
        vm((E, CP, F), BF16),
        vm(blocks, BF16),
        vm(blocks, BF16),
        vm(blocks, BF16),
        vm((E, 8, CL), F32),
        vm((E, 8, CL), F32),
        vm((4, 128, max(F, D)), F32),
        vm((RP, D), BF16),
        vm((Z, W, D), BF16),
        vm((RP, D), BF16),
        vm((Z, W, D), BF16),
        vm((Z, W, D), BF16),
        vm((RP, D), F32),
        vm((W, D), F32),
        vm((Z, W, D), BF16),
        vm((Z, W, D), BF16),
        vm((Z, W, D), BF16),
        vm((RP, D), BF16),
        vm((8, RP), F32),
        vm((Z, 8, RP), F32),
        vm((E, BP, 3 * L), BF16),
        vm((E, BP, 3 * L), BF16),
        vm((E, BP, L), BF16),
        vm((E, BP, L), BF16),
        vm((8, D), F32),
        vm((Z, 8, D), F32),
        vm((sh.small, D), F32),
        vm((E, sh.small, D), F32),
        vm((8, D), F32),
        vm((Z, 8, D), F32),
        vm((8, D), F32),
        vm((E, 8, D), F32),
        pltpu.SemaphoreType.DMA((4,)),
        pltpu.SemaphoreType.DMA((10, 2, E)),
        pltpu.SemaphoreType.DMA((11, 2, Z)),
        pltpu.SemaphoreType.DMA((11, 2, Z)),
        pltpu.SemaphoreType.DMA((2, Z)),
    ]


def on_device(
    mesh,
    patches,
    first_gain,
    first_bias,
    qkv_weight,
    out_weight,
    second_gain,
    second_bias,
    router_weight,
    up_weight,
    down_weight,
    expert_ids,
    router_noise,
    images_live,
    out_grad,
):
    row_count, model_width = patches.shape
    local_width = out_weight.shape[0]
    sh = Shapes(mesh, row_count, model_width, local_width)
    hidden_width = up_weight.shape[2]
    E, RP, D = sh.experts, sh.padded, sh.width
    tail = RP - row_count
    ids_row = jnp.pad(expert_ids.T, ((0, 0), (0, tail)), constant_values=-1)
    noise_row = jnp.pad(router_noise.T, ((0, 0), (0, tail)))
    vmem = pl.BlockSpec(memory_space=pltpu.VMEM)
    anywhere = pl.BlockSpec(memory_space=pl.ANY)
    slots = E * sh.slots
    flops = 2 * (
        6 * slots * D * hidden_width
        + 3 * RP * D * 4 * local_width
        + 4 * slots * RP * D
        + 7 * sh.heads * RP * RP * HEAD_DIM
    )
    outs = pl.pallas_call(
        functools.partial(whole_kernel, sh),
        out_shape=(
            jax.ShapeDtypeStruct((RP, D), BF16),
            jax.ShapeDtypeStruct((RP, D), BF16),
            jax.ShapeDtypeStruct((sh.share, 3 * local_width), F32),
            jax.ShapeDtypeStruct((sh.share, local_width), F32),
            jax.ShapeDtypeStruct((sh.small, D), F32),
            jax.ShapeDtypeStruct((D, hidden_width), F32),
            jax.ShapeDtypeStruct((hidden_width, D), F32),
        ),
        in_specs=[vmem] * 10
        + [pl.BlockSpec(memory_space=pltpu.SMEM)]
        + [vmem]
        + [anywhere] * 2,
        out_specs=(vmem,) * 5 + (anywhere,) * 2,
        scratch_shapes=scratch_of(sh, hidden_width),
        compiler_params=pltpu.CompilerParams(
            collective_id=0, has_side_effects=True, vmem_limit_bytes=62 << 20
        ),
        cost_estimate=pl.CostEstimate(flops=flops, bytes_accessed=16 << 20, transcendentals=0),
        name="block",
    )(
        patches,
        first_gain,
        first_bias,
        qkv_weight.reshape(D, 3 * local_width),
        out_weight,
        second_gain,
        second_bias,
        router_weight.T,
        ids_row,
        noise_row,
        images_live,
        out_grad,
        up_weight[0],
        down_weight[0],
    )
    block_out, patches_grad, qkv_grad, wout_grad, small, up_grad, down_grad = outs
    begin = lax.axis_index("expert") * sh.share
    mine = lax.dynamic_slice_in_dim(small, begin, sh.share, axis=1)
    return (
        block_out[:row_count],
        patches_grad[:row_count].astype(F32),
        mine[E + 2],
        mine[E + 3],
        qkv_grad.reshape(sh.share, 3, local_width),
        wout_grad.T,
        mine[E],
        mine[E + 1],
        mine[:E].T,
        up_grad[None],
        down_grad[None],
    )


def solution(mesh):
    placed = (
        P("expert", None),
        P(),
        P(),
        P(None, None, "tensor"),
        P("tensor", None),
        P(),
        P(),
        P(),
        P("expert", None, "tensor"),
        P("expert", "tensor", None),
        P("expert", None),
        P("expert", None),
        P("expert"),
        P("expert", None),
    )
    return jax.shard_map(
        functools.partial(on_device, mesh),
        mesh=mesh,
        in_specs=placed,
        out_specs=(
            P("expert", None),
            P("expert", None),
            P("expert"),
            P("expert"),
            P("expert", None, "tensor"),
            P("tensor", "expert"),
            P("expert"),
            P("expert"),
            P("expert", None),
            P("expert", None, "tensor"),
            P("expert", "tensor", None),
        ),
        check_vma=False,
    )
```

```python
import functools

import jax
import jax.numpy as jnp
from jax import lax
from jax.experimental import pallas as pl
from jax.experimental.pallas import tpu as pltpu
from jax.sharding import PartitionSpec as P

HEAD_DIM = 64
TOK_IMG = 197
TILE = 16
EPSILON = 1e-06
MESH = pl.DeviceIdType.MESH
F32 = jnp.float32
BF16 = jnp.bfloat16


def round_up(value, unit):
    return (value + unit - 1) // unit * unit


def nn(a, b):
    return lax.dot_general(a, b, (((1,), (0,)), ((), ())), preferred_element_type=F32)


def nt(a, b):
    return lax.dot_general(a, b, (((1,), (1,)), ((), ())), preferred_element_type=F32)


def tn(a, b):
    return lax.dot_general(a, b, (((0,), (0,)), ((), ())), preferred_element_type=F32)


def in_three(values):
    high = values.astype(BF16)
    rest = values - high.astype(F32)
    middle = rest.astype(BF16)
    return high, middle, (rest - middle.astype(F32)).astype(BF16)


def normalize(values):
    center = values - jnp.mean(values, axis=-1, keepdims=True)
    scale = lax.rsqrt(jnp.mean(center * center, axis=-1, keepdims=True) + EPSILON)
    return center * scale, scale


def norm_back(normal, scale, grad_normal):
    return scale * (
        grad_normal
        - jnp.mean(grad_normal, axis=-1, keepdims=True)
        - normal * jnp.mean(grad_normal * normal, axis=-1, keepdims=True)
    )


class Shapes:
    def __init__(self, mesh, row_count, model_width, local_width):
        self.experts = mesh.shape["expert"]
        self.depth = mesh.shape["tensor"]
        self.rows = row_count
        self.width = model_width
        self.local = local_width
        self.heads = local_width // HEAD_DIM
        self.padded = round_up(row_count, TILE)
        self.capacity = (3 * row_count + self.experts - 1) // self.experts
        self.slots = round_up(self.capacity, TILE)
        self.slot_lanes = round_up(self.slots, 128)
        self.step = (self.padded - TILE) // self.depth
        self.window = self.step + TILE
        self.share = model_width // self.experts
        self.share_rows = round_up(self.share, TILE)
        self.small = round_up(self.experts + 4, 8)
        self.half_rows = round_up(self.padded // 2, TILE)
        self.chunk = 256
        self.chunks = model_width // self.chunk
        parts = range(self.chunks)
        e_kinds = ["c", "g", "x", "gg", "eo", "qg", "og", "sp", "fp"] + [f"ei{c}" for c in parts]
        z_kinds = ["w", "m", "gz", "bo", "mg", "wz", "sz", "pg", "fz"]
        z_kinds += [f"{n}{c}" for n in ("mix", "in", "first") for c in parts]
        self.e_kinds = {n: i for i, n in enumerate(e_kinds)}
        self.z_kinds = {n: i for i, n in enumerate(z_kinds)}


INPUTS = (
    "gain1", "bias1", "gain2", "bias2", "router_t", "ids_row", "noise_row", "images_live", "wout",
    "out_grad", "patches", "wqkv", "up", "down",
)
OUTPUTS = (
    "block_out", "patches_grad", "qkv_out", "wout_out", "small_out", "up_out", "down_out",
)
SCRATCH = (
    "gain1", "bias1", "gain2", "bias2", "router_t", "ids_row", "noise_row", "images_live",
    "patches", "out_grad", "up", "down", "wqkv", "wfull", "pt", "og", "first_low", "q_s", "k_s",
    "v_s", "probs_s", "mixed", "mixed_all", "resid", "second_low", "place", "x_send", "x_recv",
    "c_send", "c_recv", "g_send", "g_recv", "act", "slope", "delta", "hid", "eo_send", "eo_home",
    "ei_home", "gg_send", "gg_home", "acc", "mix_part", "mix_recv", "mix_pass", "in_part",
    "in_recv", "in_pass", "first_recv", "first_pass", "rterm", "resid_win", "bo_all",
    "pg_all", "mg_send", "mg_recv", "mixed_grad", "wz_send", "wz_recv", "gz_send", "gz_recv", "qg_send", "qg_recv", "og_wsend",
    "og_wrecv", "sz_send", "sz_recv", "sp_send", "sp_recv", "fz_send", "fz_recv", "fp_send",
    "fp_recv", "qkv_sum", "wout_sum", "small_sum", "local_sem", "in_sem", "out_sem", "e_sem",
    "z_sem", "z_extra", "w_sem",
)


def whole_kernel(sh, *refs):
    E, Z, NC = sh.experts, sh.depth, sh.chunks
    R, RP, D = sh.rows, sh.padded, sh.width
    CP, CL, CW = sh.slots, sh.slot_lanes, sh.chunk
    inputs = dict(zip(INPUTS, refs))
    outputs = dict(zip(OUTPUTS, refs[len(INPUTS) :]))
    m = dict(zip(SCRATCH, refs[len(INPUTS) + len(OUTPUTS) :]))
    e_sem, z_sem, z_extra, w_sem, local_sem, in_sem, out_sem = (
        m[n] for n in ("e_sem", "z_sem", "z_extra", "w_sem", "local_sem", "in_sem", "out_sem")
    )
    me = lax.axis_index("expert")
    mz = lax.axis_index("tensor")

    def plane(step):
        return lax.rem(me + step, E)

    def before(step):
        return lax.rem(me - step + E, E)

    def above(step):
        return lax.rem(mz + step, Z)

    def below(step):
        return lax.rem(mz - step + Z, Z)

    def remote(src, dst, sems, kind, sent, received, expert, position):
        return pltpu.make_async_remote_copy(
            src_ref=src,
            dst_ref=dst,
            send_sem=sems.at[kind, 0, sent],
            recv_sem=sems.at[kind, 1, received],
            device_id=(expert, position),
            device_id_type=MESH,
        )

    def to_plane(src, dst, name, step):
        return remote(src, dst, e_sem, sh.e_kinds[name], step, step, plane(step), mz)

    def back_to(src, dst, name, step):
        return remote(src, dst, e_sem, sh.e_kinds[name], step, step, before(step), mz)

    def to_depth(src, dst, name, step, sems=None):
        sems = z_sem if sems is None else sems
        return remote(src, dst, sems, sh.z_kinds[name], step, step, me, above(step))

    relayed = Z == 4
    between = (mz > 0) & (mz < Z - 1)

    def direct(step, hold=False):
        if not relayed:
            return mz >= 0
        if step == 1:
            return mz < Z - 1
        if step == Z - 1:
            return mz > 0
        return jnp.logical_not(between) if hold else mz >= 0

    def arrives(step):
        if not relayed:
            return mz >= 0
        if step == 1:
            return mz > 0
        if step == Z - 1:
            return mz < Z - 1
        return mz >= 0

    order = (2, 1, 3) if relayed else tuple(range(1, Z))

    loads = {}
    for at, name in enumerate(INPUTS):
        dest = m["wfull"].at[mz] if name == "wout" else m[name]
        loads[name] = pltpu.make_async_copy(inputs[name], dest, in_sem.at[at])
        loads[name].start()

    def loaded(*names):
        for name in names:
            loads[name].wait()

    stores = []

    def store(src, dst, condition=None):
        copy = pltpu.make_async_copy(src, dst, out_sem.at[len(stores)])
        stores.append((copy, condition))
        if condition is None:
            copy.start()
        else:

            @pl.when(condition)
            def _():
                copy.start()

    gain1, bias1, gain2, bias2, router_t, ids_row, noise_row, images_live = (
        m[n] for n in INPUTS[:8]
    )
    barrier = pltpu.get_barrier_semaphore()
    for step in range(1, E):
        pl.semaphore_signal(barrier, inc=1, device_id=(plane(step), mz), device_id_type=MESH)
    for step in range(1, Z):
        pl.semaphore_signal(barrier, inc=1, device_id=(me, above(step)), device_id_type=MESH)

    S, W = sh.step, sh.window

    def tail_of(position):
        if isinstance(position, int):
            return pl.ds(position * S + TILE, S)
        return pl.ds(pl.multiple_of(position * S + TILE, TILE), S)

    def window_of(position):
        return pl.ds(pl.multiple_of(position * S, TILE), W)

    head, tail = pl.ds(0, TILE), pl.ds(TILE, S)

    class Scatter:
        def __init__(self, name, part, recv, passing):
            self.name, self.part, self.recv, self.passing = name, part, recv, passing

        def send_to(self, step):
            target = above(step)
            return (
                to_depth(self.part.at[tail_of(target)], self.recv.at[mz, tail], self.name, step),
                to_depth(self.part.at[head], self.recv.at[mz, head], self.name, step, z_extra),
                target == 0,
            )

        def pass_to(self):
            source = self.passing
            return (
                to_depth(source.at[tail], self.recv.at[mz, tail], self.name, 2),
                to_depth(source.at[head], self.recv.at[mz, head], self.name, 2, z_extra),
                above(2) == 0,
            )

        def far(self):
            kind = sh.z_kinds[self.name]
            up_to, down_to = (
                remote(
                    self.part.at[tail_of(Z - 1 - end)],
                    self.passing.at[tail],
                    z_sem,
                    kind,
                    0,
                    0,
                    me,
                    1 if end == 0 else Z - 2,
                )
                for end in (0, Z - 1)
            )
            down_head = remote(
                self.part.at[head],
                self.passing.at[head],
                z_extra,
                kind,
                0,
                0,
                me,
                Z - 2,
            )
            return up_to, down_to, down_head

        def start(self):
            if relayed:
                up_to, down_to, down_head = self.far()

                @pl.when(mz == 0)
                def _():
                    up_to.start()

                @pl.when(mz == Z - 1)
                def _():
                    down_to.start()
                    down_head.start()

            for step in order:
                body, first, is_head = self.send_to(step)

                @pl.when(direct(step, hold=True))
                def _():
                    body.start()

                @pl.when(direct(step, hold=True) & is_head)
                def _():
                    first.start()

        def relay(self):
            if not relayed:
                return

            @pl.when(between)
            def _():
                up_to, down_to, down_head = self.far()
                up_to.wait_recv()

                @pl.when(mz == Z - 2)
                def _():
                    down_head.wait_recv()

                target = above(2)
                self.passing[...] = (
                    self.passing[...].astype(F32) + self.part[window_of(target)].astype(F32)
                ).astype(BF16)
                body, first, is_head = self.pass_to()
                body.start()

                @pl.when(is_head)
                def _():
                    first.start()

        def total(self):
            value = self.part[window_of(mz)].astype(F32)
            for step in order:
                source = below(step)
                here = arrives(step)
                body = to_depth(
                    self.part.at[tail_of(0)], self.recv.at[source, tail], self.name, step
                )
                first = to_depth(
                    self.part.at[head], self.recv.at[source, head], self.name, step, z_extra
                )

                @pl.when(here)
                def _():
                    body.wait_recv()

                @pl.when(here & (mz == 0))
                def _():
                    first.wait_recv()

                value = value + jnp.where(here, self.recv[source].astype(F32), 0.0)
            return value

        def finish(self):
            if relayed:
                up_to, down_to, down_head = self.far()

                @pl.when(mz == 0)
                def _():
                    up_to.wait_send()

                @pl.when(mz == Z - 1)
                def _():
                    down_to.wait_send()
                    down_head.wait_send()

            for step in order:
                body, first, is_head = self.send_to(step)

                @pl.when(direct(step))
                def _():
                    body.wait_send()

                @pl.when(direct(step) & is_head)
                def _():
                    first.wait_send()

    class Gather:
        def __init__(self, name, every, body=(), first=None):
            self.name, self.every, self.body, self.first = name, every, body, first

        def copies(self, origin, step):
            block = self.every.at[(origin,) + self.body]
            found = [(to_depth(block, block, self.name, step), True)]
            if self.first is not None:
                block = self.every.at[(origin,) + self.first]
                found.append((to_depth(block, block, self.name, step, z_extra), origin == 0))
            return found

        def passed(self):
            kind, origin = sh.z_kinds[self.name], below(2)
            target, step = (Z - 1) * (mz - 1), 2 * mz - 1
            found = []
            for part, sems, holds in ((self.body, z_sem, True), (self.first, z_extra, origin == 0)):
                if part is None:
                    continue
                block = self.every.at[(origin,) + part]
                found.append(
                    (
                        remote(block, block, sems, kind, 0, step, me, target),
                        holds,
                    )
                )
            return found

        def each(self, found, condition, act):
            for copy, holds in found:

                @pl.when(condition & holds)
                def _():
                    act(copy)

        def start(self):
            for step in order:
                self.each(self.copies(mz, step), direct(step), lambda c: c.start())

        def arrival(self, step):
            self.each(self.copies(below(step), step), mz >= 0, lambda c: c.wait_recv())

        def relay(self):
            if relayed:
                self.arrival(2)
                self.each(self.passed(), between, lambda c: c.start())

        def rest(self):
            return tuple(step for step in order if not (relayed and step == 2))

        def finish(self):
            for step in order:
                self.each(self.copies(mz, step), direct(step), lambda c: c.wait_send())
            if relayed:
                self.each(self.passed(), between, lambda c: c.wait_send())

    def windows(name, every):
        return Gather(name, every, (tail,), (head,))

    def put_out(every, name, positions):
        for position in positions:
            out = outputs[name]
            store(every.at[position, tail], out.at[tail_of(position)])
            store(every.at[position, head], out.at[head], position == 0)

    def put_together(every, dest):
        dest[0:TILE] = every[0, 0:TILE]
        for position in range(Z):
            dest[TILE + S * position : TILE + S * (position + 1)] = every[position, TILE:W]

    def scatters(name, part, recv, passing):
        return [
            Scatter(f"{name}{c}", part.at[c], recv.at[c], passing.at[c]) for c in range(NC)
        ]

    window = window_of(mz)
    own = (lax.broadcasted_iota(jnp.int32, (W, 1), 0) >= TILE) | (mz == 0)

    loaded("ids_row", "images_live", "noise_row")
    live_rows = images_live[...].reshape(1, 1) * TOK_IMG
    lane = lax.broadcasted_iota(jnp.int32, (1, R), 1)
    live = (lane < live_rows).astype(F32)
    expert_of = lax.broadcasted_iota(jnp.int32, (E, R), 0)
    ids = ids_row[...]
    hot = [(expert_of == ids[k : k + 1]).astype(F32) * live for k in range(2)]
    earlier = (
        lax.broadcasted_iota(jnp.int32, (R, R), 0) < lax.broadcasted_iota(jnp.int32, (R, R), 1)
    ).astype(BF16)
    counts = [nn(h.astype(BF16), earlier) for h in hot]
    counts[1] = counts[1] + jnp.sum(hot[0], axis=1, keepdims=True)
    start = expert_of.astype(F32) * CP
    spot = [
        jnp.where(live > 0, jnp.sum(hot[k] * (counts[k] + start), axis=0, keepdims=True), -1.0)
        for k in range(2)
    ]
    blank = jnp.zeros((1, RP - R), F32)
    live, *hot = (
        jnp.concatenate([v, jnp.zeros((v.shape[0], RP - R), F32)], axis=1) for v in (live, *hot)
    )
    noise = jnp.concatenate([noise_row[...], jnp.zeros((2, RP - R), F32)], axis=1)
    spot_row = [jnp.concatenate([s, blank - 1.0], axis=1).astype(jnp.int32) for s in spot]
    eye_rows = lax.broadcasted_iota(jnp.int32, (RP, RP), 0) == lax.broadcasted_iota(
        jnp.int32, (RP, RP), 1
    )
    spot_col = [
        jnp.sum(jnp.where(eye_rows, s.astype(F32), 0.0), axis=1, keepdims=True).astype(jnp.int32)
        for s in spot_row
    ]

    def spread(e):
        slot = lax.broadcasted_iota(jnp.int32, (CP, RP), 0) + e * CP
        return slot == spot_row[0], slot == spot_row[1]

    eye_slots = lax.broadcasted_iota(jnp.int32, (CP, CL), 0) == lax.broadcasted_iota(
        jnp.int32, (CP, CL), 1
    )

    def as_row(column):
        return jnp.sum(jnp.where(eye_slots, column, 0.0), axis=0, keepdims=True)

    def as_column(row):
        return jnp.sum(jnp.where(eye_slots, row, 0.0), axis=1, keepdims=True)

    loaded("wout")
    pl.semaphore_wait(barrier, E - 1 + Z - 1)
    half = D // 2
    core = lax.rem(me, 2)
    sibling = me + 1 - 2 * core
    columns = pl.ds(pl.multiple_of(core * half, 128), half)
    weights = Gather("w", m["wfull"], (slice(None), columns))
    weights.start()

    row_of = lax.broadcasted_iota(jnp.int32, (R, 1), 0)
    og, pt = m["og"], m["pt"]
    og[pl.ds(RP - TILE, TILE)] = jnp.zeros((TILE, D), BF16)
    loaded("out_grad")
    og[0:R] = jnp.where(row_of < live_rows, m["out_grad"][...], jnp.zeros((), BF16))
    c_send, c_recv = m["c_send"], m["c_recv"]

    def pack_cotangent(step, carry):
        e = plane(step)
        s0, s1 = spread(e)
        c_send[e] = nn((s0 | s1).astype(BF16), og[...]).astype(BF16)

        @pl.when(step > 0)
        def _():
            to_plane(c_send.at[e], c_recv.at[me], "c", step).start()

        return carry

    lax.fori_loop(0, E, pack_cotangent, 0)
    c_recv[me] = c_send[me]

    pt[pl.ds(RP - TILE, TILE)] = jnp.zeros((TILE, D), BF16)
    loaded("patches", "gain1", "bias1", "gain2", "bias2", "router_t")
    pt[0:R] = m["patches"][...]
    first_low, wqkv = m["first_low"], m["wqkv"]
    g1, b1 = gain1[...].reshape(1, D), bias1[...].reshape(1, D)
    g2, b2 = gain2[...].reshape(1, D), bias2[...].reshape(1, D)
    normal, _ = normalize(pt[...].astype(F32))
    first_low[...] = (normal * g1 + b1).astype(BF16)
    loaded("wqkv")
    projected = nt(first_low[...], wqkv[...]).astype(BF16)
    q_s, k_s, v_s, probs_s = m["q_s"], m["k_s"], m["v_s"], m["probs_s"]
    for h in range(sh.heads):
        for part, dest in enumerate((q_s, k_s, v_s)):
            begin = part * sh.local + h * HEAD_DIM
            dest[h] = projected[:, begin : begin + HEAD_DIM]
    row2 = lax.broadcasted_iota(jnp.int32, (RP, RP), 0)
    col2 = lax.broadcasted_iota(jnp.int32, (RP, RP), 1)
    same = ((row2 >= TOK_IMG) == (col2 >= TOK_IMG)) & (col2 < R)
    scale = HEAD_DIM ** (-0.5)
    heads = []
    for h in range(sh.heads):
        scores = jnp.where(same, nt(q_s[h], k_s[h]) * scale, -1e30)
        exponent = jnp.exp(scores - jnp.max(scores, axis=1, keepdims=True))
        probs = exponent / jnp.sum(exponent, axis=1, keepdims=True)
        probs_s[h] = probs
        heads.append(nn(probs.astype(BF16), v_s[h]).astype(BF16))
    mixed, mixed_all = m["mixed"], m["mixed_all"]
    mixed[...] = jnp.concatenate(heads, axis=1)
    HR, L = sh.half_rows, sh.local
    mixed_all[mz] = jnp.concatenate([mixed[0:HR], mixed[RP - HR : RP]], axis=1)
    mixing = Gather("m", mixed_all)
    mixing.start()

    wfull = m["wfull"]

    def to_sibling(step):
        block = wfull.at[below(step), :, columns]
        return remote(block, block, w_sem, 0, step, step, sibling, mz)

    weights.relay()
    if relayed:
        to_sibling(2).start()
    for step in weights.rest():
        weights.arrival(step)
        to_sibling(step).start()

    resid, second_low = m["resid"], m["second_low"]

    def attend(position):
        block = mixed_all[position]
        weight = wfull[position]
        return nn(block[:, 0:L], weight), nn(block[2 * HR - RP :, L : 2 * L], weight)

    low, high = attend(mz)
    resid[0:HR] = pt[0:HR].astype(F32) + low
    resid[HR:RP] = pt[HR:RP].astype(F32) + high
    mixing.relay()
    for step in order:
        if not (relayed and step == 2):
            mixing.arrival(step)
        to_sibling(step).wait_recv()
        low, high = attend(below(step))
        resid[0:HR] += low
        resid[HR:RP] += high

    normal, _ = normalize(resid[...])
    second_low[...] = (normal * g2 + b2).astype(BF16)
    logits = nt(router_t[...], second_low[...])
    chosen = [
        jnp.sum(hot[k] * logits, axis=0, keepdims=True) + noise[k : k + 1, :] for k in range(2)
    ]
    top = jnp.maximum(chosen[0], chosen[1])
    powers = [jnp.exp(c - top) for c in chosen]
    gates = [p / (powers[0] + powers[1]) for p in powers]
    x_send, x_recv, g_send, g_recv = m["x_send"], m["x_recv"], m["g_send"], m["g_recv"]

    def pack_rows(step, carry):
        e = plane(step)
        s0, s1 = spread(e)
        x_send[e] = nn((s0 | s1).astype(BF16), second_low[...]).astype(BF16)
        gate = jnp.sum(
            jnp.where(s0, gates[0], 0.0) + jnp.where(s1, gates[1], 0.0), axis=1, keepdims=True
        )
        g_send[e] = jnp.broadcast_to(as_row(gate), (8, CL))

        @pl.when(step > 0)
        def _():
            to_plane(g_send.at[e], g_recv.at[me], "g", step).start()
            to_plane(x_send.at[e], x_recv.at[me], "x", step).start()

        return carry

    lax.fori_loop(0, E, pack_rows, 0)
    g_recv[me] = g_send[me]
    x_recv[me] = x_send[me]
    place = m["place"]
    slot_lane = lax.broadcasted_iota(jnp.int32, (RP, E * CP), 1)
    place[...] = ((slot_lane == spot_col[0]) | (slot_lane == spot_col[1])).astype(BF16)

    loaded("up", "down")
    up, down, act, slope = m["up"], m["down"], m["act"], m["slope"]
    delta, hid, eo_send, eo_home = m["delta"], m["hid"], m["eo_send"], m["eo_home"]
    gg_send, gg_home, ei_home = m["gg_send"], m["gg_home"], m["ei_home"]

    def forward(step, carry):
        group = before(step)

        @pl.when(step > 0)
        def _():
            to_plane(g_send.at[0], g_recv.at[group], "g", step).wait_recv()
            to_plane(x_send.at[0], x_recv.at[group], "x", step).wait_recv()
            to_plane(c_send.at[0], c_recv.at[group], "c", step).wait_recv()

        hidden = nn(x_recv[group], up[...])
        below_it = 0.5 * (1.0 + lax.erf(hidden * (0.5**0.5)))
        bell = jnp.exp(-0.5 * hidden * hidden) * 0.3989422804014327
        act[group] = (hidden * below_it).astype(BF16)
        slope[group] = (below_it + hidden * bell).astype(BF16)
        result = nn(act[group], down[...])
        gate = as_column(g_recv[group][0:1])
        given = c_recv[group].astype(F32)
        dots = jnp.sum(given * result, axis=1, keepdims=True)
        gg_send[group] = jnp.broadcast_to(as_row(dots), (8, CL))
        eo_send[group] = (gate * result).astype(BF16)
        delta[group] = (gate * given).astype(BF16)

        @pl.when(step > 0)
        def _():
            back_to(gg_send.at[group], gg_home.at[me], "gg", step).start()
            back_to(eo_send.at[group], eo_home.at[me], "eo", step).start()

        return carry

    lax.fori_loop(0, E, forward, 0)
    gg_home[me] = gg_send[me]
    eo_home[me] = eo_send[me]

    def cotangent_left(step, carry):
        to_plane(c_send.at[0], c_recv.at[0], "c", step).wait_send()
        return carry

    lax.fori_loop(1, E, cotangent_left, 0)
    ei_send = c_send

    def lanes(c):
        return pl.ds(c * CW, CW)

    for c in range(NC):

        def backward(step, carry):
            group = before(step)
            if c == 0:
                hid[group] = (nt(delta[group], down[...]) * slope[group]).astype(BF16)
            ei_send[group, :, lanes(c)] = nt(hid[group], up[lanes(c), :]).astype(BF16)

            @pl.when(step > 0)
            def _():
                back_to(
                    ei_send.at[group, :, lanes(c)], ei_home.at[me, :, lanes(c)], f"ei{c}", step
                ).start()

            return carry

        lax.fori_loop(0, E, backward, 0)
    ei_home[me] = ei_send[me]

    strip = 128
    F = up.shape[1]
    acc = m["acc"]

    def flat(ref, first, size):
        return ref[:, :, pl.ds(pl.multiple_of(first, 128), size)].reshape(E * CP, size)

    def strip_copy(i, out, slot):
        return pltpu.make_async_copy(
            acc.at[slot], out.at[pl.ds(pl.multiple_of(i * strip, strip), strip)], local_sem.at[slot]
        )

    def strips(out, lhs, rhs, count, slot):
        def one(i, carry):
            at = slot + lax.rem(i, 2)

            @pl.when(i >= 2)
            def _():
                strip_copy(i - 2, out, at).wait()

            acc[at] = tn(flat(lhs, i * strip, strip), flat(rhs, 0, rhs.shape[2])).astype(BF16)
            strip_copy(i, out, at).start()
            return carry

        lax.fori_loop(0, count, one, 0)

    strips(outputs["up_out"], x_recv, hid, D // strip, 0)
    strips(outputs["down_out"], act, delta, F // strip, 2)

    mix_part, in_part = m["mix_part"], m["in_part"]
    mixes = scatters("mix", mix_part, m["mix_recv"], m["mix_pass"])
    for step in range(1, E):
        to_plane(eo_send.at[0], eo_home.at[plane(step)], "eo", step).wait_recv()
    for c in range(NC):
        home = eo_home[:, :, lanes(c)].reshape(E * CP, CW)
        mix_part[c] = nn(place[...], home).astype(BF16)
        mixes[c].start()
    for step in range(1, E):
        to_plane(gg_send.at[0], gg_home.at[plane(step)], "gg", step).wait_recv()

    def pick_dots(e, totals):
        s0, s1 = spread(e)
        column = as_column(gg_home[e][0:1])
        return (
            totals[0] + jnp.sum(jnp.where(s0, column, 0.0), axis=0, keepdims=True),
            totals[1] + jnp.sum(jnp.where(s1, column, 0.0), axis=0, keepdims=True),
        )

    nothing = jnp.zeros((1, RP), F32)
    dots0, dots1 = lax.fori_loop(0, E, pick_dots, (nothing, nothing))
    gz_send, gz_recv = m["gz_send"], m["gz_recv"]
    gz_send[...] = jnp.zeros((8, RP), F32)
    gz_send[0:1] = dots0
    gz_send[1:2] = dots1
    for step in range(1, Z):
        to_depth(gz_send, gz_recv.at[mz], "gz", step).start()
    for mix in mixes:
        mix.relay()
    gate_grad = gz_send[...]
    for step in range(1, Z):
        to_depth(gz_send, gz_recv.at[below(step)], "gz", step).wait_recv()
        gate_grad = gate_grad + gz_recv[below(step)]
    both = gates[0] * gate_grad[0:1] + gates[1] * gate_grad[1:2]
    logit_grad = sum(hot[k] * (gates[k] * (gate_grad[k : k + 1] - both)) for k in range(2))
    parts = in_three(logit_grad)
    router_grad = sum(nn(p, second_low[...]) for p in parts)
    rterm = m["rterm"]
    rterm[...] = sum(tn(p, router_t[...]) for p in parts)

    ins = scatters("in", in_part, m["in_recv"], m["in_pass"])
    bo_all, pg_all = m["bo_all"], m["pg_all"]
    bo_gather = windows("bo", bo_all)
    for c in range(NC):
        for step in range(1, E):
            to_plane(
                ei_send.at[0, :, lanes(c)], ei_home.at[plane(step), :, lanes(c)], f"ei{c}", step
            ).wait_recv()
        home = ei_home[:, :, lanes(c)].reshape(E * CP, CW)
        in_part[c] = nn(place[...], home).astype(BF16)
        ins[c].start()
        if c == 0:
            mixture = jnp.concatenate([mix.total() for mix in mixes], axis=1)
            at = lax.broadcasted_iota(jnp.int32, (W, 1), 0) + mz * S
            bo_all[mz] = jnp.where(at < live_rows, resid[window] + mixture, 0.0).astype(BF16)
            bo_gather.start()
        ins[c].relay()
        if c == NC - 2:
            bo_gather.relay()

    cot = og[window].astype(F32)
    normal, spread_scale = normalize(resid[window])
    second_grad = jnp.concatenate([part.total() for part in ins], axis=1) + rterm[window]
    resid_grad = cot + norm_back(normal, spread_scale, second_grad * g2)
    resid_win = m["resid_win"]
    resid_win[...] = resid_grad
    attended_grad = jnp.where(own, resid_grad, 0.0).astype(BF16)
    mg_send, mg_recv = m["mg_send"], m["mg_recv"]

    def to_heads(step, sent, received):
        yield to_depth(mg_send.at[sent, tail], mg_recv.at[received, tail], "mg", step), mz >= 0
        first = to_depth(
            mg_send.at[sent, head], mg_recv.at[received, head], "mg", step, z_extra
        )
        yield first, received == 0

    def each(found, act):
        for copy, condition in found:

            @pl.when(condition)
            def _():
                act(copy)

    for step in order:
        mg_send[above(step)] = nt(attended_grad, wfull[above(step)]).astype(BF16)
        each(to_heads(step, above(step), mz), lambda c: c.start())
    mg_recv[mz] = nt(attended_grad, wfull[mz]).astype(BF16)
    sz_send, sz_recv = m["sz_send"], m["sz_recv"]
    sz_send[...] = jnp.zeros((8, D), F32)
    sz_send[0:1] = jnp.sum(jnp.where(own, second_grad * normal, 0.0), axis=0, keepdims=True)
    sz_send[1:2] = jnp.sum(jnp.where(own, second_grad, 0.0), axis=0, keepdims=True)
    for step in range(1, Z):
        to_depth(sz_send, sz_recv.at[mz], "sz", step).start()

    B, BP = sh.share, sh.share_rows
    qg_send, qg_recv, og_wsend, og_wrecv = (
        m[n] for n in ("qg_send", "qg_recv", "og_wsend", "og_wrecv")
    )
    lower = mz < Z // 2
    at_rows = pl.ds(pl.multiple_of(lax.rem(mz, Z // 2) * S, TILE), W)
    mixed_win = jnp.concatenate(
        [
            jnp.where(
                lower, mixed_all[p, at_rows][:, 0:L], mixed_all[p, at_rows][:, L : 2 * L]
            )
            for p in range(Z)
        ],
        axis=1,
    )
    wout_grad = tn(attended_grad, mixed_win)
    for e in range(E):
        og_wsend[e, 0:B] = wout_grad[e * B : (e + 1) * B].astype(BF16)
    for step in range(1, E):
        to_plane(og_wsend.at[plane(step)], og_wrecv.at[me], "og", step).start()
    for step in order:
        each(to_heads(step, 0, below(step)), lambda c: c.wait_recv())
    mixed_grad = m["mixed_grad"]
    put_together(mg_recv, mixed_grad)

    grads = [[], [], []]
    for h in range(sh.heads):
        mg = mixed_grad[:, h * HEAD_DIM : (h + 1) * HEAD_DIM]
        probs = probs_s[h]
        prob_grad = nt(mg, v_s[h])
        score_grad = (
            probs * (prob_grad - jnp.sum(prob_grad * probs, axis=1, keepdims=True))
        ).astype(BF16)
        grads[0].append((nn(score_grad, k_s[h]) * scale).astype(BF16))
        grads[1].append((tn(score_grad, q_s[h]) * scale).astype(BF16))
        grads[2].append(tn(probs.astype(BF16), mg).astype(BF16))
    projected_grad = jnp.concatenate(grads[0] + grads[1] + grads[2], axis=1)
    for mix in mixes:
        mix.finish()
    first_part = mix_part
    firsts = scatters("first", first_part, m["first_recv"], m["first_pass"])
    for c in range(NC):
        first_part[c] = nn(projected_grad, wqkv[:, lanes(c)]).astype(BF16)
        firsts[c].start()

    qkv_grad = tn(first_low[...], projected_grad)
    for e in range(E):
        qg_send[e, 0:B] = qkv_grad[e * B : (e + 1) * B].astype(BF16)
    for step in range(1, E):
        to_plane(qg_send.at[plane(step)], qg_recv.at[me], "qg", step).start()
    for first in firsts:
        first.relay()
    sp_send, sp_recv, fp_send, fp_recv = (m[n] for n in ("sp_send", "sp_recv", "fp_send", "fp_recv"))
    sums = sz_send[...]
    for step in range(1, Z):
        to_depth(sz_send, sz_recv.at[below(step)], "sz", step).wait_recv()
        sums = sums + sz_recv[below(step)]
    sp_send[0:E] = router_grad
    sp_send[E : E + 4] = sums[0:4]
    for step in range(1, E):
        to_plane(sp_send, sp_recv.at[me], "sp", step).start()

    for step in bo_gather.rest():
        bo_gather.arrival(step)
    put_out(bo_all, "block_out", range(Z))

    wz_send, wz_recv = m["wz_send"], m["wz_recv"]
    total_w = og_wsend[me].astype(F32)
    for step in range(1, E):
        source = before(step)
        to_plane(og_wsend.at[0], og_wrecv.at[source], "og", step).wait_recv()
        total_w = total_w + og_wrecv[source].astype(F32)
    for position in range(Z):
        wz_send[position] = total_w[:, position * L : (position + 1) * L].astype(BF16)
    for step in order:
        to_depth(wz_send.at[above(step)], wz_recv.at[mz], "wz", step).start()

    normal, spread_scale = normalize(pt[window].astype(F32))
    first_grad = jnp.concatenate([first.total() for first in firsts], axis=1)
    patch_grad = resid_win[...] + norm_back(normal, spread_scale, first_grad * g1)
    pg_all[mz] = patch_grad.astype(BF16)
    pg_gather = windows("pg", pg_all)
    fz_send, fz_recv = m["fz_send"], m["fz_recv"]
    fz_send[...] = jnp.zeros((8, D), F32)
    fz_send[0:1] = jnp.sum(jnp.where(own, first_grad * normal, 0.0), axis=0, keepdims=True)
    fz_send[1:2] = jnp.sum(jnp.where(own, first_grad, 0.0), axis=0, keepdims=True)
    for step in range(1, Z):
        to_depth(fz_send, fz_recv.at[mz], "fz", step).start()
    pg_gather.start()
    sums = fz_send[...]
    for step in range(1, Z):
        to_depth(fz_send, fz_recv.at[below(step)], "fz", step).wait_recv()
        sums = sums + fz_recv[below(step)]
    fp_send[...] = sums
    for step in range(1, E):
        to_plane(fp_send, fp_recv.at[me], "fp", step).start()

    pg_gather.relay()
    total = qg_send[me].astype(F32)
    total_s = sp_send[...]
    for step in range(1, E):
        source = before(step)
        to_plane(qg_send.at[0], qg_recv.at[source], "qg", step).wait_recv()
        total = total + qg_recv[source].astype(F32)
        to_plane(sp_send, sp_recv.at[source], "sp", step).wait_recv()
        total_s = total_s + sp_recv[source]
    qkv_sum, wout_sum, small_sum = m["qkv_sum"], m["wout_sum"], m["small_sum"]
    for part in range(3):
        qkv_sum[part] = total[0:B, part * L : (part + 1) * L]
    store(qkv_sum, outputs["qkv_out"])
    total_w = wz_send[mz].astype(F32)
    for step in order:
        to_depth(wz_send.at[0], wz_recv.at[below(step)], "wz", step).wait_recv()
        total_w = total_w + wz_recv[below(step)].astype(F32)
    wout_sum[...] = total_w[0:B]
    store(wout_sum, outputs["wout_out"])
    small_sum[...] = jnp.zeros((sh.small, D), F32)
    small_sum[0:E] = total_s[0:E]
    small_sum[E : E + 2] = total_s[E : E + 2]
    total_f = fp_send[...]
    for step in range(1, E):
        source = before(step)
        to_plane(fp_send, fp_recv.at[source], "fp", step).wait_recv()
        total_f = total_f + fp_recv[source]
    small_sum[E + 2 : E + 4] = total_f[0:2]
    store(small_sum, outputs["small_out"])

    for step in (0,) + order:
        position = below(step)
        if step and not (relayed and step == 2):
            pg_gather.arrival(step)
        put_out(pg_all, "patches_grad", [position])

    for step in range(1, Z):
        to_sibling(step).wait_send()

    def sent(step, carry):
        to_plane(g_send.at[0], g_recv.at[0], "g", step).wait_send()
        to_plane(x_send.at[0], x_recv.at[0], "x", step).wait_send()
        back_to(gg_send.at[0], gg_home.at[0], "gg", step).wait_send()
        back_to(eo_send.at[0], eo_home.at[0], "eo", step).wait_send()
        for c in range(NC):
            back_to(
                ei_send.at[0, :, lanes(c)], ei_home.at[0, :, lanes(c)], f"ei{c}", step
            ).wait_send()
        to_plane(qg_send.at[0], qg_recv.at[0], "qg", step).wait_send()
        to_plane(og_wsend.at[0], og_wrecv.at[0], "og", step).wait_send()
        to_plane(sp_send, sp_recv.at[0], "sp", step).wait_send()
        to_plane(fp_send, fp_recv.at[0], "fp", step).wait_send()
        return carry

    lax.fori_loop(1, E, sent, 0)
    for scatter in ins + firsts:
        scatter.finish()
    for gather in (weights, mixing, bo_gather, pg_gather):
        gather.finish()
    for step in range(1, Z):
        each(to_heads(step, 0, mz), lambda c: c.wait_send())
        to_depth(wz_send.at[0], wz_recv.at[0], "wz", step).wait_send()
        to_depth(gz_send, gz_recv.at[0], "gz", step).wait_send()
        to_depth(sz_send, sz_recv.at[0], "sz", step).wait_send()
        to_depth(fz_send, fz_recv.at[0], "fz", step).wait_send()
    for last in (2, 1):
        strip_copy(D // strip - last, outputs["up_out"], (D // strip - last) % 2).wait()
        strip_copy(F // strip - last, outputs["down_out"], 2 + (F // strip - last) % 2).wait()
    for copy, condition in stores:
        if condition is None:
            copy.wait()
        else:

            @pl.when(condition)
            def _():
                copy.wait()


def scratch_of(sh, F):
    E, Z, RP, R, D, NC = sh.experts, sh.depth, sh.padded, sh.rows, sh.width, sh.chunks
    CP, CL, CW, W = sh.slots, sh.slot_lanes, sh.chunk, sh.window
    B, BP = sh.share, sh.share_rows
    L, H = sh.local, sh.heads
    blocks = ((E, CP, D), BF16)
    dots = ((E, 8, CL), F32)
    rows = ((RP, D), BF16)
    part = ((NC, RP, CW), BF16)
    recv = ((NC, Z, W, CW), BF16)
    passing = ((NC, W, CW), BF16)
    every = ((Z, W, D), BF16)
    head = ((H, RP, HEAD_DIM), BF16)
    shapes = {
        "gain1": ((D,), F32),
        "bias1": ((D,), F32),
        "gain2": ((D,), F32),
        "bias2": ((D,), F32),
        "router_t": ((E, D), BF16),
        "ids_row": ((2, R), jnp.int32),
        "noise_row": ((2, R), F32),
        "images_live": ((1,), jnp.int32),
        "patches": ((R, D), BF16),
        "out_grad": ((R, D), BF16),
        "up": ((D, F), BF16),
        "down": ((F, D), BF16),
        "wqkv": ((3 * L, D), BF16),
        "wfull": ((Z, L, D), BF16),
        "pt": rows,
        "og": rows,
        "first_low": rows,
        "q_s": head,
        "k_s": head,
        "v_s": head,
        "probs_s": ((H, RP, RP), F32),
        "mixed": ((RP, L), BF16),
        "mixed_all": ((Z, sh.half_rows, 2 * L), BF16),
        "resid": ((RP, D), F32),
        "second_low": rows,
        "place": ((RP, E * CP), BF16),
        "x_send": blocks,
        "x_recv": blocks,
        "c_send": blocks,
        "c_recv": blocks,
        "g_send": dots,
        "g_recv": dots,
        "act": ((E, CP, F), BF16),
        "slope": ((E, CP, F), BF16),
        "delta": blocks,
        "hid": ((E, CP, F), BF16),
        "eo_send": blocks,
        "eo_home": blocks,
        "ei_home": blocks,
        "gg_send": dots,
        "gg_home": dots,
        "acc": ((4, 128, max(F, D)), BF16),
        "mix_part": part,
        "mix_recv": recv,
        "mix_pass": passing,
        "in_part": part,
        "in_recv": recv,
        "in_pass": passing,
        "first_recv": recv,
        "first_pass": passing,
        "rterm": ((RP, D), F32),
        "resid_win": ((W, D), F32),
        "bo_all": every,
        "pg_all": every,
        "mg_send": ((Z, W, L), BF16),
        "mg_recv": ((Z, W, L), BF16),
        "mixed_grad": ((RP, L), BF16),
        "wz_send": ((Z, BP, L), BF16),
        "wz_recv": ((Z, BP, L), BF16),
        "gz_send": ((8, RP), F32),
        "gz_recv": ((Z, 8, RP), F32),
        "qg_send": ((E, BP, 3 * L), BF16),
        "qg_recv": ((E, BP, 3 * L), BF16),
        "og_wsend": ((E, BP, Z * L), BF16),
        "og_wrecv": ((E, BP, Z * L), BF16),
        "sz_send": ((8, D), F32),
        "sz_recv": ((Z, 8, D), F32),
        "sp_send": ((sh.small, D), F32),
        "sp_recv": ((E, sh.small, D), F32),
        "fz_send": ((8, D), F32),
        "fz_recv": ((Z, 8, D), F32),
        "fp_send": ((8, D), F32),
        "fp_recv": ((E, 8, D), F32),
        "qkv_sum": ((3, B, L), F32),
        "wout_sum": ((B, L), F32),
        "small_sum": ((sh.small, D), F32),
    }
    sems = {
        "local_sem": (4,),
        "in_sem": (len(INPUTS),),
        "out_sem": (4 * Z + 3,),
        "e_sem": (len(sh.e_kinds), 2, E),
        "z_sem": (len(sh.z_kinds), 2, Z),
        "z_extra": (len(sh.z_kinds), 2, Z),
        "w_sem": (1, 2, Z),
    }
    return [
        pltpu.VMEM(*shapes[n]) if n in shapes else pltpu.SemaphoreType.DMA(sems[n]) for n in SCRATCH
    ]


def outputs_kernel(sh, pieces, *refs):
    given, outs, held, made = refs[:7], refs[7:18], refs[18:25], refs[25:36]
    in_sem, out_sem = refs[36:]
    wout, small = held[5:]
    loads = [
        pltpu.make_async_copy(src, dst, in_sem.at[at])
        for at, (src, dst) in enumerate(zip(given[5:], (wout, small)))
    ]
    steps = []
    for src, through, ready, dst, number in zip(given, held, made, outs, pieces):
        rows = src.shape[0] // number
        for piece in range(number):
            at = pl.ds(piece * rows, rows)
            part = [ref if number == 1 else ref.at[at] for ref in (src, through, ready, dst)]
            load = pltpu.make_async_copy(part[0], part[1], in_sem.at[len(loads) + len(steps)])
            steps.append((load, part))
    for load in loads + [load for load, _ in steps]:
        load.start()
    for load in loads:
        load.wait()
    E, width = sh.experts, sh.width
    begin = lax.axis_index("expert") * sh.share
    mine = pltpu.roll(small[...], lax.rem(width - begin, width), 1)[:, 0 : sh.share]
    made[5][...] = wout[...].T
    made[6][...] = mine[0:E]
    for at, gain in enumerate(made[7:]):
        gain[...] = mine[E + at]
    stores = []

    def store(src, dst):
        stores.append(pltpu.make_async_copy(src, dst, out_sem.at[len(stores)]))
        stores[-1].start()

    for src, dst in zip(made[5:], outs[5:]):
        store(src, dst)
    for load, (_, through, ready, dst) in steps:
        load.wait()
        if through.dtype == ready.dtype:
            store(through, dst)
        else:
            ready[...] = through[...].astype(ready.dtype)
            store(ready, dst)
    for copy in stores:
        copy.wait()


def on_device(
    mesh,
    patches,
    first_gain,
    first_bias,
    qkv_weight,
    out_weight,
    second_gain,
    second_bias,
    router_weight,
    up_weight,
    down_weight,
    expert_ids,
    router_noise,
    images_live,
    out_grad,
):
    row_count, model_width = patches.shape
    local_width = out_weight.shape[0]
    sh = Shapes(mesh, row_count, model_width, local_width)
    hidden_width = up_weight.shape[2]
    E, RP, D = sh.experts, sh.padded, sh.width
    anywhere = pl.BlockSpec(memory_space=pl.ANY)
    slots = E * sh.slots
    flops = 2 * (
        6 * slots * D * hidden_width
        + 3 * RP * D * 4 * local_width
        + 4 * slots * RP * D
        + 7 * sh.heads * RP * RP * HEAD_DIM
    )
    outs = pl.pallas_call(
        functools.partial(whole_kernel, sh),
        out_shape=(
            jax.ShapeDtypeStruct((RP, D), BF16),
            jax.ShapeDtypeStruct((RP, D), BF16),
            jax.ShapeDtypeStruct((3, sh.share, local_width), F32),
            jax.ShapeDtypeStruct((sh.share, local_width), F32),
            jax.ShapeDtypeStruct((sh.small, D), F32),
            jax.ShapeDtypeStruct((D, hidden_width), BF16),
            jax.ShapeDtypeStruct((hidden_width, D), BF16),
        ),
        in_specs=[anywhere] * len(INPUTS),
        out_specs=(anywhere,) * len(OUTPUTS),
        scratch_shapes=scratch_of(sh, hidden_width),
        compiler_params=pltpu.CompilerParams(
            collective_id=0, has_side_effects=True, vmem_limit_bytes=62 << 20
        ),
        cost_estimate=pl.CostEstimate(flops=flops, bytes_accessed=16 << 20, transcendentals=0),
        name="block",
    )(
        first_gain,
        first_bias,
        second_gain,
        second_bias,
        router_weight.T,
        expert_ids.T,
        router_noise.T,
        images_live,
        out_weight,
        out_grad,
        patches,
        qkv_weight.transpose(1, 2, 0).reshape(3 * local_width, D),
        up_weight[0],
        down_weight[0],
    )
    block_out, patches_grad, qkv_grad, wout_grad, small, up_grad, down_grad = outs
    pieces = (1, 1, 1, 4, 4)
    wholes = (block_out[:row_count], patches_grad[:row_count], qkv_grad, up_grad, down_grad)
    inputs = wholes + (wout_grad, small)
    kinds = (BF16, F32, F32, F32, F32)
    results = tuple(jax.ShapeDtypeStruct(w.shape, kind) for w, kind in zip(wholes, kinds)) + (
        jax.ShapeDtypeStruct((local_width, sh.share), F32),
        jax.ShapeDtypeStruct((E, sh.share), F32),
    )
    results += (jax.ShapeDtypeStruct((sh.share,), F32),) * 4
    copies = sum(pieces)
    results = pl.pallas_call(
        functools.partial(outputs_kernel, sh, pieces),
        out_shape=results,
        in_specs=[anywhere] * len(inputs),
        out_specs=(anywhere,) * len(results),
        scratch_shapes=[pltpu.VMEM(w.shape, w.dtype) for w in inputs + results]
        + [pltpu.SemaphoreType.DMA((copies + 2,)), pltpu.SemaphoreType.DMA((copies + 6,))],
        compiler_params=pltpu.CompilerParams(vmem_limit_bytes=62 << 20),
        name="outputs",
    )(*inputs)
    block_out, patches_grad, qkv_grad, up_grad, down_grad, wout_grad, router_grad = results[:7]
    gain2_grad, bias2_grad, gain1_grad, bias1_grad = results[7:]
    return (
        block_out,
        patches_grad,
        gain1_grad,
        bias1_grad,
        qkv_grad.transpose(1, 0, 2),
        wout_grad,
        gain2_grad,
        bias2_grad,
        router_grad.T,
        up_grad[None],
        down_grad[None],
    )


def solution(mesh):
    placed = (
        P("expert", None),
        P(),
        P(),
        P(None, None, "tensor"),
        P("tensor", None),
        P(),
        P(),
        P(),
        P("expert", None, "tensor"),
        P("expert", "tensor", None),
        P("expert", None),
        P("expert", None),
        P("expert"),
        P("expert", None),
    )
    return jax.shard_map(
        functools.partial(on_device, mesh),
        mesh=mesh,
        in_specs=placed,
        out_specs=(
            P("expert", None),
            P("expert", None),
            P("expert"),
            P("expert"),
            P("expert", None, "tensor"),
            P("tensor", "expert"),
            P("expert"),
            P("expert"),
            P("expert", None),
            P("expert", None, "tensor"),
            P("expert", "tensor", None),
        ),
        check_vma=False,
    )
```

```python
import functools
from types import SimpleNamespace

import jax
import jax.numpy as jnp
from jax import lax
from jax.experimental import pallas as pl
from jax.experimental.pallas import tpu as pltpu
from jax.sharding import PartitionSpec as P

HEAD_DIM = 64
TOK_IMG = 197
TILE = 16
EPSILON = 1e-06
MESH = pl.DeviceIdType.MESH
F32 = jnp.float32
BF16 = jnp.bfloat16


def round_up(value, unit):
    return (value + unit - 1) // unit * unit


def nn(a, b):
    return lax.dot_general(a, b, (((1,), (0,)), ((), ())), preferred_element_type=F32)


def nt(a, b):
    return lax.dot_general(a, b, (((1,), (1,)), ((), ())), preferred_element_type=F32)


def tn(a, b):
    return lax.dot_general(a, b, (((0,), (0,)), ((), ())), preferred_element_type=F32)


def in_three(values):
    high = values.astype(BF16)
    rest = values - high.astype(F32)
    middle = rest.astype(BF16)
    return high, middle, (rest - middle.astype(F32)).astype(BF16)


def normalize(values):
    center = values - jnp.mean(values, axis=-1, keepdims=True)
    scale = lax.rsqrt(jnp.mean(center * center, axis=-1, keepdims=True) + EPSILON)
    return center * scale, scale


def norm_back(normal, scale, grad_normal):
    return scale * (
        grad_normal
        - jnp.mean(grad_normal, axis=-1, keepdims=True)
        - normal * jnp.mean(grad_normal * normal, axis=-1, keepdims=True)
    )


class Shapes:
    def __init__(self, mesh, row_count, model_width, local_width):
        self.experts = mesh.shape["expert"]
        self.depth = mesh.shape["tensor"]
        self.rows = row_count
        self.width = model_width
        self.local = local_width
        self.heads = local_width // HEAD_DIM
        self.padded = round_up(row_count, TILE)
        self.capacity = (3 * row_count + self.experts - 1) // self.experts
        self.slots = round_up(self.capacity, TILE)
        self.split = self.depth * TILE if self.slots >= 2 * self.depth * TILE else 0
        self.common = self.slots - self.split
        self.slot_lanes = round_up(self.slots, 128)
        self.step = (self.padded - TILE) // self.depth
        self.window = self.step + TILE
        self.share = model_width // self.experts
        self.share_rows = round_up(self.share, TILE)
        self.small = round_up(self.experts + 4, 8)
        self.near_lanes = min(256, model_width)
        self.half_rows = round_up(self.padded // 2, TILE)
        self.chunk = 256
        self.chunks = model_width // self.chunk
        (
            self.e_c,
            self.e_g,
            self.e_x,
            self.e_gg,
            self.e_eo,
            self.e_xs,
            self.e_ei,
        ) = range(7)
        self.e_kinds = self.e_ei + self.chunks
        self.chips = self.experts // 2
        self.s_w, self.s_qg, self.s_og, self.s_sp = range(4)
        self.s_kinds = 4
        (
            self.z_w,
            self.z_m,
            self.z_gz,
            self.z_bo,
            self.z_mg,
            self.z_wz,
            self.z_pg,
            self.z_zs,
            self.z_mix,
            self.z_first,
            self.z_x,
        ) = range(11)
        self.z_in = self.z_x + 2
        self.z_kinds = self.z_in + self.chunks


    def near(self, expert):
        return jnp.minimum(expert * self.share // 128 * 128, self.width - self.near_lanes)


def whole_kernel(sh, fields, *refs):
    E, Z, NC = sh.experts, sh.depth, sh.chunks
    R, RP, D = sh.rows, sh.padded, sh.width
    CP, CL, CW = sh.slots, sh.slot_lanes, sh.chunk
    taken = iter(refs)
    inputs, outputs, m = (SimpleNamespace(**{f: next(taken) for f in group}) for group in fields)
    e_sem, z_sem, z_extra, s_sem, c_sem = m.e_sem, m.z_sem, m.z_extra, m.s_sem, m.c_sem
    local_sem, in_sem, out_sem = m.local_sem, m.in_sem, m.out_sem
    me = lax.axis_index("expert")
    mz = lax.axis_index("tensor")

    def plane(step):
        return lax.rem(me + step, E)

    def before(step):
        return lax.rem(me - step + E, E)

    def above(step):
        return lax.rem(mz + step, Z)

    def below(step):
        return lax.rem(mz - step + Z, Z)

    def remote(src, dst, sems, kind, sent, received, expert, position):
        return pltpu.make_async_remote_copy(
            src_ref=src,
            dst_ref=dst,
            send_sem=sems.at[kind, 0, sent],
            recv_sem=sems.at[kind, 1, received],
            device_id=(expert, position),
            device_id_type=MESH,
        )

    def to_plane(src, dst, kind, step):
        return remote(src, dst, e_sem, kind, step, step, plane(step), mz)

    core = lax.rem(me, 2)
    chip = me // 2
    sibling = me + 1 - 2 * core

    def to_sibling(src, dst, kind, step=0):
        return remote(src, dst, s_sem, kind, step, step, sibling, mz)

    def to_chip(src, dst, kind, step):
        target = lax.rem(chip + step, sh.chips)
        return remote(src, dst, c_sem, kind, step, step, 2 * target + core, mz)

    def chip_after(step):
        return lax.rem(chip + step, sh.chips)

    def chip_before(step):
        return lax.rem(chip - step + sh.chips, sh.chips)

    class ChipSum:
        def __init__(self, kind, send, pair, recv):
            self.kind, self.send, self.pair, self.recv = kind, send, pair, recv

        def halves(self):
            return to_sibling(self.send.at[1 - core], self.pair, self.kind)

        def start(self):
            self.halves().start()

        def cross(self):
            self.halves().wait_recv()
            half = self.send[core].astype(F32) + self.pair[...].astype(F32)
            self.send[core] = half.astype(self.send.dtype)
            for step in range(1, sh.chips):
                self.block(step, chip_after(step)).start()

        def block(self, step, target):
            return to_chip(self.send.at[core, target], self.recv.at[chip], self.kind, step)

        def total(self):
            value = self.send[core, chip].astype(F32)
            for step in range(1, sh.chips):
                source = chip_before(step)
                to_chip(
                    self.send.at[core, 0], self.recv.at[source], self.kind, step
                ).wait_recv()
                value = value + self.recv[source].astype(F32)
            return value

        def finish(self):
            self.halves().wait_send()
            for step in range(1, sh.chips):
                self.block(step, 0).wait_send()

    class SmallSum:
        def __init__(self, kind, send, pair, half, recv):
            self.kind, self.send, self.pair, self.half, self.recv = kind, send, pair, half, recv

        def exchange(self):
            return to_sibling(self.send, self.pair, self.kind)

        def start(self):
            self.exchange().start()

        def cross(self):
            self.exchange().wait_recv()
            self.half[...] = self.send[...] + self.pair[...]
            for step in range(1, sh.chips):
                to_chip(self.half, self.recv.at[chip], self.kind, step).start()

        def total(self):
            value = self.half[...]
            for step in range(1, sh.chips):
                source = chip_before(step)
                to_chip(self.half, self.recv.at[source], self.kind, step).wait_recv()
                value = value + self.recv[source]
            return value

        def finish(self):
            self.exchange().wait_send()
            for step in range(1, sh.chips):
                to_chip(self.half, self.recv.at[chip], self.kind, step).wait_send()

    def back_to(src, dst, kind, step):
        return remote(src, dst, e_sem, kind, step, step, before(step), mz)

    def to_depth(src, dst, kind, step, sems=None):
        sems = z_sem if sems is None else sems
        return remote(src, dst, sems, kind, step, step, me, above(step))

    relayed = Z == 4
    between = (mz > 0) & (mz < Z - 1)

    def direct(step, hold=False):
        if not relayed:
            return mz >= 0
        if step == 1:
            return mz < Z - 1
        if step == Z - 1:
            return mz > 0
        return jnp.logical_not(between) if hold else mz >= 0

    def arrives(step):
        if not relayed:
            return mz >= 0
        if step == 1:
            return mz > 0
        if step == Z - 1:
            return mz < Z - 1
        return mz >= 0

    order = (2, 1, 3) if relayed else tuple(range(1, Z))

    m.wout = m.wfull.at[mz]
    loads = SimpleNamespace()
    for at, (field, source) in enumerate(vars(inputs).items()):
        copy = pltpu.make_async_copy(source, getattr(m, field), in_sem.at[at])
        copy.start()
        setattr(loads, field, copy)

    def loaded(*copies):
        for copy in copies:
            copy.wait()

    stores = []

    def store(src, dst, condition=None):
        copy = pltpu.make_async_copy(src, dst, out_sem.at[len(stores)])
        stores.append((copy, condition))
        if condition is None:
            copy.start()
        else:

            @pl.when(condition)
            def _():
                copy.start()

    gain1, bias1, gain2, bias2 = m.gain1, m.bias1, m.gain2, m.bias2
    router_t, ids_row, noise_row, images_live = m.router_t, m.ids_row, m.noise_row, m.images_live
    barrier = pltpu.get_barrier_semaphore()
    for step in range(1, E):
        pl.semaphore_signal(barrier, inc=1, device_id=(plane(step), mz), device_id_type=MESH)
    for step in range(1, Z):
        pl.semaphore_signal(barrier, inc=1, device_id=(me, above(step)), device_id_type=MESH)

    S, W = sh.step, sh.window

    def tail_of(position):
        if isinstance(position, int):
            return pl.ds(position * S + TILE, S)
        return pl.ds(pl.multiple_of(position * S + TILE, TILE), S)

    def window_of(position):
        return pl.ds(pl.multiple_of(position * S, TILE), W)

    head, tail = pl.ds(0, TILE), pl.ds(TILE, S)

    class Scatter:
        def __init__(self, kind, part, recv, passing):
            self.kind, self.part, self.recv, self.passing = kind, part, recv, passing

        def send_to(self, step):
            target = above(step)
            return (
                to_depth(self.part.at[tail_of(target)], self.recv.at[mz, tail], self.kind, step),
                to_depth(self.part.at[head], self.recv.at[mz, head], self.kind, step, z_extra),
                target == 0,
            )

        def pass_to(self):
            source = self.passing
            return (
                to_depth(source.at[tail], self.recv.at[mz, tail], self.kind, 2),
                to_depth(source.at[head], self.recv.at[mz, head], self.kind, 2, z_extra),
                above(2) == 0,
            )

        def far(self):
            kind = self.kind
            up_to, down_to = (
                remote(
                    self.part.at[tail_of(Z - 1 - end)],
                    self.passing.at[tail],
                    z_sem,
                    kind,
                    0,
                    0,
                    me,
                    1 if end == 0 else Z - 2,
                )
                for end in (0, Z - 1)
            )
            down_head = remote(
                self.part.at[head],
                self.passing.at[head],
                z_extra,
                kind,
                0,
                0,
                me,
                Z - 2,
            )
            return up_to, down_to, down_head

        def start(self):
            if relayed:
                up_to, down_to, down_head = self.far()

                @pl.when(mz == 0)
                def _():
                    up_to.start()

                @pl.when(mz == Z - 1)
                def _():
                    down_to.start()
                    down_head.start()

            for step in order:
                body, first, is_head = self.send_to(step)

                @pl.when(direct(step, hold=True))
                def _():
                    body.start()

                @pl.when(direct(step, hold=True) & is_head)
                def _():
                    first.start()

        def relay(self):
            if not relayed:
                return

            @pl.when(between)
            def _():
                up_to, down_to, down_head = self.far()
                up_to.wait_recv()

                @pl.when(mz == Z - 2)
                def _():
                    down_head.wait_recv()

                target = above(2)
                self.passing[...] = (
                    self.passing[...].astype(F32) + self.part[window_of(target)].astype(F32)
                ).astype(BF16)
                body, first, is_head = self.pass_to()
                body.start()

                @pl.when(is_head)
                def _():
                    first.start()

        def total(self):
            value = self.part[window_of(mz)].astype(F32)
            for step in order:
                source = below(step)
                here = arrives(step)
                body = to_depth(
                    self.part.at[tail_of(0)], self.recv.at[source, tail], self.kind, step
                )
                first = to_depth(
                    self.part.at[head], self.recv.at[source, head], self.kind, step, z_extra
                )

                @pl.when(here)
                def _():
                    body.wait_recv()

                @pl.when(here & (mz == 0))
                def _():
                    first.wait_recv()

                value = value + jnp.where(here, self.recv[source].astype(F32), 0.0)
            return value

        def finish(self):
            if relayed:
                up_to, down_to, down_head = self.far()

                @pl.when(mz == 0)
                def _():
                    up_to.wait_send()

                @pl.when(mz == Z - 1)
                def _():
                    down_to.wait_send()
                    down_head.wait_send()

            for step in order:
                body, first, is_head = self.send_to(step)

                @pl.when(direct(step))
                def _():
                    body.wait_send()

                @pl.when(direct(step) & is_head)
                def _():
                    first.wait_send()

    class Gather:
        def __init__(self, kind, every, body=(), first=None):
            self.kind, self.every, self.body, self.first = kind, every, body, first

        def blocks(self, origin):
            found = [(self.every.at[(origin,) + self.body], z_sem, True)]
            if self.first is not None:
                found.append((self.every.at[(origin,) + self.first], z_extra, origin == 0))
            return found

        def copies(self, origin, step):
            return [
                (to_depth(block, block, self.kind, step, sems), holds)
                for block, sems, holds in self.blocks(origin)
            ]

        def passed(self):
            target, step = (Z - 1) * (mz - 1), 2 * mz - 1
            return [
                (remote(block, block, sems, self.kind, 0, step, me, target), holds)
                for block, sems, holds in self.blocks(below(2))
            ]

        def each(self, found, condition, act):
            for copy, holds in found:

                @pl.when(condition & holds)
                def _():
                    act(copy)

        def start(self):
            for step in order:
                self.each(self.copies(mz, step), direct(step), lambda c: c.start())

        def arrival(self, step):
            self.each(self.copies(below(step), step), mz >= 0, lambda c: c.wait_recv())

        def relay(self):
            if relayed:
                self.arrival(2)
                self.each(self.passed(), between, lambda c: c.start())

        def rest(self):
            return tuple(step for step in order if not (relayed and step == 2))

        def finish(self):
            for step in order:
                self.each(self.copies(mz, step), direct(step), lambda c: c.wait_send())
            if relayed:
                self.each(self.passed(), between, lambda c: c.wait_send())

    def split_rows(position):
        return pl.ds(pl.multiple_of(sh.common + position * TILE, TILE), TILE)

    class Strips(Gather):
        def blocks(self, origin):
            return [(self.every.at[self.body, split_rows(origin)], z_sem, True)]

    def windows(kind, every):
        return Gather(kind, every, (tail,), (head,))

    def put_out(every, out, positions):
        for position in positions:
            store(every.at[position, tail], out.at[tail_of(position)])
            store(every.at[position, head], out.at[head], position == 0)

    def put_together(every, dest):
        dest[0:TILE] = every[0, 0:TILE]
        for position in range(Z):
            dest[TILE + S * position : TILE + S * (position + 1)] = every[position, TILE:W]

    def scatters(kind, part, recv, passing):
        return [
            Scatter(kind + c, part.at[c], recv.at[c], passing.at[c]) for c in range(NC)
        ]

    window = window_of(mz)
    own = (lax.broadcasted_iota(jnp.int32, (W, 1), 0) >= TILE) | (mz == 0)

    loaded(loads.ids_row, loads.images_live, loads.noise_row)
    live_rows = images_live[...].reshape(1, 1) * TOK_IMG
    lane = lax.broadcasted_iota(jnp.int32, (1, R), 1)
    live = (lane < live_rows).astype(F32)
    expert_of = lax.broadcasted_iota(jnp.int32, (E, R), 0)
    ids = ids_row[...]
    hot = [(expert_of == ids[k : k + 1]).astype(F32) * live for k in range(2)]
    earlier = (
        lax.broadcasted_iota(jnp.int32, (R, R), 0) < lax.broadcasted_iota(jnp.int32, (R, R), 1)
    ).astype(BF16)
    counts = [nn(h.astype(BF16), earlier) for h in hot]
    counts[1] = counts[1] + jnp.sum(hot[0], axis=1, keepdims=True)
    start = expert_of.astype(F32) * CP
    spot = [
        jnp.where(live > 0, jnp.sum(hot[k] * (counts[k] + start), axis=0, keepdims=True), -1.0)
        for k in range(2)
    ]
    blank = jnp.zeros((1, RP - R), F32)
    live, *hot = (
        jnp.concatenate([v, jnp.zeros((v.shape[0], RP - R), F32)], axis=1) for v in (live, *hot)
    )
    noise = jnp.concatenate([noise_row[...], jnp.zeros((2, RP - R), F32)], axis=1)
    spot_row = [jnp.concatenate([s, blank - 1.0], axis=1).astype(jnp.int32) for s in spot]
    eye_rows = lax.broadcasted_iota(jnp.int32, (RP, RP), 0) == lax.broadcasted_iota(
        jnp.int32, (RP, RP), 1
    )
    spot_col = [
        jnp.sum(jnp.where(eye_rows, s.astype(F32), 0.0), axis=1, keepdims=True).astype(jnp.int32)
        for s in spot_row
    ]

    def spread(e):
        slot = lax.broadcasted_iota(jnp.int32, (CP, RP), 0) + e * CP
        return slot == spot_row[0], slot == spot_row[1]

    eye_slots = lax.broadcasted_iota(jnp.int32, (CP, CL), 0) == lax.broadcasted_iota(
        jnp.int32, (CP, CL), 1
    )

    def as_row(column):
        return jnp.sum(jnp.where(eye_slots, column, 0.0), axis=0, keepdims=True)

    def as_column(row):
        return jnp.sum(jnp.where(eye_slots, row, 0.0), axis=1, keepdims=True)

    loaded(loads.wout)
    pl.semaphore_wait(barrier, E - 1 + Z - 1)
    half = D // 2
    columns = pl.ds(pl.multiple_of(core * half, 128), half)
    weights = Gather(sh.z_w, m.wfull, (slice(None), columns))
    weights.start()

    row_of = lax.broadcasted_iota(jnp.int32, (R, 1), 0)
    og, pt = m.og, m.pt
    og[pl.ds(RP - TILE, TILE)] = jnp.zeros((TILE, D), BF16)
    loaded(loads.out_grad)
    og[0:R] = jnp.where(row_of < live_rows, m.out_grad[...], jnp.zeros((), BF16))
    c_send, c_recv = m.c_send, m.c_recv

    def pack_cotangent(step, carry):
        e = plane(step)
        s0, s1 = spread(e)
        c_send[e] = nn((s0 | s1).astype(BF16), og[...]).astype(BF16)

        @pl.when(step > 0)
        def _():
            to_plane(c_send.at[e], c_recv.at[step], sh.e_c, step).start()

        return carry

    lax.fori_loop(0, E, pack_cotangent, 0)
    c_recv[0] = c_send[me]

    pt[pl.ds(RP - TILE, TILE)] = jnp.zeros((TILE, D), BF16)
    loaded(loads.patches, loads.gain1, loads.bias1, loads.gain2, loads.bias2, loads.router_t)
    pt[0:R] = m.patches[...]
    first_low, wqkv = m.first_low, m.wqkv
    g1, b1 = gain1[...].reshape(1, D), bias1[...].reshape(1, D)
    g2, b2 = gain2[...].reshape(1, D), bias2[...].reshape(1, D)
    normal, _ = normalize(pt[...].astype(F32))
    first_low[...] = (normal * g1 + b1).astype(BF16)
    loaded(loads.wqkv)
    projected = nt(first_low[...], wqkv[...]).astype(BF16)
    q_s, k_s, v_s, probs_s = m.q_s, m.k_s, m.v_s, m.probs_s
    for h in range(sh.heads):
        for part, dest in enumerate((q_s, k_s, v_s)):
            begin = part * sh.local + h * HEAD_DIM
            dest[h] = projected[:, begin : begin + HEAD_DIM]
    row2 = lax.broadcasted_iota(jnp.int32, (RP, RP), 0)
    col2 = lax.broadcasted_iota(jnp.int32, (RP, RP), 1)
    same = ((row2 >= TOK_IMG) == (col2 >= TOK_IMG)) & (col2 < R)
    scale = HEAD_DIM ** (-0.5)
    heads = []
    for h in range(sh.heads):
        scores = jnp.where(same, nt(q_s[h], k_s[h]) * scale, -1e30)
        exponent = jnp.exp(scores - jnp.max(scores, axis=1, keepdims=True))
        probs = exponent / jnp.sum(exponent, axis=1, keepdims=True)
        probs_s[h] = probs
        heads.append(nn(probs.astype(BF16), v_s[h]).astype(BF16))
    mixed, mixed_all = m.mixed, m.mixed_all
    mixed[...] = jnp.concatenate(heads, axis=1)
    HR, L = sh.half_rows, sh.local
    mixed_all[mz] = jnp.concatenate([mixed[0:HR], mixed[RP - HR : RP]], axis=1)
    mixing = Gather(sh.z_m, mixed_all)
    mixing.start()

    wfull = m.wfull

    def to_other(step):
        block = wfull.at[below(step), :, columns]
        return to_sibling(block, block, sh.s_w, step)

    weights.relay()
    if relayed:
        to_other(2).start()
    for step in weights.rest():
        weights.arrival(step)
        to_other(step).start()

    resid, second_low = m.resid, m.second_low

    def attend(position):
        block = mixed_all[position]
        weight = wfull[position]
        return nn(block[:, 0:L], weight), nn(block[2 * HR - RP :, L : 2 * L], weight)

    low, high = attend(mz)
    resid[0:HR] = pt[0:HR].astype(F32) + low
    resid[HR:RP] = pt[HR:RP].astype(F32) + high
    mixing.relay()
    for step in order:
        if not (relayed and step == 2):
            mixing.arrival(step)
        to_other(step).wait_recv()
        low, high = attend(below(step))
        resid[0:HR] += low
        resid[HR:RP] += high

    normal, _ = normalize(resid[...])
    second_low[...] = (normal * g2 + b2).astype(BF16)
    logits = nt(router_t[...], second_low[...])
    chosen = [
        jnp.sum(hot[k] * logits, axis=0, keepdims=True) + noise[k : k + 1, :] for k in range(2)
    ]
    top = jnp.maximum(chosen[0], chosen[1])
    powers = [jnp.exp(c - top) for c in chosen]
    gates = [p / (powers[0] + powers[1]) for p in powers]
    x_send, x_recv, g_send, g_recv = m.x_send, m.x_recv, m.g_send, m.g_recv

    def pack_rows(step, carry):
        e = plane(step)
        s0, s1 = spread(e)
        x_send[e] = nn((s0 | s1).astype(BF16), second_low[...]).astype(BF16)
        gate = jnp.sum(
            jnp.where(s0, gates[0], 0.0) + jnp.where(s1, gates[1], 0.0), axis=1, keepdims=True
        )
        g_send[e] = jnp.broadcast_to(as_row(gate), (8, CL))

        @pl.when(step > 0)
        def _():
            to_plane(g_send.at[e], g_recv.at[step], sh.e_g, step).start()
            if sh.split:
                strip_to(e, step).start()
            else:
                common_to(e, step).start()

        return carry

    common = pl.ds(0, sh.common)

    def common_to(sent, step):
        return to_plane(x_send.at[sent, common], x_recv.at[step, common], sh.e_x, step)

    def strip_to(sent, step):
        rows = split_rows(mz)
        return to_plane(x_send.at[sent, rows], x_recv.at[step, rows], sh.e_xs, step)

    lax.fori_loop(0, E, pack_rows, 0)
    if sh.split:

        def send_common(step, carry):
            common_to(plane(step), step).start()
            return carry

        lax.fori_loop(1, E, send_common, 0)
        x_recv[0, split_rows(mz)] = x_send[me, split_rows(mz)]
    g_recv[0] = g_send[me]
    x_recv[0, common] = x_send[me, common]
    place = m.place
    slot_lane = lax.broadcasted_iota(jnp.int32, (RP, E * CP), 1)
    place[...] = ((slot_lane == spot_col[0]) | (slot_lane == spot_col[1])).astype(BF16)

    loaded(loads.up, loads.down)
    up, down, act, slope = m.up, m.down, m.act, m.slope
    delta, hid, eo_send, eo_home = m.delta, m.hid, m.eo_send, m.eo_home
    gg_send, gg_home, ei_home = m.gg_send, m.gg_home, m.ei_home

    halves = ((0, E // 2), (E // 2, E))
    x_strips = [Strips(sh.z_x + at, x_recv, pl.ds(a, b - a)) for at, (a, b) in enumerate(halves)]
    if sh.split:

        def strip_arrived(step, carry):
            strip_to(0, step).wait_recv()
            return carry

        for strips_of, (a, b) in zip(x_strips, halves):
            lax.fori_loop(max(a, 1), b, strip_arrived, 0)
            strips_of.start()

    def forward(step, carry):

        @pl.when(step > 0)
        def _():
            to_plane(g_send.at[0], g_recv.at[step], sh.e_g, step).wait_recv()
            common_to(0, step).wait_recv()
            to_plane(c_send.at[0], c_recv.at[step], sh.e_c, step).wait_recv()

        hidden = nn(x_recv[step], up[...])
        below_it = 0.5 * (1.0 + lax.erf(hidden * (0.5**0.5)))
        bell = jnp.exp(-0.5 * hidden * hidden) * 0.3989422804014327
        act[step] = (hidden * below_it).astype(BF16)
        slope[step] = (below_it + hidden * bell).astype(BF16)
        result = nn(act[step], down[...])
        gate = as_column(g_recv[step][0:1])
        given = c_recv[step].astype(F32)
        dots = jnp.sum(given * result, axis=1, keepdims=True)
        gg_send[step] = jnp.broadcast_to(as_row(dots), (8, CL))
        eo_send[step] = (gate * result).astype(BF16)
        delta[step] = (gate * given).astype(BF16)

        @pl.when(step > 0)
        def _():
            back_to(gg_send.at[step], gg_home.at[me], sh.e_gg, step).start()
            back_to(eo_send.at[step], eo_home.at[me], sh.e_eo, step).start()

        return carry

    for strips_of, (a, b) in zip(x_strips, halves):
        if sh.split:
            strips_of.relay()
            for step in strips_of.rest():
                strips_of.arrival(step)
        lax.fori_loop(a, b, forward, 0)
    gg_home[me] = gg_send[0]
    eo_home[me] = eo_send[0]

    def cotangent_left(step, carry):
        to_plane(c_send.at[0], c_recv.at[0], sh.e_c, step).wait_send()
        return carry

    lax.fori_loop(1, E, cotangent_left, 0)
    ei_send = c_send

    def lanes(c):
        return pl.ds(c * CW, CW)

    for c in range(NC):

        def backward(step, carry):
            if c == 0:
                hid[step] = (nt(delta[step], down[...]) * slope[step]).astype(BF16)
            ei_send[step, :, lanes(c)] = nt(hid[step], up[lanes(c), :]).astype(BF16)

            @pl.when(step > 0)
            def _():
                back_to(
                    ei_send.at[step, :, lanes(c)], ei_home.at[me, :, lanes(c)], sh.e_ei + c, step
                ).start()

            return carry

        lax.fori_loop(0, E, backward, 0)
    ei_home[me] = ei_send[0]

    strip = 128
    F = up.shape[1]
    acc = m.acc

    def flat(ref, first, size):
        return ref[:, :, pl.ds(pl.multiple_of(first, 128), size)].reshape(E * CP, size)

    def strip_copy(i, out, slot):
        return pltpu.make_async_copy(
            acc.at[slot], out.at[pl.ds(pl.multiple_of(i * strip, strip), strip)], local_sem.at[slot]
        )

    def strips(out, lhs, rhs, count, slot):
        def one(i, carry):
            at = slot + lax.rem(i, 2)

            @pl.when(i >= 2)
            def _():
                strip_copy(i - 2, out, at).wait()

            acc[at] = tn(flat(lhs, i * strip, strip), flat(rhs, 0, rhs.shape[2])).astype(BF16)
            strip_copy(i, out, at).start()
            return carry

        lax.fori_loop(0, count, one, 0)

    strips(outputs.up_out, x_recv, hid, D // strip, 0)
    strips(outputs.down_out, act, delta, F // strip, 2)

    for step in range(1, E):
        to_plane(gg_send.at[0], gg_home.at[plane(step)], sh.e_gg, step).wait_recv()

    def pick_dots(e, totals):
        s0, s1 = spread(e)
        column = as_column(gg_home[e][0:1])
        return (
            totals[0] + jnp.sum(jnp.where(s0, column, 0.0), axis=0, keepdims=True),
            totals[1] + jnp.sum(jnp.where(s1, column, 0.0), axis=0, keepdims=True),
        )

    nothing = jnp.zeros((1, RP), F32)
    dots0, dots1 = lax.fori_loop(0, E, pick_dots, (nothing, nothing))
    gz_send, gz_recv = m.gz_send, m.gz_recv
    gz_send[...] = jnp.zeros((8, RP), F32)
    gz_send[0:1] = dots0
    gz_send[1:2] = dots1
    for step in range(1, Z):
        to_depth(gz_send, gz_recv.at[mz], sh.z_gz, step).start()
    mix_part, in_part = m.mix_part, m.in_part
    mix = Scatter(sh.z_mix, mix_part, m.mix_recv, m.mix_pass)
    for step in range(1, E):
        to_plane(eo_send.at[0], eo_home.at[plane(step)], sh.e_eo, step).wait_recv()
    mix_part[...] = nn(place[...], eo_home[...].reshape(E * CP, D)).astype(BF16)
    mix.start()
    mix.relay()
    gate_grad = gz_send[...]
    for step in range(1, Z):
        to_depth(gz_send, gz_recv.at[below(step)], sh.z_gz, step).wait_recv()
        gate_grad = gate_grad + gz_recv[below(step)]
    both = gates[0] * gate_grad[0:1] + gates[1] * gate_grad[1:2]
    logit_grad = sum(hot[k] * (gates[k] * (gate_grad[k : k + 1] - both)) for k in range(2))
    parts = in_three(logit_grad)
    router_grad = sum(nn(p, second_low[...]) for p in parts)
    rterm = m.rterm
    rterm[...] = sum(tn(p, router_t[...]) for p in parts)

    ins = scatters(sh.z_in, in_part, m.in_recv, m.in_pass)
    bo_all, pg_all = m.bo_all, m.pg_all
    bo_gather = windows(sh.z_bo, bo_all)
    for c in range(NC):
        for step in range(1, E):
            to_plane(
                ei_send.at[0, :, lanes(c)], ei_home.at[plane(step), :, lanes(c)], sh.e_ei + c, step
            ).wait_recv()
        home = ei_home[:, :, lanes(c)].reshape(E * CP, CW)
        in_part[c] = nn(place[...], home).astype(BF16)
        ins[c].start()
        if c == 0:
            mixture = mix.total()
            at = lax.broadcasted_iota(jnp.int32, (W, 1), 0) + mz * S
            bo_all[mz] = jnp.where(at < live_rows, resid[window] + mixture, 0.0).astype(BF16)
        ins[c].relay()

    cot = og[window].astype(F32)
    normal, spread_scale = normalize(resid[window])
    second_grad = jnp.concatenate([part.total() for part in ins], axis=1) + rterm[window]
    resid_grad = cot + norm_back(normal, spread_scale, second_grad * g2)
    resid_win = m.resid_win
    resid_win[...] = resid_grad
    attended_grad = jnp.where(own, resid_grad, 0.0).astype(BF16)
    mg_send, mg_recv = m.mg_send, m.mg_recv

    def to_heads(step, sent, received):
        yield to_depth(mg_send.at[sent, tail], mg_recv.at[received, tail], sh.z_mg, step), mz >= 0
        first = to_depth(
            mg_send.at[sent, head], mg_recv.at[received, head], sh.z_mg, step, z_extra
        )
        yield first, received == 0

    def each(found, act):
        for copy, condition in found:

            @pl.when(condition)
            def _():
                act(copy)

    for step in order:
        mg_send[above(step)] = nt(attended_grad, wfull[above(step)]).astype(BF16)
        each(to_heads(step, above(step), mz), lambda c: c.start())
    mg_recv[mz] = nt(attended_grad, wfull[mz]).astype(BF16)
    normal, _ = normalize(resid[...])
    share = jnp.concatenate([in_part[c].astype(F32) for c in range(NC)], axis=1)
    share = share + jnp.where(mz == 0, rterm[...], 0.0)
    m.sp_send[...] = jnp.zeros((sh.small, D), F32)
    m.sp_send[0:E] = jnp.where(mz == 0, router_grad, 0.0)
    m.sp_send[E : E + 1] = jnp.sum(share * normal, axis=0, keepdims=True)
    m.sp_send[E + 1 : E + 2] = jnp.sum(share, axis=0, keepdims=True)

    bo_gather.start()

    B, BP = sh.share, sh.share_rows
    qg = ChipSum(sh.s_qg, m.qg_send, m.qg_pair, m.qg_recv)
    wg = ChipSum(sh.s_og, m.wg_send, m.wg_pair, m.wg_recv)
    lower = mz < Z // 2
    at_rows = pl.ds(pl.multiple_of(lax.rem(mz, Z // 2) * S, TILE), W)
    mixed_win = jnp.concatenate(
        [
            jnp.where(
                lower, mixed_all[p, at_rows][:, 0:L], mixed_all[p, at_rows][:, L : 2 * L]
            )
            for p in range(Z)
        ],
        axis=1,
    )
    wout_grad = tn(attended_grad, mixed_win)
    for e in range(E):
        m.wg_send[e % 2, e // 2, 0:B] = wout_grad[e * B : (e + 1) * B].astype(BF16)
    wg.start()
    for step in order:
        each(to_heads(step, 0, below(step)), lambda c: c.wait_recv())
    wg.cross()
    mixed_grad = m.mixed_grad
    put_together(mg_recv, mixed_grad)

    grads = [[], [], []]
    for h in range(sh.heads):
        mg = mixed_grad[:, h * HEAD_DIM : (h + 1) * HEAD_DIM]
        probs = probs_s[h]
        prob_grad = nt(mg, v_s[h])
        score_grad = (
            probs * (prob_grad - jnp.sum(prob_grad * probs, axis=1, keepdims=True))
        ).astype(BF16)
        grads[0].append((nn(score_grad, k_s[h]) * scale).astype(BF16))
        grads[1].append((tn(score_grad, q_s[h]) * scale).astype(BF16))
        grads[2].append(tn(probs.astype(BF16), mg).astype(BF16))
    projected_grad = jnp.concatenate(grads[0] + grads[1] + grads[2], axis=1)
    mix.finish()
    first_part = mix_part
    first = Scatter(sh.z_first, first_part, m.first_recv, m.first_pass)
    first_part[...] = nn(projected_grad, wqkv[...]).astype(BF16)
    first.start()

    qkv_grad = tn(first_low[...], projected_grad)
    for e in range(E):
        m.qg_send[e % 2, e // 2, 0:B] = qkv_grad[e * B : (e + 1) * B].astype(BF16)
    qg.start()
    normal, _ = normalize(pt[...].astype(F32))
    share = first_part[...].astype(F32)
    m.sp_send[E + 2 : E + 3] = jnp.sum(share * normal, axis=0, keepdims=True)
    m.sp_send[E + 3 : E + 4] = jnp.sum(share, axis=0, keepdims=True)
    smalls = SmallSum(sh.s_sp, m.sp_send, m.sp_pair, m.sp_half, m.sp_recv)
    smalls.start()
    first.relay()
    smalls.cross()

    bo_gather.relay()
    for step in bo_gather.rest():
        bo_gather.arrival(step)
    put_out(bo_all, outputs.block_out, range(Z))

    wz_send, wz_recv = m.wz_send, m.wz_recv
    total_w = wg.total()
    for position in range(Z):
        wz_send[position] = total_w[:, position * L : (position + 1) * L].astype(BF16)
    for step in order:
        to_depth(wz_send.at[above(step)], wz_recv.at[mz], sh.z_wz, step).start()
    zs_send, zs_recv = m.zs_send, m.zs_recv
    near = pl.ds(pl.multiple_of(sh.near(me), 128), sh.near_lanes)
    m.sp_total[...] = smalls.total()
    zs_send[...] = m.sp_total[:, near]
    for step in order:
        to_depth(zs_send, zs_recv.at[mz], sh.z_zs, step).start()

    normal, spread_scale = normalize(pt[window].astype(F32))
    first_grad = first.total()
    patch_grad = resid_win[...] + norm_back(normal, spread_scale, first_grad * g1)
    pg_all[mz] = patch_grad.astype(BF16)
    pg_gather = windows(sh.z_pg, pg_all)
    pg_gather.start()
    qg.cross()
    pg_gather.relay()
    total = qg.total()
    qkv_sum, wout_sum, small_sum = m.qkv_sum, m.wout_sum, m.small_sum
    for part in range(3):
        qkv_sum[part] = total[0:B, part * L : (part + 1) * L]
    store(qkv_sum, outputs.qkv_out)
    total_w = wz_send[mz].astype(F32)
    for step in order:
        to_depth(wz_send.at[0], wz_recv.at[below(step)], sh.z_wz, step).wait_recv()
        total_w = total_w + wz_recv[below(step)].astype(F32)
    wout_sum[...] = total_w[0:B]
    store(wout_sum, outputs.wout_out)
    small_sum[...] = zs_send[...]
    for step in order:
        to_depth(zs_send, zs_recv.at[below(step)], sh.z_zs, step).wait_recv()
        small_sum[...] += zs_recv[below(step)]
    store(small_sum, outputs.small_out)

    for step in (0,) + order:
        position = below(step)
        if step and not (relayed and step == 2):
            pg_gather.arrival(step)
        put_out(pg_all, outputs.patches_grad, [position])

    for step in range(1, Z):
        to_other(step).wait_send()

    def left(step, carry):
        to_plane(g_send.at[0], g_recv.at[0], sh.e_g, step).wait_send()
        common_to(0, step).wait_send()
        if sh.split:
            strip_to(0, step).wait_send()
        back_to(gg_send.at[0], gg_home.at[0], sh.e_gg, step).wait_send()
        back_to(eo_send.at[0], eo_home.at[0], sh.e_eo, step).wait_send()
        for c in range(NC):
            back_to(
                ei_send.at[0, :, lanes(c)], ei_home.at[0, :, lanes(c)], sh.e_ei + c, step
            ).wait_send()
        return carry

    lax.fori_loop(1, E, left, 0)
    for sent in ins + [first, qg, wg, smalls]:
        sent.finish()
    if sh.split:
        for strips_of in x_strips:
            strips_of.finish()
    for gather in (weights, mixing, bo_gather, pg_gather):
        gather.finish()
    for step in range(1, Z):
        each(to_heads(step, 0, mz), lambda c: c.wait_send())
        to_depth(wz_send.at[0], wz_recv.at[0], sh.z_wz, step).wait_send()
        to_depth(gz_send, gz_recv.at[0], sh.z_gz, step).wait_send()
        to_depth(zs_send, zs_recv.at[0], sh.z_zs, step).wait_send()
    for last in (2, 1):
        strip_copy(D // strip - last, outputs.up_out, (D // strip - last) % 2).wait()
        strip_copy(F // strip - last, outputs.down_out, 2 + (F // strip - last) % 2).wait()
    for copy, condition in stores:
        if condition is None:
            copy.wait()
        else:

            @pl.when(condition)
            def _():
                copy.wait()


def scratch_of(sh, F, in_count):
    E, Z, RP, R, D, NC = sh.experts, sh.depth, sh.padded, sh.rows, sh.width, sh.chunks
    CP, CL, CW, W = sh.slots, sh.slot_lanes, sh.chunk, sh.window
    B, BP, C = sh.share, sh.share_rows, sh.chips
    L, H = sh.local, sh.heads
    blocks = ((E, CP, D), BF16)
    dots = ((E, 8, CL), F32)
    rows = ((RP, D), BF16)
    part = ((NC, RP, CW), BF16)
    recv = ((NC, Z, W, CW), BF16)
    passing = ((NC, W, CW), BF16)
    every = ((Z, W, D), BF16)
    head = ((H, RP, HEAD_DIM), BF16)
    shapes = dict(
        gain1=((D,), F32),
        bias1=((D,), F32),
        gain2=((D,), F32),
        bias2=((D,), F32),
        router_t=((E, D), BF16),
        ids_row=((2, R), jnp.int32),
        noise_row=((2, R), F32),
        images_live=((1,), jnp.int32),
        patches=((R, D), BF16),
        out_grad=((R, D), BF16),
        up=((D, F), BF16),
        down=((F, D), BF16),
        wqkv=((3 * L, D), BF16),
        wfull=((Z, L, D), BF16),
        pt=rows,
        og=rows,
        first_low=rows,
        q_s=head,
        k_s=head,
        v_s=head,
        probs_s=((H, RP, RP), F32),
        mixed=((RP, L), BF16),
        mixed_all=((Z, sh.half_rows, 2 * L), BF16),
        resid=((RP, D), F32),
        second_low=rows,
        place=((RP, E * CP), BF16),
        x_send=blocks,
        x_recv=blocks,
        c_send=blocks,
        c_recv=blocks,
        g_send=dots,
        g_recv=dots,
        act=((E, CP, F), BF16),
        slope=((E, CP, F), BF16),
        delta=blocks,
        hid=((E, CP, F), BF16),
        eo_send=blocks,
        eo_home=blocks,
        ei_home=blocks,
        gg_send=dots,
        gg_home=dots,
        acc=((4, 128, max(F, D)), BF16),
        mix_part=rows,
        mix_recv=every,
        mix_pass=((W, D), BF16),
        in_part=part,
        in_recv=recv,
        in_pass=passing,
        first_recv=every,
        first_pass=((W, D), BF16),
        rterm=((RP, D), F32),
        resid_win=((W, D), F32),
        bo_all=every,
        pg_all=every,
        mg_send=((Z, W, L), BF16),
        mg_recv=((Z, W, L), BF16),
        mixed_grad=((RP, L), BF16),
        wz_send=((Z, BP, L), BF16),
        wz_recv=((Z, BP, L), BF16),
        gz_send=((8, RP), F32),
        gz_recv=((Z, 8, RP), F32),
        qg_send=((2, C, BP, 3 * L), BF16),
        qg_pair=((C, BP, 3 * L), BF16),
        qg_recv=((C, BP, 3 * L), BF16),
        wg_send=((2, C, BP, Z * L), BF16),
        wg_pair=((C, BP, Z * L), BF16),
        wg_recv=((C, BP, Z * L), BF16),
        sp_send=((sh.small, D), F32),
        sp_pair=((sh.small, D), F32),
        sp_half=((sh.small, D), F32),
        sp_total=((sh.small, D), F32),
        sp_recv=((C, sh.small, D), F32),
        qkv_sum=((3, B, L), F32),
        wout_sum=((B, L), F32),
        zs_send=((sh.small, sh.near_lanes), F32),
        zs_recv=((Z, sh.small, sh.near_lanes), F32),
        small_sum=((sh.small, sh.near_lanes), F32),
    )
    sems = dict(
        local_sem=4,
        in_sem=in_count,
        out_sem=4 * Z + 3,
        e_sem=(sh.e_kinds, 2, E),
        z_sem=(sh.z_kinds, 2, Z),
        z_extra=(sh.z_kinds, 2, Z),
        s_sem=(sh.s_kinds, 2, Z),
        c_sem=(sh.s_kinds, 2, sh.chips),
    )
    scratch = {field: pltpu.VMEM(*shape) for field, shape in shapes.items()}
    for field, shape in sems.items():
        scratch[field] = pltpu.SemaphoreType.DMA(shape if isinstance(shape, tuple) else (shape,))
    return scratch


def outputs_kernel(sh, pieces, *refs):
    given, outs, held, made = refs[:7], refs[7:18], refs[18:25], refs[25:36]
    in_sem, out_sem = refs[36:]
    wout, small = held[5:]
    loads = [
        pltpu.make_async_copy(src, dst, in_sem.at[at])
        for at, (src, dst) in enumerate(zip(given[5:], (wout, small)))
    ]
    steps = []
    for src, through, ready, dst, number in zip(given, held, made, outs, pieces):
        rows = src.shape[0] // number
        for piece in range(number):
            at = pl.ds(piece * rows, rows)
            part = [ref if number == 1 else ref.at[at] for ref in (src, through, ready, dst)]
            load = pltpu.make_async_copy(part[0], part[1], in_sem.at[len(loads) + len(steps)])
            steps.append((load, part))
    for load in loads + [load for load, _ in steps]:
        load.start()
    for load in loads:
        load.wait()
    E, lanes = sh.experts, sh.near_lanes
    me = lax.axis_index("expert")
    begin = me * sh.share - sh.near(me)
    mine = pltpu.roll(small[...], lax.rem(lanes - begin, lanes), 1)[:, 0 : sh.share]
    made[5][...] = wout[...].T
    made[6][...] = mine[0:E]
    for at, gain in enumerate(made[7:]):
        gain[...] = mine[E + at]
    stores = []

    def store(src, dst):
        stores.append(pltpu.make_async_copy(src, dst, out_sem.at[len(stores)]))
        stores[-1].start()

    for src, dst in zip(made[5:], outs[5:]):
        store(src, dst)
    for load, (_, through, ready, dst) in steps:
        load.wait()
        if through.dtype == ready.dtype:
            store(through, dst)
        else:
            ready[...] = through[...].astype(ready.dtype)
            store(ready, dst)
    for copy in stores:
        copy.wait()


def on_device(
    mesh,
    patches,
    first_gain,
    first_bias,
    qkv_weight,
    out_weight,
    second_gain,
    second_bias,
    router_weight,
    up_weight,
    down_weight,
    expert_ids,
    router_noise,
    images_live,
    out_grad,
):
    row_count, model_width = patches.shape
    local_width = out_weight.shape[0]
    sh = Shapes(mesh, row_count, model_width, local_width)
    hidden_width = up_weight.shape[2]
    E, RP, D = sh.experts, sh.padded, sh.width
    anywhere = pl.BlockSpec(memory_space=pl.ANY)
    slots = E * sh.slots
    flops = 2 * (
        6 * slots * D * hidden_width
        + 3 * RP * D * 4 * local_width
        + 4 * slots * RP * D
        + 7 * sh.heads * RP * RP * HEAD_DIM
    )
    inputs = dict(
        gain1=first_gain,
        bias1=first_bias,
        gain2=second_gain,
        bias2=second_bias,
        router_t=router_weight.T,
        ids_row=expert_ids.T,
        noise_row=router_noise.T,
        images_live=images_live,
        wout=out_weight,
        out_grad=out_grad,
        patches=patches,
        wqkv=qkv_weight.transpose(1, 2, 0).reshape(3 * local_width, D),
        up=up_weight[0],
        down=down_weight[0],
    )
    outputs = dict(
        block_out=jax.ShapeDtypeStruct((RP, D), BF16),
        patches_grad=jax.ShapeDtypeStruct((RP, D), BF16),
        qkv_out=jax.ShapeDtypeStruct((3, sh.share, local_width), F32),
        wout_out=jax.ShapeDtypeStruct((sh.share, local_width), F32),
        small_out=jax.ShapeDtypeStruct((sh.small, sh.near_lanes), F32),
        up_out=jax.ShapeDtypeStruct((D, hidden_width), BF16),
        down_out=jax.ShapeDtypeStruct((hidden_width, D), BF16),
    )
    scratch = scratch_of(sh, hidden_width, len(inputs))
    fields = tuple(tuple(group) for group in (inputs, outputs, scratch))
    outs = pl.pallas_call(
        functools.partial(whole_kernel, sh, fields),
        out_shape=tuple(outputs.values()),
        in_specs=[anywhere] * len(inputs),
        out_specs=(anywhere,) * len(outputs),
        scratch_shapes=list(scratch.values()),
        compiler_params=pltpu.CompilerParams(
            collective_id=0, has_side_effects=True, vmem_limit_bytes=62 << 20
        ),
        cost_estimate=pl.CostEstimate(flops=flops, bytes_accessed=16 << 20, transcendentals=0),
        name="block",
    )(*inputs.values())
    block_out, patches_grad, qkv_grad, wout_grad, small, up_grad, down_grad = outs
    pieces = (1, 1, 1, 4, 4)
    wholes = (block_out[:row_count], patches_grad[:row_count], qkv_grad, up_grad, down_grad)
    inputs = wholes + (wout_grad, small)
    kinds = (BF16, F32, F32, F32, F32)
    results = tuple(jax.ShapeDtypeStruct(w.shape, kind) for w, kind in zip(wholes, kinds)) + (
        jax.ShapeDtypeStruct((local_width, sh.share), F32),
        jax.ShapeDtypeStruct((E, sh.share), F32),
    )
    results += (jax.ShapeDtypeStruct((sh.share,), F32),) * 4
    copies = sum(pieces)
    results = pl.pallas_call(
        functools.partial(outputs_kernel, sh, pieces),
        out_shape=results,
        in_specs=[anywhere] * len(inputs),
        out_specs=(anywhere,) * len(results),
        scratch_shapes=[pltpu.VMEM(w.shape, w.dtype) for w in inputs + results]
        + [pltpu.SemaphoreType.DMA((copies + 2,)), pltpu.SemaphoreType.DMA((copies + 6,))],
        compiler_params=pltpu.CompilerParams(vmem_limit_bytes=62 << 20),
        name="outputs",
    )(*inputs)
    block_out, patches_grad, qkv_grad, up_grad, down_grad, wout_grad, router_grad = results[:7]
    gain2_grad, bias2_grad, gain1_grad, bias1_grad = results[7:]
    return (
        block_out,
        patches_grad,
        gain1_grad,
        bias1_grad,
        qkv_grad.transpose(1, 0, 2),
        wout_grad,
        gain2_grad,
        bias2_grad,
        router_grad.T,
        up_grad[None],
        down_grad[None],
    )


def solution(mesh):
    placed = (
        P("expert", None),
        P(),
        P(),
        P(None, None, "tensor"),
        P("tensor", None),
        P(),
        P(),
        P(),
        P("expert", None, "tensor"),
        P("expert", "tensor", None),
        P("expert", None),
        P("expert", None),
        P("expert"),
        P("expert", None),
    )
    return jax.shard_map(
        functools.partial(on_device, mesh),
        mesh=mesh,
        in_specs=placed,
        out_specs=(
            P("expert", None),
            P("expert", None),
            P("expert"),
            P("expert"),
            P("expert", None, "tensor"),
            P("tensor", "expert"),
            P("expert"),
            P("expert"),
            P("expert", None),
            P("expert", None, "tensor"),
            P("expert", "tensor", None),
        ),
        check_vma=False,
    )
```

```python
import functools
from types import SimpleNamespace

import jax
import jax.numpy as jnp
from jax import lax
from jax.experimental import pallas as pl
from jax.experimental.pallas import tpu as pltpu
from jax.sharding import PartitionSpec as P

HEAD_DIM = 64
TOK_IMG = 197
TILE = 16
EPSILON = 1e-06
MESH = pl.DeviceIdType.MESH
F32 = jnp.float32
BF16 = jnp.bfloat16


def round_up(value, unit):
    return (value + unit - 1) // unit * unit


def nn(a, b):
    return lax.dot_general(a, b, (((1,), (0,)), ((), ())), preferred_element_type=F32)


def nt(a, b):
    return lax.dot_general(a, b, (((1,), (1,)), ((), ())), preferred_element_type=F32)


def tn(a, b):
    return lax.dot_general(a, b, (((0,), (0,)), ((), ())), preferred_element_type=F32)


def in_three(values):
    high = values.astype(BF16)
    rest = values - high.astype(F32)
    middle = rest.astype(BF16)
    return high, middle, (rest - middle.astype(F32)).astype(BF16)


def normalize(values):
    center = values - jnp.mean(values, axis=-1, keepdims=True)
    scale = lax.rsqrt(jnp.mean(center * center, axis=-1, keepdims=True) + EPSILON)
    return center * scale, scale


def norm_back(normal, scale, grad_normal):
    return scale * (
        grad_normal
        - jnp.mean(grad_normal, axis=-1, keepdims=True)
        - normal * jnp.mean(grad_normal * normal, axis=-1, keepdims=True)
    )


class Shapes:
    def __init__(self, mesh, row_count, model_width, local_width):
        self.experts = mesh.shape["expert"]
        self.depth = mesh.shape["tensor"]
        self.rows = row_count
        self.width = model_width
        self.local = local_width
        self.heads = local_width // HEAD_DIM
        self.padded = round_up(row_count, TILE)
        self.capacity = (3 * row_count + self.experts - 1) // self.experts
        self.slots = round_up(self.capacity, TILE)
        self.split = self.depth * TILE if self.slots >= 2 * self.depth * TILE else 0
        self.common = self.slots - self.split
        self.slot_lanes = round_up(self.slots, 128)
        self.step = (self.padded - TILE) // self.depth
        self.window = self.step + TILE
        self.share = model_width // self.experts
        self.share_rows = round_up(self.share, TILE)
        self.small = round_up(self.experts + 4, 8)
        self.near_lanes = min(256, model_width)
        self.half_rows = round_up(self.padded // 2, TILE)
        self.chunk = 256
        self.chunks = model_width // self.chunk
        (
            self.e_c,
            self.e_g,
            self.e_x,
            self.e_xs,
            self.e_gg,
            self.e_eo,
            self.e_ei,
        ) = range(7)
        self.e_single = self.e_gg
        self.e_kinds = self.e_ei + self.chunks
        self.chips = self.experts // 2
        self.s_w, self.s_qg, self.s_og, self.s_sp = range(4)
        self.s_kinds = 4
        (
            self.z_w,
            self.z_m,
            self.z_gz,
            self.z_wz,
            self.z_zs,
            self.z_x,
            self.z_y,
            self.z_bo,
            self.z_mg,
            self.z_pg,
            self.z_mix,
            self.z_first,
            self.z_in,
        ) = range(13)
        self.z_heads = self.z_bo
        self.z_kinds = self.z_in + self.chunks


    def near(self, expert):
        return jnp.minimum(expert * self.share // 128 * 128, self.width - self.near_lanes)


def whole_kernel(sh, fields, *refs):
    E, Z, NC = sh.experts, sh.depth, sh.chunks
    R, RP, D = sh.rows, sh.padded, sh.width
    CP, CL, CW = sh.slots, sh.slot_lanes, sh.chunk
    taken = iter(refs)
    inputs, outputs, m = (SimpleNamespace(**{f: next(taken) for f in group}) for group in fields)
    e_sem, z_sem, z_extra, s_sem, c_sem = m.e_sem, m.z_sem, m.z_extra, m.s_sem, m.c_sem
    local_sem, in_sem, out_sem = m.local_sem, m.in_sem, m.out_sem
    me = lax.axis_index("expert")
    mz = lax.axis_index("tensor")

    def plane(step):
        return lax.rem(me + step, E)

    def before(step):
        return lax.rem(me - step + E, E)

    def above(step):
        return lax.rem(mz + step, Z)

    def below(step):
        return lax.rem(mz - step + Z, Z)

    def remote(src, dst, sems, kind, sent, received, expert, position):
        if sems is e_sem:
            single = sh.e_single
            place_of = kind * E + received if kind < single else single * E + kind - single
            send_sem, recv_sem = m.e_out.at[kind], e_sem.at[place_of]
        else:
            row = kind - sh.z_heads if sems is z_extra else kind
            send_sem, recv_sem = sems.at[row, 0, sent], sems.at[row, 1, received]
        return pltpu.make_async_remote_copy(
            src_ref=src,
            dst_ref=dst,
            send_sem=send_sem,
            recv_sem=recv_sem,
            device_id=(expert, position),
            device_id_type=MESH,
        )

    def to_plane(src, dst, kind, step):
        return remote(src, dst, e_sem, kind, step, step, plane(step), mz)

    core = lax.rem(me, 2)
    chip = me // 2
    sibling = me + 1 - 2 * core

    def to_sibling(src, dst, kind, step=0):
        return remote(src, dst, s_sem, kind, step, step, sibling, mz)

    def to_chip(src, dst, kind, step):
        target = lax.rem(chip + step, sh.chips)
        return remote(src, dst, c_sem, kind, step, step, 2 * target + core, mz)

    def chip_after(step):
        return lax.rem(chip + step, sh.chips)

    def chip_before(step):
        return lax.rem(chip - step + sh.chips, sh.chips)

    class ChipSum:
        def __init__(self, kind, send, pair, recv):
            self.kind, self.send, self.pair, self.recv = kind, send, pair, recv

        def halves(self):
            return to_sibling(self.send.at[1 - core], self.pair, self.kind)

        def start(self):
            self.halves().start()

        def cross(self):
            self.halves().wait_recv()
            half = self.send[core].astype(F32) + self.pair[...].astype(F32)
            self.send[core] = half.astype(self.send.dtype)
            for step in range(1, sh.chips):
                self.block(step, chip_after(step)).start()

        def block(self, step, target):
            return to_chip(self.send.at[core, target], self.recv.at[chip], self.kind, step)

        def total(self):
            value = self.send[core, chip].astype(F32)
            for step in range(1, sh.chips):
                source = chip_before(step)
                to_chip(
                    self.send.at[core, 0], self.recv.at[source], self.kind, step
                ).wait_recv()
                value = value + self.recv[source].astype(F32)
            return value

        def finish(self):
            self.halves().wait_send()
            for step in range(1, sh.chips):
                self.block(step, 0).wait_send()

    class SmallSum:
        def __init__(self, kind, send, pair, half, recv):
            self.kind, self.send, self.pair, self.half, self.recv = kind, send, pair, half, recv

        def exchange(self):
            return to_sibling(self.send, self.pair, self.kind)

        def start(self):
            self.exchange().start()

        def cross(self):
            self.exchange().wait_recv()
            self.half[...] = self.send[...] + self.pair[...]
            for step in range(1, sh.chips):
                to_chip(self.half, self.recv.at[chip], self.kind, step).start()

        def total(self):
            value = self.half[...]
            for step in range(1, sh.chips):
                source = chip_before(step)
                to_chip(self.half, self.recv.at[source], self.kind, step).wait_recv()
                value = value + self.recv[source]
            return value

        def finish(self):
            self.exchange().wait_send()
            for step in range(1, sh.chips):
                to_chip(self.half, self.recv.at[chip], self.kind, step).wait_send()

    def back_to(src, dst, kind, step):
        return remote(src, dst, e_sem, kind, step, step, before(step), mz)

    def to_depth(src, dst, kind, step, sems=None):
        sems = z_sem if sems is None else sems
        return remote(src, dst, sems, kind, step, step, me, above(step))

    relayed = Z == 4
    between = (mz > 0) & (mz < Z - 1)

    def direct(step, hold=False):
        if not relayed:
            return mz >= 0
        if step == 1:
            return mz < Z - 1
        if step == Z - 1:
            return mz > 0
        return jnp.logical_not(between) if hold else mz >= 0

    def arrives(step):
        if not relayed:
            return mz >= 0
        if step == 1:
            return mz > 0
        if step == Z - 1:
            return mz < Z - 1
        return mz >= 0

    order = (2, 1, 3) if relayed else tuple(range(1, Z))

    m.wout = m.wfull.at[mz]
    loads = SimpleNamespace()
    for at, (field, source) in enumerate(vars(inputs).items()):
        copy = pltpu.make_async_copy(source, getattr(m, field), in_sem.at[at])
        copy.start()
        setattr(loads, field, copy)

    def loaded(*copies):
        for copy in copies:
            copy.wait()

    stores = []

    def store(src, dst, condition=None):
        copy = pltpu.make_async_copy(src, dst, out_sem.at[len(stores)])
        stores.append((copy, condition))
        if condition is None:
            copy.start()
        else:

            @pl.when(condition)
            def _():
                copy.start()

    gain1, bias1, gain2, bias2 = m.gain1, m.bias1, m.gain2, m.bias2
    router_t, ids_row, noise_row, images_live = m.router_t, m.ids_row, m.noise_row, m.images_live
    barrier = pltpu.get_barrier_semaphore()
    for step in range(1, E):
        pl.semaphore_signal(barrier, inc=1, device_id=(plane(step), mz), device_id_type=MESH)
    for step in range(1, Z):
        pl.semaphore_signal(barrier, inc=1, device_id=(me, above(step)), device_id_type=MESH)

    S, W = sh.step, sh.window

    def tail_of(position):
        if isinstance(position, int):
            return pl.ds(position * S + TILE, S)
        return pl.ds(pl.multiple_of(position * S + TILE, TILE), S)

    def window_of(position):
        return pl.ds(pl.multiple_of(position * S, TILE), W)

    head, tail = pl.ds(0, TILE), pl.ds(TILE, S)

    class Scatter:
        def __init__(self, kind, part, recv, passing):
            self.kind, self.part, self.recv, self.passing = kind, part, recv, passing

        def send_to(self, step):
            target = above(step)
            return (
                to_depth(self.part.at[tail_of(target)], self.recv.at[mz, tail], self.kind, step),
                to_depth(self.part.at[head], self.recv.at[mz, head], self.kind, step, z_extra),
                target == 0,
            )

        def pass_to(self):
            source = self.passing
            return (
                to_depth(source.at[tail], self.recv.at[mz, tail], self.kind, 2),
                to_depth(source.at[head], self.recv.at[mz, head], self.kind, 2, z_extra),
                above(2) == 0,
            )

        def far(self):
            kind = self.kind
            up_to, down_to = (
                remote(
                    self.part.at[tail_of(Z - 1 - end)],
                    self.passing.at[tail],
                    z_sem,
                    kind,
                    0,
                    0,
                    me,
                    1 if end == 0 else Z - 2,
                )
                for end in (0, Z - 1)
            )
            down_head = remote(
                self.part.at[head],
                self.passing.at[head],
                z_extra,
                kind,
                0,
                0,
                me,
                Z - 2,
            )
            return up_to, down_to, down_head

        def start(self):
            if relayed:
                up_to, down_to, down_head = self.far()

                @pl.when(mz == 0)
                def _():
                    up_to.start()

                @pl.when(mz == Z - 1)
                def _():
                    down_to.start()
                    down_head.start()

            for step in order:
                body, first, is_head = self.send_to(step)

                @pl.when(direct(step, hold=True))
                def _():
                    body.start()

                @pl.when(direct(step, hold=True) & is_head)
                def _():
                    first.start()

        def relay(self):
            if not relayed:
                return

            @pl.when(between)
            def _():
                up_to, down_to, down_head = self.far()
                up_to.wait_recv()

                @pl.when(mz == Z - 2)
                def _():
                    down_head.wait_recv()

                target = above(2)
                self.passing[...] = (
                    self.passing[...].astype(F32) + self.part[window_of(target)].astype(F32)
                ).astype(BF16)
                body, first, is_head = self.pass_to()
                body.start()

                @pl.when(is_head)
                def _():
                    first.start()

        def total(self):
            value = self.part[window_of(mz)].astype(F32)
            for step in order:
                source = below(step)
                here = arrives(step)
                body = to_depth(
                    self.part.at[tail_of(0)], self.recv.at[source, tail], self.kind, step
                )
                first = to_depth(
                    self.part.at[head], self.recv.at[source, head], self.kind, step, z_extra
                )

                @pl.when(here)
                def _():
                    body.wait_recv()

                @pl.when(here & (mz == 0))
                def _():
                    first.wait_recv()

                value = value + jnp.where(here, self.recv[source].astype(F32), 0.0)
            return value

        def finish(self):
            if relayed:
                up_to, down_to, down_head = self.far()

                @pl.when(mz == 0)
                def _():
                    up_to.wait_send()

                @pl.when(mz == Z - 1)
                def _():
                    down_to.wait_send()
                    down_head.wait_send()

            for step in order:
                body, first, is_head = self.send_to(step)

                @pl.when(direct(step))
                def _():
                    body.wait_send()

                @pl.when(direct(step) & is_head)
                def _():
                    first.wait_send()

    class Gather:
        def __init__(self, kind, every, body=(), first=None):
            self.kind, self.every, self.body, self.first = kind, every, body, first

        def blocks(self, origin):
            found = [(self.every.at[(origin,) + self.body], z_sem, True)]
            if self.first is not None:
                found.append((self.every.at[(origin,) + self.first], z_extra, origin == 0))
            return found

        def copies(self, origin, step):
            return [
                (to_depth(block, block, self.kind, step, sems), holds)
                for block, sems, holds in self.blocks(origin)
            ]

        def passed(self):
            target, step = (Z - 1) * (mz - 1), 2 * mz - 1
            return [
                (remote(block, block, sems, self.kind, 0, step, me, target), holds)
                for block, sems, holds in self.blocks(below(2))
            ]

        def each(self, found, condition, act):
            for copy, holds in found:

                @pl.when(condition & holds)
                def _():
                    act(copy)

        def start(self):
            for step in order:
                self.each(self.copies(mz, step), direct(step), lambda c: c.start())

        def arrival(self, step):
            self.each(self.copies(below(step), step), mz >= 0, lambda c: c.wait_recv())

        def relay(self):
            if relayed:
                self.arrival(2)
                self.each(self.passed(), between, lambda c: c.start())

        def rest(self):
            return tuple(step for step in order if not (relayed and step == 2))

        def finish(self):
            for step in order:
                self.each(self.copies(mz, step), direct(step), lambda c: c.wait_send())
            if relayed:
                self.each(self.passed(), between, lambda c: c.wait_send())

    def split_rows(position):
        return pl.ds(pl.multiple_of(sh.common + position * TILE, TILE), TILE)

    class Strips(Gather):
        def blocks(self, origin):
            return [(self.every.at[self.body, split_rows(origin)], z_sem, True)]

    def windows(kind, every):
        return Gather(kind, every, (tail,), (head,))

    def put_out(every, out, positions):
        for position in positions:
            store(every.at[position, tail], out.at[tail_of(position)])
            store(every.at[position, head], out.at[head], position == 0)

    def put_together(every, dest):
        dest[0:TILE] = every[0, 0:TILE]
        for position in range(Z):
            dest[TILE + S * position : TILE + S * (position + 1)] = every[position, TILE:W]

    def scatters(kind, part, recv, passing):
        return [
            Scatter(kind + c, part.at[c], recv.at[c], passing.at[c]) for c in range(NC)
        ]

    window = window_of(mz)
    own = (lax.broadcasted_iota(jnp.int32, (W, 1), 0) >= TILE) | (mz == 0)

    loaded(loads.ids_row, loads.images_live, loads.noise_row)
    live_rows = images_live[...].reshape(1, 1) * TOK_IMG
    lane = lax.broadcasted_iota(jnp.int32, (1, R), 1)
    live = (lane < live_rows).astype(F32)
    expert_of = lax.broadcasted_iota(jnp.int32, (E, R), 0)
    ids = ids_row[...]
    hot = [(expert_of == ids[k : k + 1]).astype(F32) * live for k in range(2)]
    earlier = (
        lax.broadcasted_iota(jnp.int32, (R, R), 0) < lax.broadcasted_iota(jnp.int32, (R, R), 1)
    ).astype(BF16)
    counts = [nn(h.astype(BF16), earlier) for h in hot]
    counts[1] = counts[1] + jnp.sum(hot[0], axis=1, keepdims=True)
    start = expert_of.astype(F32) * CP
    spot = [
        jnp.where(live > 0, jnp.sum(hot[k] * (counts[k] + start), axis=0, keepdims=True), -1.0)
        for k in range(2)
    ]
    blank = jnp.zeros((1, RP - R), F32)
    live, *hot = (
        jnp.concatenate([v, jnp.zeros((v.shape[0], RP - R), F32)], axis=1) for v in (live, *hot)
    )
    noise = jnp.concatenate([noise_row[...], jnp.zeros((2, RP - R), F32)], axis=1)
    spot_row = [jnp.concatenate([s, blank - 1.0], axis=1).astype(jnp.int32) for s in spot]
    eye_rows = lax.broadcasted_iota(jnp.int32, (RP, RP), 0) == lax.broadcasted_iota(
        jnp.int32, (RP, RP), 1
    )
    spot_col = [
        jnp.sum(jnp.where(eye_rows, s.astype(F32), 0.0), axis=1, keepdims=True).astype(jnp.int32)
        for s in spot_row
    ]

    def spread(e):
        slot = lax.broadcasted_iota(jnp.int32, (CP, RP), 0) + e * CP
        return slot == spot_row[0], slot == spot_row[1]

    eye_slots = lax.broadcasted_iota(jnp.int32, (CP, CL), 0) == lax.broadcasted_iota(
        jnp.int32, (CP, CL), 1
    )

    def as_row(column):
        return jnp.sum(jnp.where(eye_slots, column, 0.0), axis=0, keepdims=True)

    def as_column(row):
        return jnp.sum(jnp.where(eye_slots, row, 0.0), axis=1, keepdims=True)

    loaded(loads.wout)
    pl.semaphore_wait(barrier, E - 1 + Z - 1)
    half = D // 2
    columns = pl.ds(pl.multiple_of(core * half, 128), half)
    weights = Gather(sh.z_w, m.wfull, (slice(None), columns))
    weights.start()

    row_of = lax.broadcasted_iota(jnp.int32, (R, 1), 0)
    og, pt = m.og, m.pt
    og[pl.ds(RP - TILE, TILE)] = jnp.zeros((TILE, D), BF16)
    loaded(loads.out_grad)
    og[0:R] = jnp.where(row_of < live_rows, m.out_grad[...], jnp.zeros((), BF16))
    c_send, c_recv = m.c_send, m.c_recv

    def pack_cotangent(step, carry):
        e = plane(step)
        s0, s1 = spread(e)
        c_send[e] = nn((s0 | s1).astype(BF16), og[...]).astype(BF16)

        @pl.when(step > 0)
        def _():
            to_plane(c_send.at[e], c_recv.at[step], sh.e_c, step).start()

        return carry

    lax.fori_loop(0, E, pack_cotangent, 0)
    c_recv[0] = c_send[me]

    pt[pl.ds(RP - TILE, TILE)] = jnp.zeros((TILE, D), BF16)
    loaded(loads.patches, loads.gain1, loads.bias1, loads.gain2, loads.bias2, loads.router_t)
    pt[0:R] = m.patches[...]
    first_low, wqkv = m.first_low, m.wqkv
    g1, b1 = gain1[...].reshape(1, D), bias1[...].reshape(1, D)
    g2, b2 = gain2[...].reshape(1, D), bias2[...].reshape(1, D)
    normal, _ = normalize(pt[...].astype(F32))
    first_low[...] = (normal * g1 + b1).astype(BF16)
    loaded(loads.wqkv)
    projected = nt(first_low[...], wqkv[...]).astype(BF16)
    q_s, k_s, v_s, probs_s = m.q_s, m.k_s, m.v_s, m.probs_s
    for h in range(sh.heads):
        for part, dest in enumerate((q_s, k_s, v_s)):
            begin = part * sh.local + h * HEAD_DIM
            dest[h] = projected[:, begin : begin + HEAD_DIM]
    row2 = lax.broadcasted_iota(jnp.int32, (RP, RP), 0)
    col2 = lax.broadcasted_iota(jnp.int32, (RP, RP), 1)
    same = ((row2 >= TOK_IMG) == (col2 >= TOK_IMG)) & (col2 < R)
    scale = HEAD_DIM ** (-0.5)
    heads = []
    for h in range(sh.heads):
        scores = jnp.where(same, nt(q_s[h], k_s[h]) * scale, -1e30)
        exponent = jnp.exp(scores - jnp.max(scores, axis=1, keepdims=True))
        probs = exponent / jnp.sum(exponent, axis=1, keepdims=True)
        probs_s[h] = probs
        heads.append(nn(probs.astype(BF16), v_s[h]).astype(BF16))
    mixed, mixed_all = m.mixed, m.mixed_all
    mixed[...] = jnp.concatenate(heads, axis=1)
    HR, L = sh.half_rows, sh.local
    mixed_all[mz] = jnp.concatenate([mixed[0:HR], mixed[RP - HR : RP]], axis=1)
    mixing = Gather(sh.z_m, mixed_all)
    mixing.start()

    wfull = m.wfull

    def to_other(step):
        block = wfull.at[below(step), :, columns]
        return to_sibling(block, block, sh.s_w, step)

    weights.relay()
    if relayed:
        to_other(2).start()
    for step in weights.rest():
        weights.arrival(step)
        to_other(step).start()

    resid, second_low = m.resid, m.second_low

    def attend(position):
        block = mixed_all[position]
        weight = wfull[position]
        return nn(block[:, 0:L], weight), nn(block[2 * HR - RP :, L : 2 * L], weight)

    low, high = attend(mz)
    resid[0:HR] = pt[0:HR].astype(F32) + low
    resid[HR:RP] = pt[HR:RP].astype(F32) + high
    mixing.relay()
    for step in order:
        if not (relayed and step == 2):
            mixing.arrival(step)
        to_other(step).wait_recv()
        low, high = attend(below(step))
        resid[0:HR] += low
        resid[HR:RP] += high

    normal, _ = normalize(resid[...])
    second_low[...] = (normal * g2 + b2).astype(BF16)
    logits = nt(router_t[...], second_low[...])
    chosen = [
        jnp.sum(hot[k] * logits, axis=0, keepdims=True) + noise[k : k + 1, :] for k in range(2)
    ]
    top = jnp.maximum(chosen[0], chosen[1])
    powers = [jnp.exp(c - top) for c in chosen]
    gates = [p / (powers[0] + powers[1]) for p in powers]
    x_send, x_recv, g_send, g_recv = m.x_send, m.x_recv, m.g_send, m.g_recv

    def pack_rows(step, carry):
        e = plane(step)
        s0, s1 = spread(e)
        x_send[e] = nn((s0 | s1).astype(BF16), second_low[...]).astype(BF16)
        gate = jnp.sum(
            jnp.where(s0, gates[0], 0.0) + jnp.where(s1, gates[1], 0.0), axis=1, keepdims=True
        )
        g_send[e] = jnp.broadcast_to(as_row(gate), (8, CL))

        @pl.when(step > 0)
        def _():
            to_plane(g_send.at[e], g_recv.at[step], sh.e_g, step).start()
            if sh.split:
                strip_to(e, step).start()
            else:
                common_to(e, step).start()

        return carry

    common = pl.ds(0, sh.common)

    def common_to(sent, step):
        return to_plane(x_send.at[sent, common], x_recv.at[step, common], sh.e_x, step)

    def strip_to(sent, step):
        rows = split_rows(mz)
        return to_plane(x_send.at[sent, rows], x_recv.at[step, rows], sh.e_xs, step)

    lax.fori_loop(0, E, pack_rows, 0)
    if sh.split:

        def send_common(step, carry):
            common_to(plane(step), step).start()
            return carry

        lax.fori_loop(1, E, send_common, 0)
        x_recv[0, split_rows(mz)] = x_send[me, split_rows(mz)]
    g_recv[0] = g_send[me]
    x_recv[0, common] = x_send[me, common]
    place = m.place
    slot_lane = lax.broadcasted_iota(jnp.int32, (RP, E * CP), 1)
    place[...] = ((slot_lane == spot_col[0]) | (slot_lane == spot_col[1])).astype(BF16)

    loaded(loads.up, loads.down)
    up, down, act, slope = m.up, m.down, m.act, m.slope
    delta, hid, eo_send, eo_home = m.delta, m.hid, m.eo_send, m.eo_home
    gg_send, gg_home, ei_home = m.gg_send, m.gg_home, m.ei_home

    halves = ((0, E // 2), (E // 2, E))
    x_strips = [Strips(sh.z_x + at, x_recv, pl.ds(a, b - a)) for at, (a, b) in enumerate(halves)]
    if sh.split:

        def strip_arrived(step, carry):
            strip_to(0, step).wait_recv()
            return carry

        for strips_of, (a, b) in zip(x_strips, halves):
            lax.fori_loop(max(a, 1), b, strip_arrived, 0)
            strips_of.start()

    def forward(step, carry):

        @pl.when(step > 0)
        def _():
            to_plane(g_send.at[0], g_recv.at[step], sh.e_g, step).wait_recv()
            common_to(0, step).wait_recv()
            to_plane(c_send.at[0], c_recv.at[step], sh.e_c, step).wait_recv()

        hidden = nn(x_recv[step], up[...])
        below_it = 0.5 * (1.0 + lax.erf(hidden * (0.5**0.5)))
        bell = jnp.exp(-0.5 * hidden * hidden) * 0.3989422804014327
        act[step] = (hidden * below_it).astype(BF16)
        slope[step] = (below_it + hidden * bell).astype(BF16)
        result = nn(act[step], down[...])
        gate = as_column(g_recv[step][0:1])
        given = c_recv[step].astype(F32)
        dots = jnp.sum(given * result, axis=1, keepdims=True)
        gg_send[step] = jnp.broadcast_to(as_row(dots), (8, CL))
        eo_send[step] = (gate * result).astype(BF16)
        delta[step] = (gate * given).astype(BF16)

        @pl.when(step > 0)
        def _():
            back_to(gg_send.at[step], gg_home.at[me], sh.e_gg, step).start()
            back_to(eo_send.at[step], eo_home.at[me], sh.e_eo, step).start()

        return carry

    for strips_of, (a, b) in zip(x_strips, halves):
        if sh.split:
            strips_of.relay()
            for step in strips_of.rest():
                strips_of.arrival(step)
        lax.fori_loop(a, b, forward, 0)
    gg_home[me] = gg_send[0]
    eo_home[me] = eo_send[0]

    others = pl.ds(0, E - 1)
    to_plane(c_send.at[others], c_recv.at[others], sh.e_c, 1).wait_send()
    ei_send = c_send

    def lanes(c):
        return pl.ds(c * CW, CW)

    for c in range(NC):

        def backward(step, carry):
            if c == 0:
                hid[step] = (nt(delta[step], down[...]) * slope[step]).astype(BF16)
            ei_send[step, :, lanes(c)] = nt(hid[step], up[lanes(c), :]).astype(BF16)

            @pl.when(step > 0)
            def _():
                back_to(
                    ei_send.at[step, :, lanes(c)], ei_home.at[me, :, lanes(c)], sh.e_ei + c, step
                ).start()

            return carry

        lax.fori_loop(0, E, backward, 0)
    ei_home[me] = ei_send[0]

    strip = 128
    F = up.shape[1]
    acc = m.acc

    def flat(ref, first, size):
        return ref[:, :, pl.ds(pl.multiple_of(first, 128), size)].reshape(E * CP, size)

    def strip_copy(i, out, slot):
        return pltpu.make_async_copy(
            acc.at[slot], out.at[pl.ds(pl.multiple_of(i * strip, strip), strip)], local_sem.at[slot]
        )

    def strips(out, lhs, rhs, count, slot):
        def one(i, carry):
            at = slot + lax.rem(i, 2)

            @pl.when(i >= 2)
            def _():
                strip_copy(i - 2, out, at).wait()

            acc[at] = tn(flat(lhs, i * strip, strip), flat(rhs, 0, rhs.shape[2])).astype(BF16)
            strip_copy(i, out, at).start()
            return carry

        lax.fori_loop(0, count, one, 0)

    strips(outputs.up_out, x_recv, hid, D // strip, 0)
    strips(outputs.down_out, act, delta, F // strip, 2)

    to_plane(gg_send.at[others], gg_home.at[others], sh.e_gg, 1).wait_recv()

    def pick_dots(e, totals):
        s0, s1 = spread(e)
        column = as_column(gg_home[e][0:1])
        return (
            totals[0] + jnp.sum(jnp.where(s0, column, 0.0), axis=0, keepdims=True),
            totals[1] + jnp.sum(jnp.where(s1, column, 0.0), axis=0, keepdims=True),
        )

    nothing = jnp.zeros((1, RP), F32)
    dots0, dots1 = lax.fori_loop(0, E, pick_dots, (nothing, nothing))
    gz_send, gz_recv = m.gz_send, m.gz_recv
    gz_send[...] = jnp.zeros((8, RP), F32)
    gz_send[0:1] = dots0
    gz_send[1:2] = dots1
    for step in range(1, Z):
        to_depth(gz_send, gz_recv.at[mz], sh.z_gz, step).start()
    mix_part, in_part = m.mix_part, m.in_part
    mix = Scatter(sh.z_mix, mix_part, m.mix_recv, m.mix_pass)
    to_plane(eo_send.at[others], eo_home.at[others], sh.e_eo, 1).wait_recv()
    mix_part[...] = nn(place[...], eo_home[...].reshape(E * CP, D)).astype(BF16)
    mix.start()
    mix.relay()
    gate_grad = gz_send[...]
    for step in range(1, Z):
        to_depth(gz_send, gz_recv.at[below(step)], sh.z_gz, step).wait_recv()
        gate_grad = gate_grad + gz_recv[below(step)]
    both = gates[0] * gate_grad[0:1] + gates[1] * gate_grad[1:2]
    logit_grad = sum(hot[k] * (gates[k] * (gate_grad[k : k + 1] - both)) for k in range(2))
    parts = in_three(logit_grad)
    router_grad = sum(nn(p, second_low[...]) for p in parts)
    rterm = m.rterm
    rterm[...] = sum(tn(p, router_t[...]) for p in parts)

    ins = scatters(sh.z_in, in_part, m.in_recv, m.in_pass)
    bo_all, pg_all = m.bo_all, m.pg_all
    bo_gather = windows(sh.z_bo, bo_all)
    for c in range(NC):
        to_plane(
            ei_send.at[others, :, lanes(c)], ei_home.at[others, :, lanes(c)], sh.e_ei + c, 1
        ).wait_recv()
        home = ei_home[:, :, lanes(c)].reshape(E * CP, CW)
        in_part[c] = nn(place[...], home).astype(BF16)
        ins[c].start()
        if c == 0:
            mixture = mix.total()
            at = lax.broadcasted_iota(jnp.int32, (W, 1), 0) + mz * S
            bo_all[mz] = jnp.where(at < live_rows, resid[window] + mixture, 0.0).astype(BF16)
        ins[c].relay()

    cot = og[window].astype(F32)
    normal, spread_scale = normalize(resid[window])
    second_grad = jnp.concatenate([part.total() for part in ins], axis=1) + rterm[window]
    resid_grad = cot + norm_back(normal, spread_scale, second_grad * g2)
    resid_win = m.resid_win
    resid_win[...] = resid_grad
    attended_grad = jnp.where(own, resid_grad, 0.0).astype(BF16)
    mg_send, mg_recv = m.mg_send, m.mg_recv

    def to_heads(step, sent, received):
        yield to_depth(mg_send.at[sent, tail], mg_recv.at[received, tail], sh.z_mg, step), mz >= 0
        first = to_depth(
            mg_send.at[sent, head], mg_recv.at[received, head], sh.z_mg, step, z_extra
        )
        yield first, received == 0

    def each(found, act):
        for copy, condition in found:

            @pl.when(condition)
            def _():
                act(copy)

    for step in order:
        mg_send[above(step)] = nt(attended_grad, wfull[above(step)]).astype(BF16)
        each(to_heads(step, above(step), mz), lambda c: c.start())
    mg_recv[mz] = nt(attended_grad, wfull[mz]).astype(BF16)
    normal, _ = normalize(resid[...])
    share = jnp.concatenate([in_part[c].astype(F32) for c in range(NC)], axis=1)
    share = share + jnp.where(mz == 0, rterm[...], 0.0)
    m.sp_send[...] = jnp.zeros((sh.small, D), F32)
    m.sp_send[0:E] = jnp.where(mz == 0, router_grad, 0.0)
    m.sp_send[E : E + 1] = jnp.sum(share * normal, axis=0, keepdims=True)
    m.sp_send[E + 1 : E + 2] = jnp.sum(share, axis=0, keepdims=True)

    B, BP = sh.share, sh.share_rows
    qg = ChipSum(sh.s_qg, m.qg_send, m.qg_pair, m.qg_recv)
    wg = ChipSum(sh.s_og, m.wg_send, m.wg_pair, m.wg_recv)
    lower = mz < Z // 2
    at_rows = pl.ds(pl.multiple_of(lax.rem(mz, Z // 2) * S, TILE), W)
    mixed_win = jnp.concatenate(
        [
            jnp.where(
                lower, mixed_all[p, at_rows][:, 0:L], mixed_all[p, at_rows][:, L : 2 * L]
            )
            for p in range(Z)
        ],
        axis=1,
    )
    wout_grad = tn(attended_grad, mixed_win)
    for e in range(E):
        m.wg_send[e % 2, e // 2, 0:B] = wout_grad[e * B : (e + 1) * B].astype(BF16)
    wg.start()
    bo_gather.start()
    for step in order:
        each(to_heads(step, 0, below(step)), lambda c: c.wait_recv())
    wg.cross()
    mixed_grad = m.mixed_grad
    put_together(mg_recv, mixed_grad)

    grads = [[], [], []]
    for h in range(sh.heads):
        mg = mixed_grad[:, h * HEAD_DIM : (h + 1) * HEAD_DIM]
        probs = probs_s[h]
        prob_grad = nt(mg, v_s[h])
        score_grad = (
            probs * (prob_grad - jnp.sum(prob_grad * probs, axis=1, keepdims=True))
        ).astype(BF16)
        grads[0].append((nn(score_grad, k_s[h]) * scale).astype(BF16))
        grads[1].append((tn(score_grad, q_s[h]) * scale).astype(BF16))
        grads[2].append(tn(probs.astype(BF16), mg).astype(BF16))
    projected_grad = jnp.concatenate(grads[0] + grads[1] + grads[2], axis=1)
    mix.finish()
    first_part = mix_part
    first = Scatter(sh.z_first, first_part, m.first_recv, m.first_pass)
    first_part[...] = nn(projected_grad, wqkv[...]).astype(BF16)
    first.start()

    qkv_grad = tn(first_low[...], projected_grad)
    for e in range(E):
        m.qg_send[e % 2, e // 2, 0:B] = qkv_grad[e * B : (e + 1) * B].astype(BF16)
    qg.start()
    normal, _ = normalize(pt[...].astype(F32))
    share = first_part[...].astype(F32)
    m.sp_send[E + 2 : E + 3] = jnp.sum(share * normal, axis=0, keepdims=True)
    m.sp_send[E + 3 : E + 4] = jnp.sum(share, axis=0, keepdims=True)
    smalls = SmallSum(sh.s_sp, m.sp_send, m.sp_pair, m.sp_half, m.sp_recv)
    smalls.start()
    first.relay()
    smalls.cross()

    bo_gather.relay()
    for step in bo_gather.rest():
        bo_gather.arrival(step)
    put_out(bo_all, outputs.block_out, range(Z))

    wz_send, wz_recv = m.wz_send, m.wz_recv
    total_w = wg.total()
    for position in range(Z):
        wz_send[position] = total_w[:, position * L : (position + 1) * L].astype(BF16)
    for step in order:
        to_depth(wz_send.at[above(step)], wz_recv.at[mz], sh.z_wz, step).start()
    zs_send, zs_recv = m.zs_send, m.zs_recv
    near = pl.ds(pl.multiple_of(sh.near(me), 128), sh.near_lanes)
    m.sp_total[...] = smalls.total()
    zs_send[...] = m.sp_total[:, near]
    for step in order:
        to_depth(zs_send, zs_recv.at[mz], sh.z_zs, step).start()

    normal, spread_scale = normalize(pt[window].astype(F32))
    first_grad = first.total()
    patch_grad = resid_win[...] + norm_back(normal, spread_scale, first_grad * g1)
    pg_all[mz] = patch_grad.astype(BF16)
    pg_gather = windows(sh.z_pg, pg_all)
    pg_gather.start()
    qg.cross()
    pg_gather.relay()
    total = qg.total()
    qkv_sum, wout_sum, small_sum = m.qkv_sum, m.wout_sum, m.small_sum
    for part in range(3):
        qkv_sum[part] = total[0:B, part * L : (part + 1) * L]
    store(qkv_sum, outputs.qkv_out)
    total_w = wz_send[mz].astype(F32)
    for step in order:
        to_depth(wz_send.at[0], wz_recv.at[below(step)], sh.z_wz, step).wait_recv()
        total_w = total_w + wz_recv[below(step)].astype(F32)
    wout_sum[...] = total_w[0:B]
    store(wout_sum, outputs.wout_out)
    small_sum[...] = zs_send[...]
    for step in order:
        to_depth(zs_send, zs_recv.at[below(step)], sh.z_zs, step).wait_recv()
        small_sum[...] += zs_recv[below(step)]
    store(small_sum, outputs.small_out)

    for step in (0,) + order:
        position = below(step)
        if step and not (relayed and step == 2):
            pg_gather.arrival(step)
        put_out(pg_all, outputs.patches_grad, [position])

    for step in range(1, Z):
        to_other(step).wait_send()

    to_plane(g_send.at[others], g_recv.at[others], sh.e_g, 1).wait_send()
    to_plane(x_send.at[others, common], x_recv.at[others, common], sh.e_x, 1).wait_send()
    if sh.split:
        rows = split_rows(mz)
        to_plane(x_send.at[others, rows], x_recv.at[others, rows], sh.e_xs, 1).wait_send()
    to_plane(gg_send.at[others], gg_home.at[others], sh.e_gg, 1).wait_send()
    to_plane(eo_send.at[others], eo_home.at[others], sh.e_eo, 1).wait_send()
    for c in range(NC):
        part = (others, slice(None), lanes(c))
        to_plane(ei_send.at[part], ei_home.at[part], sh.e_ei + c, 1).wait_send()
    for sent in ins + [first, qg, wg, smalls]:
        sent.finish()
    if sh.split:
        for strips_of in x_strips:
            strips_of.finish()
    for gather in (weights, mixing, bo_gather, pg_gather):
        gather.finish()
    for step in range(1, Z):
        each(to_heads(step, 0, mz), lambda c: c.wait_send())
        to_depth(wz_send.at[0], wz_recv.at[0], sh.z_wz, step).wait_send()
        to_depth(gz_send, gz_recv.at[0], sh.z_gz, step).wait_send()
        to_depth(zs_send, zs_recv.at[0], sh.z_zs, step).wait_send()
    for last in (2, 1):
        strip_copy(D // strip - last, outputs.up_out, (D // strip - last) % 2).wait()
        strip_copy(F // strip - last, outputs.down_out, 2 + (F // strip - last) % 2).wait()
    for copy, condition in stores:
        if condition is None:
            copy.wait()
        else:

            @pl.when(condition)
            def _():
                copy.wait()


def scratch_of(sh, F, in_count):
    E, Z, RP, R, D, NC = sh.experts, sh.depth, sh.padded, sh.rows, sh.width, sh.chunks
    CP, CL, CW, W = sh.slots, sh.slot_lanes, sh.chunk, sh.window
    B, BP, C = sh.share, sh.share_rows, sh.chips
    L, H = sh.local, sh.heads
    blocks = ((E, CP, D), BF16)
    dots = ((E, 8, CL), F32)
    rows = ((RP, D), BF16)
    part = ((NC, RP, CW), BF16)
    recv = ((NC, Z, W, CW), BF16)
    passing = ((NC, W, CW), BF16)
    every = ((Z, W, D), BF16)
    head = ((H, RP, HEAD_DIM), BF16)
    shapes = dict(
        gain1=((D,), F32),
        bias1=((D,), F32),
        gain2=((D,), F32),
        bias2=((D,), F32),
        router_t=((E, D), BF16),
        ids_row=((2, R), jnp.int32),
        noise_row=((2, R), F32),
        images_live=((1,), jnp.int32),
        patches=((R, D), BF16),
        out_grad=((R, D), BF16),
        up=((D, F), BF16),
        down=((F, D), BF16),
        wqkv=((3 * L, D), BF16),
        wfull=((Z, L, D), BF16),
        pt=rows,
        og=rows,
        first_low=rows,
        q_s=head,
        k_s=head,
        v_s=head,
        probs_s=((H, RP, RP), F32),
        mixed=((RP, L), BF16),
        mixed_all=((Z, sh.half_rows, 2 * L), BF16),
        resid=((RP, D), F32),
        second_low=rows,
        place=((RP, E * CP), BF16),
        x_send=blocks,
        x_recv=blocks,
        c_send=blocks,
        c_recv=blocks,
        g_send=dots,
        g_recv=dots,
        act=((E, CP, F), BF16),
        slope=((E, CP, F), BF16),
        delta=blocks,
        hid=((E, CP, F), BF16),
        eo_send=blocks,
        eo_home=blocks,
        ei_home=blocks,
        gg_send=dots,
        gg_home=dots,
        acc=((4, 128, max(F, D)), BF16),
        mix_part=rows,
        mix_recv=every,
        mix_pass=((W, D), BF16),
        in_part=part,
        in_recv=recv,
        in_pass=passing,
        first_recv=every,
        first_pass=((W, D), BF16),
        rterm=((RP, D), F32),
        resid_win=((W, D), F32),
        bo_all=every,
        pg_all=every,
        mg_send=((Z, W, L), BF16),
        mg_recv=((Z, W, L), BF16),
        mixed_grad=((RP, L), BF16),
        wz_send=((Z, BP, L), BF16),
        wz_recv=((Z, BP, L), BF16),
        gz_send=((8, RP), F32),
        gz_recv=((Z, 8, RP), F32),
        qg_send=((2, C, BP, 3 * L), BF16),
        qg_pair=((C, BP, 3 * L), BF16),
        qg_recv=((C, BP, 3 * L), BF16),
        wg_send=((2, C, BP, Z * L), BF16),
        wg_pair=((C, BP, Z * L), BF16),
        wg_recv=((C, BP, Z * L), BF16),
        sp_send=((sh.small, D), F32),
        sp_pair=((sh.small, D), F32),
        sp_half=((sh.small, D), F32),
        sp_total=((sh.small, D), F32),
        sp_recv=((C, sh.small, D), F32),
        qkv_sum=((3, B, L), F32),
        wout_sum=((B, L), F32),
        zs_send=((sh.small, sh.near_lanes), F32),
        zs_recv=((Z, sh.small, sh.near_lanes), F32),
        small_sum=((sh.small, sh.near_lanes), F32),
    )
    sems = dict(
        local_sem=4,
        in_sem=in_count,
        out_sem=4 * Z + 3,
        e_sem=sh.e_single * E + sh.e_kinds - sh.e_single,
        e_out=sh.e_kinds,
        z_sem=(sh.z_kinds, 2, Z),
        z_extra=(sh.z_kinds - sh.z_heads, 2, Z),
        s_sem=(sh.s_kinds, 2, Z),
        c_sem=(sh.s_kinds, 2, sh.chips),
    )
    scratch = {field: pltpu.VMEM(*shape) for field, shape in shapes.items()}
    for field, shape in sems.items():
        scratch[field] = pltpu.SemaphoreType.DMA(shape if isinstance(shape, tuple) else (shape,))
    return scratch


def outputs_kernel(sh, pieces, *refs):
    given, outs, held, made = refs[:7], refs[7:18], refs[18:25], refs[25:36]
    in_sem, out_sem = refs[36:]
    wout, small = held[5:]
    loads = [
        pltpu.make_async_copy(src, dst, in_sem.at[at])
        for at, (src, dst) in enumerate(zip(given[5:], (wout, small)))
    ]
    steps = []
    for src, through, ready, dst, number in zip(given, held, made, outs, pieces):
        rows = src.shape[0] // number
        for piece in range(number):
            at = pl.ds(piece * rows, rows)
            part = [ref if number == 1 else ref.at[at] for ref in (src, through, ready, dst)]
            load = pltpu.make_async_copy(part[0], part[1], in_sem.at[len(loads) + len(steps)])
            steps.append((load, part))
    for load in loads + [load for load, _ in steps]:
        load.start()
    for load in loads:
        load.wait()
    E, lanes = sh.experts, sh.near_lanes
    me = lax.axis_index("expert")
    begin = me * sh.share - sh.near(me)
    mine = pltpu.roll(small[...], lax.rem(lanes - begin, lanes), 1)[:, 0 : sh.share]
    made[5][...] = wout[...].T
    made[6][...] = mine[0:E]
    for at, gain in enumerate(made[7:]):
        gain[...] = mine[E + at]
    stores = []

    def store(src, dst):
        stores.append(pltpu.make_async_copy(src, dst, out_sem.at[len(stores)]))
        stores[-1].start()

    for src, dst in zip(made[5:], outs[5:]):
        store(src, dst)
    for load, (_, through, ready, dst) in steps:
        load.wait()
        if through.dtype == ready.dtype:
            store(through, dst)
        else:
            ready[...] = through[...].astype(ready.dtype)
            store(ready, dst)
    for copy in stores:
        copy.wait()


def on_device(
    mesh,
    patches,
    first_gain,
    first_bias,
    qkv_weight,
    out_weight,
    second_gain,
    second_bias,
    router_weight,
    up_weight,
    down_weight,
    expert_ids,
    router_noise,
    images_live,
    out_grad,
):
    row_count, model_width = patches.shape
    local_width = out_weight.shape[0]
    sh = Shapes(mesh, row_count, model_width, local_width)
    hidden_width = up_weight.shape[2]
    E, RP, D = sh.experts, sh.padded, sh.width
    anywhere = pl.BlockSpec(memory_space=pl.ANY)
    slots = E * sh.slots
    flops = 2 * (
        6 * slots * D * hidden_width
        + 3 * RP * D * 4 * local_width
        + 4 * slots * RP * D
        + 7 * sh.heads * RP * RP * HEAD_DIM
    )
    inputs = dict(
        gain1=first_gain,
        bias1=first_bias,
        gain2=second_gain,
        bias2=second_bias,
        router_t=router_weight.T,
        ids_row=expert_ids.T,
        noise_row=router_noise.T,
        images_live=images_live,
        wout=out_weight,
        out_grad=out_grad,
        patches=patches,
        wqkv=qkv_weight.transpose(1, 2, 0).reshape(3 * local_width, D),
        up=up_weight[0],
        down=down_weight[0],
    )
    outputs = dict(
        block_out=jax.ShapeDtypeStruct((RP, D), BF16),
        patches_grad=jax.ShapeDtypeStruct((RP, D), BF16),
        qkv_out=jax.ShapeDtypeStruct((3, sh.share, local_width), F32),
        wout_out=jax.ShapeDtypeStruct((sh.share, local_width), F32),
        small_out=jax.ShapeDtypeStruct((sh.small, sh.near_lanes), F32),
        up_out=jax.ShapeDtypeStruct((D, hidden_width), BF16),
        down_out=jax.ShapeDtypeStruct((hidden_width, D), BF16),
    )
    scratch = scratch_of(sh, hidden_width, len(inputs))
    fields = tuple(tuple(group) for group in (inputs, outputs, scratch))
    outs = pl.pallas_call(
        functools.partial(whole_kernel, sh, fields),
        out_shape=tuple(outputs.values()),
        in_specs=[anywhere] * len(inputs),
        out_specs=(anywhere,) * len(outputs),
        scratch_shapes=list(scratch.values()),
        compiler_params=pltpu.CompilerParams(
            collective_id=0, has_side_effects=True, vmem_limit_bytes=62 << 20
        ),
        cost_estimate=pl.CostEstimate(flops=flops, bytes_accessed=16 << 20, transcendentals=0),
        name="block",
    )(*inputs.values())
    block_out, patches_grad, qkv_grad, wout_grad, small, up_grad, down_grad = outs
    pieces = (1, 1, 1, 4, 4)
    wholes = (block_out[:row_count], patches_grad[:row_count], qkv_grad, up_grad, down_grad)
    inputs = wholes + (wout_grad, small)
    kinds = (BF16, F32, F32, F32, F32)
    results = tuple(jax.ShapeDtypeStruct(w.shape, kind) for w, kind in zip(wholes, kinds)) + (
        jax.ShapeDtypeStruct((local_width, sh.share), F32),
        jax.ShapeDtypeStruct((E, sh.share), F32),
    )
    results += (jax.ShapeDtypeStruct((sh.share,), F32),) * 4
    copies = sum(pieces)
    results = pl.pallas_call(
        functools.partial(outputs_kernel, sh, pieces),
        out_shape=results,
        in_specs=[anywhere] * len(inputs),
        out_specs=(anywhere,) * len(results),
        scratch_shapes=[pltpu.VMEM(w.shape, w.dtype) for w in inputs + results]
        + [pltpu.SemaphoreType.DMA((copies + 2,)), pltpu.SemaphoreType.DMA((copies + 6,))],
        compiler_params=pltpu.CompilerParams(vmem_limit_bytes=62 << 20),
        name="outputs",
    )(*inputs)
    block_out, patches_grad, qkv_grad, up_grad, down_grad, wout_grad, router_grad = results[:7]
    gain2_grad, bias2_grad, gain1_grad, bias1_grad = results[7:]
    return (
        block_out,
        patches_grad,
        gain1_grad,
        bias1_grad,
        qkv_grad.transpose(1, 0, 2),
        wout_grad,
        gain2_grad,
        bias2_grad,
        router_grad.T,
        up_grad[None],
        down_grad[None],
    )


def solution(mesh):
    placed = (
        P("expert", None),
        P(),
        P(),
        P(None, None, "tensor"),
        P("tensor", None),
        P(),
        P(),
        P(),
        P("expert", None, "tensor"),
        P("expert", "tensor", None),
        P("expert", None),
        P("expert", None),
        P("expert"),
        P("expert", None),
    )
    return jax.shard_map(
        functools.partial(on_device, mesh),
        mesh=mesh,
        in_specs=placed,
        out_specs=(
            P("expert", None),
            P("expert", None),
            P("expert"),
            P("expert"),
            P("expert", None, "tensor"),
            P("tensor", "expert"),
            P("expert"),
            P("expert"),
            P("expert", None),
            P("expert", None, "tensor"),
            P("expert", "tensor", None),
        ),
        check_vma=False,
    )
```

```python
import functools
from types import SimpleNamespace

import jax
import jax.numpy as jnp
from jax import lax
from jax.experimental import pallas as pl
from jax.experimental.pallas import tpu as pltpu
from jax.sharding import PartitionSpec as P

HEAD_DIM = 64
TOK_IMG = 197
TILE = 16
EPSILON = 1e-06
MESH = pl.DeviceIdType.MESH
F32 = jnp.float32
BF16 = jnp.bfloat16


def round_up(value, unit):
    return (value + unit - 1) // unit * unit


def nn(a, b):
    return lax.dot_general(a, b, (((1,), (0,)), ((), ())), preferred_element_type=F32)


def nt(a, b):
    return lax.dot_general(a, b, (((1,), (1,)), ((), ())), preferred_element_type=F32)


def tn(a, b):
    return lax.dot_general(a, b, (((0,), (0,)), ((), ())), preferred_element_type=F32)


def in_three(values):
    high = values.astype(BF16)
    rest = values - high.astype(F32)
    middle = rest.astype(BF16)
    return high, middle, (rest - middle.astype(F32)).astype(BF16)


def normalize(values):
    center = values - jnp.mean(values, axis=-1, keepdims=True)
    scale = lax.rsqrt(jnp.mean(center * center, axis=-1, keepdims=True) + EPSILON)
    return center * scale, scale


def norm_back(normal, scale, grad_normal):
    return scale * (
        grad_normal
        - jnp.mean(grad_normal, axis=-1, keepdims=True)
        - normal * jnp.mean(grad_normal * normal, axis=-1, keepdims=True)
    )


class Shapes:
    def __init__(self, mesh, row_count, model_width, local_width):
        self.experts = mesh.shape["expert"]
        self.depth = mesh.shape["tensor"]
        self.rows = row_count
        self.width = model_width
        self.local = local_width
        self.heads = local_width // HEAD_DIM
        self.padded = round_up(row_count, TILE)
        self.capacity = (3 * row_count + self.experts - 1) // self.experts
        self.slots = round_up(self.capacity, TILE)
        self.split = self.depth * TILE if self.slots >= 2 * self.depth * TILE else 0
        self.common = self.slots - self.split
        self.slot_lanes = round_up(self.slots, 128)
        self.step = (self.padded - TILE) // self.depth
        self.window = self.step + TILE
        self.share = model_width // self.experts
        self.share_rows = round_up(self.share, TILE)
        self.small = round_up(self.experts + 4, 8)
        self.near_lanes = min(256, model_width)
        self.half_rows = round_up(self.padded // 2, TILE)
        self.chunk = 256
        self.chunks = model_width // self.chunk
        (
            self.e_c,
            self.e_g,
            self.e_x,
            self.e_xs,
            self.e_gg,
            self.e_eo,
            self.e_ei,
        ) = range(7)
        self.e_single = self.e_gg
        self.e_kinds = self.e_ei + self.chunks
        self.chips = self.experts // 2
        self.s_w, self.s_qg, self.s_og, self.s_sp = range(4)
        self.s_kinds = 4
        (
            self.z_w,
            self.z_m,
            self.z_gz,
            self.z_wz,
            self.z_zs,
            self.z_x,
            self.z_y,
            self.z_bo,
            self.z_mg,
            self.z_pg,
            self.z_mix,
            self.z_in,
        ) = range(12)
        self.z_heads = self.z_bo
        self.z_first = self.z_in + self.chunks
        self.z_more = self.z_first + self.chunks
        self.z_kinds = self.z_more + 1


    def near(self, expert):
        return jnp.minimum(expert * self.share // 128 * 128, self.width - self.near_lanes)


def whole_kernel(sh, fields, *refs):
    E, Z, NC = sh.experts, sh.depth, sh.chunks
    R, RP, D = sh.rows, sh.padded, sh.width
    CP, CL, CW = sh.slots, sh.slot_lanes, sh.chunk
    taken = iter(refs)
    inputs, outputs, m = (SimpleNamespace(**{f: next(taken) for f in group}) for group in fields)
    e_sem, z_sem, z_extra, s_sem, c_sem = m.e_sem, m.z_sem, m.z_extra, m.s_sem, m.c_sem
    local_sem, in_sem, out_sem = m.local_sem, m.in_sem, m.out_sem
    me = lax.axis_index("expert")
    mz = lax.axis_index("tensor")

    def plane(step):
        return lax.rem(me + step, E)

    def before(step):
        return lax.rem(me - step + E, E)

    def above(step):
        return lax.rem(mz + step, Z)

    def below(step):
        return lax.rem(mz - step + Z, Z)

    def remote(src, dst, sems, kind, sent, received, expert, position):
        if sems is e_sem:
            single = sh.e_single
            place_of = kind * E + received if kind < single else single * E + kind - single
            send_sem, recv_sem = m.e_out.at[kind], e_sem.at[place_of]
        else:
            row = kind - sh.z_heads if sems is z_extra else kind
            send_sem, recv_sem = sems.at[row, 0, sent], sems.at[row, 1, received]
        return pltpu.make_async_remote_copy(
            src_ref=src,
            dst_ref=dst,
            send_sem=send_sem,
            recv_sem=recv_sem,
            device_id=(expert, position),
            device_id_type=MESH,
        )

    def to_plane(src, dst, kind, step):
        return remote(src, dst, e_sem, kind, step, step, plane(step), mz)

    core = lax.rem(me, 2)
    chip = me // 2
    sibling = me + 1 - 2 * core

    def to_sibling(src, dst, kind, step=0):
        return remote(src, dst, s_sem, kind, step, step, sibling, mz)

    def to_chip(src, dst, kind, step):
        target = lax.rem(chip + step, sh.chips)
        return remote(src, dst, c_sem, kind, step, step, 2 * target + core, mz)

    def chip_after(step):
        return lax.rem(chip + step, sh.chips)

    def chip_before(step):
        return lax.rem(chip - step + sh.chips, sh.chips)

    class ChipSum:
        def __init__(self, kind, send, pair, recv):
            self.kind, self.send, self.pair, self.recv = kind, send, pair, recv

        def halves(self):
            return to_sibling(self.send.at[1 - core], self.pair, self.kind)

        def start(self):
            self.halves().start()

        def cross(self):
            self.halves().wait_recv()
            half = self.send[core].astype(F32) + self.pair[...].astype(F32)
            self.send[core] = half.astype(self.send.dtype)
            for step in range(1, sh.chips):
                self.block(step, chip_after(step)).start()

        def block(self, step, target):
            return to_chip(self.send.at[core, target], self.recv.at[chip], self.kind, step)

        def total(self):
            value = self.send[core, chip].astype(F32)
            for step in range(1, sh.chips):
                source = chip_before(step)
                to_chip(
                    self.send.at[core, 0], self.recv.at[source], self.kind, step
                ).wait_recv()
                value = value + self.recv[source].astype(F32)
            return value

        def finish(self):
            self.halves().wait_send()
            for step in range(1, sh.chips):
                self.block(step, 0).wait_send()

    class SmallSum:
        def __init__(self, kind, send, pair, half, recv):
            self.kind, self.send, self.pair, self.half, self.recv = kind, send, pair, half, recv

        def exchange(self):
            return to_sibling(self.send, self.pair, self.kind)

        def start(self):
            self.exchange().start()

        def cross(self):
            self.exchange().wait_recv()
            self.half[...] = self.send[...] + self.pair[...]
            for step in range(1, sh.chips):
                to_chip(self.half, self.recv.at[chip], self.kind, step).start()

        def total(self):
            value = self.half[...]
            for step in range(1, sh.chips):
                source = chip_before(step)
                to_chip(self.half, self.recv.at[source], self.kind, step).wait_recv()
                value = value + self.recv[source]
            return value

        def finish(self):
            self.exchange().wait_send()
            for step in range(1, sh.chips):
                to_chip(self.half, self.recv.at[chip], self.kind, step).wait_send()

    def back_to(src, dst, kind, step):
        return remote(src, dst, e_sem, kind, step, step, before(step), mz)

    def to_depth(src, dst, kind, step, sems=None):
        sems = z_sem if sems is None else sems
        return remote(src, dst, sems, kind, step, step, me, above(step))

    relayed = Z == 4
    between = (mz > 0) & (mz < Z - 1)

    def direct(step, hold=False):
        if not relayed:
            return mz >= 0
        if step == 1:
            return mz < Z - 1
        if step == Z - 1:
            return mz > 0
        return jnp.logical_not(between) if hold else mz >= 0

    def arrives(step):
        if not relayed:
            return mz >= 0
        if step == 1:
            return mz > 0
        if step == Z - 1:
            return mz < Z - 1
        return mz >= 0

    order = (2, 1, 3) if relayed else tuple(range(1, Z))

    m.wout = m.wfull.at[mz]
    loads = SimpleNamespace()
    for at, (field, source) in enumerate(vars(inputs).items()):
        copy = pltpu.make_async_copy(source, getattr(m, field), in_sem.at[at])
        copy.start()
        setattr(loads, field, copy)

    def loaded(*copies):
        for copy in copies:
            copy.wait()

    stores = []

    def store(src, dst, condition=None):
        copy = pltpu.make_async_copy(src, dst, out_sem.at[len(stores)])
        stores.append((copy, condition))
        if condition is None:
            copy.start()
        else:

            @pl.when(condition)
            def _():
                copy.start()

    gain1, bias1, gain2, bias2 = m.gain1, m.bias1, m.gain2, m.bias2
    router_t, ids_row, noise_row, images_live = m.router_t, m.ids_row, m.noise_row, m.images_live
    barrier = pltpu.get_barrier_semaphore()
    for step in range(1, E):
        pl.semaphore_signal(barrier, inc=1, device_id=(plane(step), mz), device_id_type=MESH)
    for step in range(1, Z):
        pl.semaphore_signal(barrier, inc=1, device_id=(me, above(step)), device_id_type=MESH)

    S, W = sh.step, sh.window

    def tail_of(position):
        if isinstance(position, int):
            return pl.ds(position * S + TILE, S)
        return pl.ds(pl.multiple_of(position * S + TILE, TILE), S)

    def window_of(position):
        return pl.ds(pl.multiple_of(position * S, TILE), W)

    head, tail = pl.ds(0, TILE), pl.ds(TILE, S)

    class Scatter:
        def __init__(self, kind, part, recv, passing):
            self.kind, self.part, self.recv, self.passing = kind, part, recv, passing

        def send_to(self, step):
            target = above(step)
            return (
                to_depth(self.part.at[tail_of(target)], self.recv.at[mz, tail], self.kind, step),
                to_depth(self.part.at[head], self.recv.at[mz, head], self.kind, step, z_extra),
                target == 0,
            )

        def pass_to(self):
            source = self.passing
            return (
                to_depth(source.at[tail], self.recv.at[mz, tail], self.kind, 2),
                to_depth(source.at[head], self.recv.at[mz, head], self.kind, 2, z_extra),
                above(2) == 0,
            )

        def far(self):
            kind = self.kind
            up_to, down_to = (
                remote(
                    self.part.at[tail_of(Z - 1 - end)],
                    self.passing.at[tail],
                    z_sem,
                    kind,
                    0,
                    0,
                    me,
                    1 if end == 0 else Z - 2,
                )
                for end in (0, Z - 1)
            )
            down_head = remote(
                self.part.at[head],
                self.passing.at[head],
                z_extra,
                kind,
                0,
                0,
                me,
                Z - 2,
            )
            return up_to, down_to, down_head

        def start(self):
            if relayed:
                up_to, down_to, down_head = self.far()

                @pl.when(mz == 0)
                def _():
                    up_to.start()

                @pl.when(mz == Z - 1)
                def _():
                    down_to.start()
                    down_head.start()

            for step in order:
                body, first, is_head = self.send_to(step)

                @pl.when(direct(step, hold=True))
                def _():
                    body.start()

                @pl.when(direct(step, hold=True) & is_head)
                def _():
                    first.start()

        def relay(self):
            if not relayed:
                return

            @pl.when(between)
            def _():
                up_to, down_to, down_head = self.far()
                up_to.wait_recv()

                @pl.when(mz == Z - 2)
                def _():
                    down_head.wait_recv()

                target = above(2)
                self.passing[...] = (
                    self.passing[...].astype(F32) + self.part[window_of(target)].astype(F32)
                ).astype(BF16)
                body, first, is_head = self.pass_to()
                body.start()

                @pl.when(is_head)
                def _():
                    first.start()

        def total(self):
            value = self.part[window_of(mz)].astype(F32)
            for step in order:
                source = below(step)
                here = arrives(step)
                body = to_depth(
                    self.part.at[tail_of(0)], self.recv.at[source, tail], self.kind, step
                )
                first = to_depth(
                    self.part.at[head], self.recv.at[source, head], self.kind, step, z_extra
                )

                @pl.when(here)
                def _():
                    body.wait_recv()

                @pl.when(here & (mz == 0))
                def _():
                    first.wait_recv()

                value = value + jnp.where(here, self.recv[source].astype(F32), 0.0)
            return value

        def finish(self):
            if relayed:
                up_to, down_to, down_head = self.far()

                @pl.when(mz == 0)
                def _():
                    up_to.wait_send()

                @pl.when(mz == Z - 1)
                def _():
                    down_to.wait_send()
                    down_head.wait_send()

            for step in order:
                body, first, is_head = self.send_to(step)

                @pl.when(direct(step))
                def _():
                    body.wait_send()

                @pl.when(direct(step) & is_head)
                def _():
                    first.wait_send()

    class Gather:
        def __init__(self, kind, every, body=(), first=None):
            self.kind, self.every, self.body, self.first = kind, every, body, first

        def blocks(self, origin):
            found = [(self.every.at[(origin,) + self.body], z_sem, True)]
            if self.first is not None:
                found.append((self.every.at[(origin,) + self.first], z_extra, origin == 0))
            return found

        def copies(self, origin, step):
            return [
                (to_depth(block, block, self.kind, step, sems), holds)
                for block, sems, holds in self.blocks(origin)
            ]

        def passed(self):
            target, step = (Z - 1) * (mz - 1), 2 * mz - 1
            return [
                (remote(block, block, sems, self.kind, 0, step, me, target), holds)
                for block, sems, holds in self.blocks(below(2))
            ]

        def each(self, found, condition, act):
            for copy, holds in found:

                @pl.when(condition & holds)
                def _():
                    act(copy)

        def start(self):
            for step in order:
                self.each(self.copies(mz, step), direct(step), lambda c: c.start())

        def arrival(self, step):
            self.each(self.copies(below(step), step), mz >= 0, lambda c: c.wait_recv())

        def relay(self):
            if relayed:
                self.arrival(2)
                self.each(self.passed(), between, lambda c: c.start())

        def rest(self):
            return tuple(step for step in order if not (relayed and step == 2))

        def finish(self):
            for step in order:
                self.each(self.copies(mz, step), direct(step), lambda c: c.wait_send())
            if relayed:
                self.each(self.passed(), between, lambda c: c.wait_send())

    def split_rows(position):
        return pl.ds(pl.multiple_of(sh.common + position * TILE, TILE), TILE)

    class Strips(Gather):
        def blocks(self, origin):
            return [(self.every.at[self.body, split_rows(origin)], z_sem, True)]

    def windows(kind, every):
        return Gather(kind, every, (tail,), (head,))

    def put_out(every, out, positions):
        for position in positions:
            store(every.at[position, tail], out.at[tail_of(position)])
            store(every.at[position, head], out.at[head], position == 0)

    def put_together(every, dest):
        dest[0:TILE] = every[0, 0:TILE]
        for position in range(Z):
            dest[TILE + S * position : TILE + S * (position + 1)] = every[position, TILE:W]

    def scatters(kind, part, recv, passing):
        return [
            Scatter(kind + c, part.at[c], recv.at[c], passing.at[c]) for c in range(NC)
        ]

    window = window_of(mz)
    own = (lax.broadcasted_iota(jnp.int32, (W, 1), 0) >= TILE) | (mz == 0)

    loaded(loads.ids_row, loads.images_live, loads.noise_row)
    live_rows = images_live[...].reshape(1, 1) * TOK_IMG
    lane = lax.broadcasted_iota(jnp.int32, (1, R), 1)
    live = (lane < live_rows).astype(F32)
    expert_of = lax.broadcasted_iota(jnp.int32, (E, R), 0)
    ids = ids_row[...]
    hot = [(expert_of == ids[k : k + 1]).astype(F32) * live for k in range(2)]
    earlier = (
        lax.broadcasted_iota(jnp.int32, (R, R), 0) < lax.broadcasted_iota(jnp.int32, (R, R), 1)
    ).astype(BF16)
    counts = [nn(h.astype(BF16), earlier) for h in hot]
    counts[1] = counts[1] + jnp.sum(hot[0], axis=1, keepdims=True)
    start = expert_of.astype(F32) * CP
    spot = [
        jnp.where(live > 0, jnp.sum(hot[k] * (counts[k] + start), axis=0, keepdims=True), -1.0)
        for k in range(2)
    ]
    blank = jnp.zeros((1, RP - R), F32)
    live, *hot = (
        jnp.concatenate([v, jnp.zeros((v.shape[0], RP - R), F32)], axis=1) for v in (live, *hot)
    )
    noise = jnp.concatenate([noise_row[...], jnp.zeros((2, RP - R), F32)], axis=1)
    spot_row = [jnp.concatenate([s, blank - 1.0], axis=1).astype(jnp.int32) for s in spot]
    eye_rows = lax.broadcasted_iota(jnp.int32, (RP, RP), 0) == lax.broadcasted_iota(
        jnp.int32, (RP, RP), 1
    )
    spot_col = [
        jnp.sum(jnp.where(eye_rows, s.astype(F32), 0.0), axis=1, keepdims=True).astype(jnp.int32)
        for s in spot_row
    ]

    def spread(e):
        slot = lax.broadcasted_iota(jnp.int32, (CP, RP), 0) + e * CP
        return slot == spot_row[0], slot == spot_row[1]

    eye_slots = lax.broadcasted_iota(jnp.int32, (CP, CL), 0) == lax.broadcasted_iota(
        jnp.int32, (CP, CL), 1
    )

    def as_row(column):
        return jnp.sum(jnp.where(eye_slots, column, 0.0), axis=0, keepdims=True)

    def as_column(row):
        return jnp.sum(jnp.where(eye_slots, row, 0.0), axis=1, keepdims=True)

    loaded(loads.wout)
    pl.semaphore_wait(barrier, E - 1 + Z - 1)
    half = D // 2
    columns = pl.ds(pl.multiple_of(core * half, 128), half)
    weights = Gather(sh.z_w, m.wfull, (slice(None), columns))
    weights.start()

    row_of = lax.broadcasted_iota(jnp.int32, (R, 1), 0)
    og, pt = m.og, m.pt
    og[pl.ds(RP - TILE, TILE)] = jnp.zeros((TILE, D), BF16)
    loaded(loads.out_grad)
    og[0:R] = jnp.where(row_of < live_rows, m.out_grad[...], jnp.zeros((), BF16))
    c_send, c_recv = m.c_send, m.c_recv

    def pack_cotangent(step, carry):
        e = plane(step)
        s0, s1 = spread(e)
        c_send[e] = nn((s0 | s1).astype(BF16), og[...]).astype(BF16)

        @pl.when(step > 0)
        def _():
            to_plane(c_send.at[e], c_recv.at[step], sh.e_c, step).start()

        return carry

    lax.fori_loop(0, E, pack_cotangent, 0)
    c_recv[0] = c_send[me]

    pt[pl.ds(RP - TILE, TILE)] = jnp.zeros((TILE, D), BF16)
    loaded(loads.patches, loads.gain1, loads.bias1, loads.gain2, loads.bias2, loads.router_t)
    pt[0:R] = m.patches[...]
    first_low, wqkv = m.first_low, m.wqkv
    g1, b1 = gain1[...].reshape(1, D), bias1[...].reshape(1, D)
    g2, b2 = gain2[...].reshape(1, D), bias2[...].reshape(1, D)
    normal, _ = normalize(pt[...].astype(F32))
    first_low[...] = (normal * g1 + b1).astype(BF16)
    loaded(loads.wqkv)
    projected = nt(first_low[...], wqkv[...]).astype(BF16)
    q_s, k_s, v_s, probs_s = m.q_s, m.k_s, m.v_s, m.probs_s
    for h in range(sh.heads):
        for part, dest in enumerate((q_s, k_s, v_s)):
            begin = part * sh.local + h * HEAD_DIM
            dest[h] = projected[:, begin : begin + HEAD_DIM]
    row2 = lax.broadcasted_iota(jnp.int32, (RP, RP), 0)
    col2 = lax.broadcasted_iota(jnp.int32, (RP, RP), 1)
    same = ((row2 >= TOK_IMG) == (col2 >= TOK_IMG)) & (col2 < R)
    scale = HEAD_DIM ** (-0.5)
    heads = []
    for h in range(sh.heads):
        scores = jnp.where(same, nt(q_s[h], k_s[h]) * scale, -1e30)
        exponent = jnp.exp(scores - jnp.max(scores, axis=1, keepdims=True))
        probs = exponent / jnp.sum(exponent, axis=1, keepdims=True)
        probs_s[h] = probs
        heads.append(nn(probs.astype(BF16), v_s[h]).astype(BF16))
    mixed, mixed_all = m.mixed, m.mixed_all
    mixed[...] = jnp.concatenate(heads, axis=1)
    HR, L = sh.half_rows, sh.local
    mixed_all[mz] = jnp.concatenate([mixed[0:HR], mixed[RP - HR : RP]], axis=1)
    mixing = Gather(sh.z_m, mixed_all)
    mixing.start()

    wfull = m.wfull

    def to_other(step):
        block = wfull.at[below(step), :, columns]
        return to_sibling(block, block, sh.s_w, step)

    weights.relay()
    if relayed:
        to_other(2).start()
    for step in weights.rest():
        weights.arrival(step)
        to_other(step).start()

    resid, second_low = m.resid, m.second_low

    def attend(position):
        block = mixed_all[position]
        weight = wfull[position]
        return nn(block[:, 0:L], weight), nn(block[2 * HR - RP :, L : 2 * L], weight)

    low, high = attend(mz)
    resid[0:HR] = pt[0:HR].astype(F32) + low
    resid[HR:RP] = pt[HR:RP].astype(F32) + high
    mixing.relay()
    for step in order:
        if not (relayed and step == 2):
            mixing.arrival(step)
        to_other(step).wait_recv()
        low, high = attend(below(step))
        resid[0:HR] += low
        resid[HR:RP] += high

    normal, _ = normalize(resid[...])
    second_low[...] = (normal * g2 + b2).astype(BF16)
    logits = nt(router_t[...], second_low[...])
    chosen = [
        jnp.sum(hot[k] * logits, axis=0, keepdims=True) + noise[k : k + 1, :] for k in range(2)
    ]
    top = jnp.maximum(chosen[0], chosen[1])
    powers = [jnp.exp(c - top) for c in chosen]
    gates = [p / (powers[0] + powers[1]) for p in powers]
    x_send, x_recv, g_send, g_recv = m.x_send, m.x_recv, m.g_send, m.g_recv

    def pack_rows(step, carry):
        e = plane(step)
        s0, s1 = spread(e)
        x_send[e] = nn((s0 | s1).astype(BF16), second_low[...]).astype(BF16)
        gate = jnp.sum(
            jnp.where(s0, gates[0], 0.0) + jnp.where(s1, gates[1], 0.0), axis=1, keepdims=True
        )
        g_send[e] = jnp.broadcast_to(as_row(gate), (8, CL))

        @pl.when(step > 0)
        def _():
            to_plane(g_send.at[e], g_recv.at[step], sh.e_g, step).start()
            if sh.split:
                strip_to(e, step).start()
            else:
                common_to(e, step).start()

        return carry

    common = pl.ds(0, sh.common)

    def common_to(sent, step):
        return to_plane(x_send.at[sent, common], x_recv.at[step, common], sh.e_x, step)

    def strip_to(sent, step):
        rows = split_rows(mz)
        return to_plane(x_send.at[sent, rows], x_recv.at[step, rows], sh.e_xs, step)

    lax.fori_loop(0, E, pack_rows, 0)
    if sh.split:

        def send_common(step, carry):
            common_to(plane(step), step).start()
            return carry

        lax.fori_loop(1, E, send_common, 0)
        x_recv[0, split_rows(mz)] = x_send[me, split_rows(mz)]
    g_recv[0] = g_send[me]
    x_recv[0, common] = x_send[me, common]
    place = m.place
    slot_lane = lax.broadcasted_iota(jnp.int32, (RP, E * CP), 1)
    place[...] = ((slot_lane == spot_col[0]) | (slot_lane == spot_col[1])).astype(BF16)

    loaded(loads.up, loads.down)
    up, down, act, slope = m.up, m.down, m.act, m.slope
    delta, hid, eo_send, eo_home = m.delta, m.hid, m.eo_send, m.eo_home
    gg_send, gg_home, ei_home = m.gg_send, m.gg_home, m.ei_home

    halves = ((0, E // 2), (E // 2, E))
    x_strips = [Strips(sh.z_x + at, x_recv, pl.ds(a, b - a)) for at, (a, b) in enumerate(halves)]
    if sh.split:

        def strip_arrived(step, carry):
            strip_to(0, step).wait_recv()
            return carry

        for strips_of, (a, b) in zip(x_strips, halves):
            lax.fori_loop(max(a, 1), b, strip_arrived, 0)
            strips_of.start()

    def forward(step, carry):

        @pl.when(step > 0)
        def _():
            to_plane(g_send.at[0], g_recv.at[step], sh.e_g, step).wait_recv()
            common_to(0, step).wait_recv()
            to_plane(c_send.at[0], c_recv.at[step], sh.e_c, step).wait_recv()

        hidden = nn(x_recv[step], up[...])
        below_it = 0.5 * (1.0 + lax.erf(hidden * (0.5**0.5)))
        bell = jnp.exp(-0.5 * hidden * hidden) * 0.3989422804014327
        act[step] = (hidden * below_it).astype(BF16)
        slope[step] = (below_it + hidden * bell).astype(BF16)
        result = nn(act[step], down[...])
        gate = as_column(g_recv[step][0:1])
        given = c_recv[step].astype(F32)
        dots = jnp.sum(given * result, axis=1, keepdims=True)
        gg_send[step] = jnp.broadcast_to(as_row(dots), (8, CL))
        eo_send[step] = (gate * result).astype(BF16)
        delta[step] = (gate * given).astype(BF16)

        @pl.when(step > 0)
        def _():
            back_to(gg_send.at[step], gg_home.at[me], sh.e_gg, step).start()
            back_to(eo_send.at[step], eo_home.at[me], sh.e_eo, step).start()

        return carry

    for strips_of, (a, b) in zip(x_strips, halves):
        if sh.split:
            strips_of.relay()
            for step in strips_of.rest():
                strips_of.arrival(step)
        lax.fori_loop(a, b, forward, 0)
    gg_home[me] = gg_send[0]
    eo_home[me] = eo_send[0]

    others = pl.ds(0, E - 1)
    to_plane(c_send.at[others], c_recv.at[others], sh.e_c, 1).wait_send()
    ei_send = c_send

    def lanes(c):
        return pl.ds(c * CW, CW)

    for c in range(NC):

        def backward(step, carry):
            if c == 0:
                hid[step] = (nt(delta[step], down[...]) * slope[step]).astype(BF16)
            ei_send[step, :, lanes(c)] = nt(hid[step], up[lanes(c), :]).astype(BF16)

            @pl.when(step > 0)
            def _():
                back_to(
                    ei_send.at[step, :, lanes(c)], ei_home.at[me, :, lanes(c)], sh.e_ei + c, step
                ).start()

            return carry

        lax.fori_loop(0, E, backward, 0)
    ei_home[me] = ei_send[0]

    strip = 128
    F = up.shape[1]
    acc = m.acc

    def flat(ref, first, size):
        return ref[:, :, pl.ds(pl.multiple_of(first, 128), size)].reshape(E * CP, size)

    def strip_copy(i, out, slot):
        return pltpu.make_async_copy(
            acc.at[slot], out.at[pl.ds(pl.multiple_of(i * strip, strip), strip)], local_sem.at[slot]
        )

    def strips(out, lhs, rhs, count, slot):
        def one(i, carry):
            at = slot + lax.rem(i, 2)

            @pl.when(i >= 2)
            def _():
                strip_copy(i - 2, out, at).wait()

            acc[at] = tn(flat(lhs, i * strip, strip), flat(rhs, 0, rhs.shape[2])).astype(BF16)
            strip_copy(i, out, at).start()
            return carry

        lax.fori_loop(0, count, one, 0)

    strips(outputs.up_out, x_recv, hid, D // strip, 0)
    strips(outputs.down_out, act, delta, F // strip, 2)

    to_plane(gg_send.at[others], gg_home.at[others], sh.e_gg, 1).wait_recv()

    def pick_dots(e, totals):
        s0, s1 = spread(e)
        column = as_column(gg_home[e][0:1])
        return (
            totals[0] + jnp.sum(jnp.where(s0, column, 0.0), axis=0, keepdims=True),
            totals[1] + jnp.sum(jnp.where(s1, column, 0.0), axis=0, keepdims=True),
        )

    nothing = jnp.zeros((1, RP), F32)
    dots0, dots1 = lax.fori_loop(0, E, pick_dots, (nothing, nothing))
    gz_send, gz_recv = m.gz_send, m.gz_recv
    gz_send[...] = jnp.zeros((8, RP), F32)
    gz_send[0:1] = dots0
    gz_send[1:2] = dots1
    for step in range(1, Z):
        to_depth(gz_send, gz_recv.at[mz], sh.z_gz, step).start()
    mix_part, in_part = m.mix_part, m.in_part
    mix = Scatter(sh.z_mix, mix_part, m.mix_recv, m.mix_pass)
    to_plane(eo_send.at[others], eo_home.at[others], sh.e_eo, 1).wait_recv()
    mix_part[...] = nn(place[...], eo_home[...].reshape(E * CP, D)).astype(BF16)
    mix.start()
    mix.relay()
    gate_grad = gz_send[...]
    for step in range(1, Z):
        to_depth(gz_send, gz_recv.at[below(step)], sh.z_gz, step).wait_recv()
        gate_grad = gate_grad + gz_recv[below(step)]
    both = gates[0] * gate_grad[0:1] + gates[1] * gate_grad[1:2]
    logit_grad = sum(hot[k] * (gates[k] * (gate_grad[k : k + 1] - both)) for k in range(2))
    parts = in_three(logit_grad)
    router_grad = sum(nn(p, second_low[...]) for p in parts)
    rterm = m.rterm
    rterm[...] = sum(tn(p, router_t[...]) for p in parts)

    ins = scatters(sh.z_in, in_part, m.in_recv, m.in_pass)
    bo_all, pg_all = m.bo_all, m.pg_all
    bo_gather = windows(sh.z_bo, bo_all)
    for c in range(NC):
        to_plane(
            ei_send.at[others, :, lanes(c)], ei_home.at[others, :, lanes(c)], sh.e_ei + c, 1
        ).wait_recv()
        home = ei_home[:, :, lanes(c)].reshape(E * CP, CW)
        in_part[c] = nn(place[...], home).astype(BF16)
        ins[c].start()
        if c == 0:
            mixture = mix.total()
            at = lax.broadcasted_iota(jnp.int32, (W, 1), 0) + mz * S
            bo_all[mz] = jnp.where(at < live_rows, resid[window] + mixture, 0.0).astype(BF16)
        ins[c].relay()

    cot = og[window].astype(F32)
    normal, spread_scale = normalize(resid[window])
    second_grad = jnp.concatenate([part.total() for part in ins], axis=1) + rterm[window]
    resid_grad = cot + norm_back(normal, spread_scale, second_grad * g2)
    resid_win = m.resid_win
    resid_win[...] = resid_grad
    attended_grad = jnp.where(own, resid_grad, 0.0).astype(BF16)
    mg_send, mg_recv = m.mg_send, m.mg_recv

    def to_heads(step, sent, received):
        yield to_depth(mg_send.at[sent, tail], mg_recv.at[received, tail], sh.z_mg, step), mz >= 0
        first = to_depth(
            mg_send.at[sent, head], mg_recv.at[received, head], sh.z_mg, step, z_extra
        )
        yield first, received == 0

    def each(found, act):
        for copy, condition in found:

            @pl.when(condition)
            def _():
                act(copy)

    for step in order:
        mg_send[above(step)] = nt(attended_grad, wfull[above(step)]).astype(BF16)
        each(to_heads(step, above(step), mz), lambda c: c.start())
    mg_recv[mz] = nt(attended_grad, wfull[mz]).astype(BF16)
    normal, _ = normalize(resid[...])
    share = jnp.concatenate([in_part[c].astype(F32) for c in range(NC)], axis=1)
    share = share + jnp.where(mz == 0, rterm[...], 0.0)
    m.sp_send[...] = jnp.zeros((sh.small, D), F32)
    m.sp_send[0:E] = jnp.where(mz == 0, router_grad, 0.0)
    m.sp_send[E : E + 1] = jnp.sum(share * normal, axis=0, keepdims=True)
    m.sp_send[E + 1 : E + 2] = jnp.sum(share, axis=0, keepdims=True)

    B, BP = sh.share, sh.share_rows
    qg = ChipSum(sh.s_qg, m.qg_send, m.qg_pair, m.qg_recv)
    wg = ChipSum(sh.s_og, m.wg_send, m.wg_pair, m.wg_recv)
    lower = mz < Z // 2
    at_rows = pl.ds(pl.multiple_of(lax.rem(mz, Z // 2) * S, TILE), W)
    mixed_win = jnp.concatenate(
        [
            jnp.where(
                lower, mixed_all[p, at_rows][:, 0:L], mixed_all[p, at_rows][:, L : 2 * L]
            )
            for p in range(Z)
        ],
        axis=1,
    )
    wout_grad = tn(attended_grad, mixed_win)
    for e in range(E):
        m.wg_send[e % 2, e // 2, 0:B] = wout_grad[e * B : (e + 1) * B].astype(BF16)
    wg.start()
    bo_gather.start()
    for step in order:
        each(to_heads(step, 0, below(step)), lambda c: c.wait_recv())
    wg.cross()
    mixed_grad = m.mixed_grad
    put_together(mg_recv, mixed_grad)

    grads = [[], [], []]
    for h in range(sh.heads):
        mg = mixed_grad[:, h * HEAD_DIM : (h + 1) * HEAD_DIM]
        probs = probs_s[h]
        prob_grad = nt(mg, v_s[h])
        score_grad = (
            probs * (prob_grad - jnp.sum(prob_grad * probs, axis=1, keepdims=True))
        ).astype(BF16)
        grads[0].append((nn(score_grad, k_s[h]) * scale).astype(BF16))
        grads[1].append((tn(score_grad, q_s[h]) * scale).astype(BF16))
        grads[2].append(tn(probs.astype(BF16), mg).astype(BF16))
    projected_grad = jnp.concatenate(grads[0] + grads[1] + grads[2], axis=1)
    mix.finish()
    first_part = mix_part
    first = Scatter(sh.z_first, first_part, m.first_recv, m.first_pass)
    first_part[...] = nn(projected_grad, wqkv[...]).astype(BF16)
    first.start()

    qkv_grad = tn(first_low[...], projected_grad)
    for e in range(E):
        m.qg_send[e % 2, e // 2, 0:B] = qkv_grad[e * B : (e + 1) * B].astype(BF16)
    qg.start()
    normal, _ = normalize(pt[...].astype(F32))
    share = first_part[...].astype(F32)
    m.sp_send[E + 2 : E + 3] = jnp.sum(share * normal, axis=0, keepdims=True)
    m.sp_send[E + 3 : E + 4] = jnp.sum(share, axis=0, keepdims=True)
    smalls = SmallSum(sh.s_sp, m.sp_send, m.sp_pair, m.sp_half, m.sp_recv)
    smalls.start()
    first.relay()
    smalls.cross()

    bo_gather.relay()
    for step in bo_gather.rest():
        bo_gather.arrival(step)
    put_out(bo_all, outputs.block_out, range(Z))

    wz_send, wz_recv = m.wz_send, m.wz_recv
    total_w = wg.total()
    for position in range(Z):
        wz_send[position] = total_w[:, position * L : (position + 1) * L].astype(BF16)
    for step in order:
        to_depth(wz_send.at[above(step)], wz_recv.at[mz], sh.z_wz, step).start()
    zs_send, zs_recv = m.zs_send, m.zs_recv
    near = pl.ds(pl.multiple_of(sh.near(me), 128), sh.near_lanes)
    m.sp_total[...] = smalls.total()
    zs_send[...] = m.sp_total[:, near]
    for step in order:
        to_depth(zs_send, zs_recv.at[mz], sh.z_zs, step).start()

    normal, spread_scale = normalize(pt[window].astype(F32))
    first_grad = first.total()
    patch_grad = resid_win[...] + norm_back(normal, spread_scale, first_grad * g1)
    pg_all[mz] = patch_grad.astype(BF16)
    pg_gathers = []
    for kind, first_lane in ((sh.z_pg, 0), (sh.z_more, half)):
        cols = pl.ds(first_lane, half)
        pg_gathers.append(Gather(kind, pg_all, (tail, cols), (head, cols)))
    for pg_gather in pg_gathers:
        pg_gather.start()
    qg.cross()
    for pg_gather in pg_gathers:
        pg_gather.relay()
    total = qg.total()
    qkv_sum, wout_sum, small_sum = m.qkv_sum, m.wout_sum, m.small_sum
    for part in range(3):
        qkv_sum[part] = total[0:B, part * L : (part + 1) * L]
    store(qkv_sum, outputs.qkv_out)
    total_w = wz_send[mz].astype(F32)
    for step in order:
        to_depth(wz_send.at[0], wz_recv.at[below(step)], sh.z_wz, step).wait_recv()
        total_w = total_w + wz_recv[below(step)].astype(F32)
    wout_sum[...] = total_w[0:B]
    store(wout_sum, outputs.wout_out)
    small_sum[...] = zs_send[...]
    for step in order:
        to_depth(zs_send, zs_recv.at[below(step)], sh.z_zs, step).wait_recv()
        small_sum[...] += zs_recv[below(step)]
    store(small_sum, outputs.small_out)

    for step in (0,) + order:
        position = below(step)
        if step and not (relayed and step == 2):
            for pg_gather in pg_gathers:
                pg_gather.arrival(step)
        put_out(pg_all, outputs.patches_grad, [position])

    for step in range(1, Z):
        to_other(step).wait_send()

    to_plane(g_send.at[others], g_recv.at[others], sh.e_g, 1).wait_send()
    to_plane(x_send.at[others, common], x_recv.at[others, common], sh.e_x, 1).wait_send()
    if sh.split:
        rows = split_rows(mz)
        to_plane(x_send.at[others, rows], x_recv.at[others, rows], sh.e_xs, 1).wait_send()
    to_plane(gg_send.at[others], gg_home.at[others], sh.e_gg, 1).wait_send()
    to_plane(eo_send.at[others], eo_home.at[others], sh.e_eo, 1).wait_send()
    for c in range(NC):
        part = (others, slice(None), lanes(c))
        to_plane(ei_send.at[part], ei_home.at[part], sh.e_ei + c, 1).wait_send()
    for sent in ins + [first, qg, wg, smalls]:
        sent.finish()
    if sh.split:
        for strips_of in x_strips:
            strips_of.finish()
    for gather in [weights, mixing, bo_gather] + pg_gathers:
        gather.finish()
    for step in range(1, Z):
        each(to_heads(step, 0, mz), lambda c: c.wait_send())
        to_depth(wz_send.at[0], wz_recv.at[0], sh.z_wz, step).wait_send()
        to_depth(gz_send, gz_recv.at[0], sh.z_gz, step).wait_send()
        to_depth(zs_send, zs_recv.at[0], sh.z_zs, step).wait_send()
    for last in (2, 1):
        strip_copy(D // strip - last, outputs.up_out, (D // strip - last) % 2).wait()
        strip_copy(F // strip - last, outputs.down_out, 2 + (F // strip - last) % 2).wait()
    for copy, condition in stores:
        if condition is None:
            copy.wait()
        else:

            @pl.when(condition)
            def _():
                copy.wait()


def scratch_of(sh, F, in_count):
    E, Z, RP, R, D, NC = sh.experts, sh.depth, sh.padded, sh.rows, sh.width, sh.chunks
    CP, CL, CW, W = sh.slots, sh.slot_lanes, sh.chunk, sh.window
    B, BP, C = sh.share, sh.share_rows, sh.chips
    L, H = sh.local, sh.heads
    blocks = ((E, CP, D), BF16)
    dots = ((E, 8, CL), F32)
    rows = ((RP, D), BF16)
    part = ((NC, RP, CW), BF16)
    recv = ((NC, Z, W, CW), BF16)
    passing = ((NC, W, CW), BF16)
    every = ((Z, W, D), BF16)
    head = ((H, RP, HEAD_DIM), BF16)
    shapes = dict(
        gain1=((D,), F32),
        bias1=((D,), F32),
        gain2=((D,), F32),
        bias2=((D,), F32),
        router_t=((E, D), BF16),
        ids_row=((2, R), jnp.int32),
        noise_row=((2, R), F32),
        images_live=((1,), jnp.int32),
        patches=((R, D), BF16),
        out_grad=((R, D), BF16),
        up=((D, F), BF16),
        down=((F, D), BF16),
        wqkv=((3 * L, D), BF16),
        wfull=((Z, L, D), BF16),
        pt=rows,
        og=rows,
        first_low=rows,
        q_s=head,
        k_s=head,
        v_s=head,
        probs_s=((H, RP, RP), F32),
        mixed=((RP, L), BF16),
        mixed_all=((Z, sh.half_rows, 2 * L), BF16),
        resid=((RP, D), F32),
        second_low=rows,
        place=((RP, E * CP), BF16),
        x_send=blocks,
        x_recv=blocks,
        c_send=blocks,
        c_recv=blocks,
        g_send=dots,
        g_recv=dots,
        act=((E, CP, F), BF16),
        slope=((E, CP, F), BF16),
        delta=blocks,
        hid=((E, CP, F), BF16),
        eo_send=blocks,
        eo_home=blocks,
        ei_home=blocks,
        gg_send=dots,
        gg_home=dots,
        acc=((4, 128, max(F, D)), BF16),
        mix_part=rows,
        mix_recv=every,
        mix_pass=((W, D), BF16),
        in_part=part,
        in_recv=recv,
        in_pass=passing,
        first_recv=every,
        first_pass=((W, D), BF16),
        rterm=((RP, D), F32),
        resid_win=((W, D), F32),
        bo_all=every,
        pg_all=every,
        mg_send=((Z, W, L), BF16),
        mg_recv=((Z, W, L), BF16),
        mixed_grad=((RP, L), BF16),
        wz_send=((Z, BP, L), BF16),
        wz_recv=((Z, BP, L), BF16),
        gz_send=((8, RP), F32),
        gz_recv=((Z, 8, RP), F32),
        qg_send=((2, C, BP, 3 * L), BF16),
        qg_pair=((C, BP, 3 * L), BF16),
        qg_recv=((C, BP, 3 * L), BF16),
        wg_send=((2, C, BP, Z * L), BF16),
        wg_pair=((C, BP, Z * L), BF16),
        wg_recv=((C, BP, Z * L), BF16),
        sp_send=((sh.small, D), F32),
        sp_pair=((sh.small, D), F32),
        sp_half=((sh.small, D), F32),
        sp_total=((sh.small, D), F32),
        sp_recv=((C, sh.small, D), F32),
        qkv_sum=((3, B, L), F32),
        wout_sum=((B, L), F32),
        zs_send=((sh.small, sh.near_lanes), F32),
        zs_recv=((Z, sh.small, sh.near_lanes), F32),
        small_sum=((sh.small, sh.near_lanes), F32),
    )
    sems = dict(
        local_sem=4,
        in_sem=in_count,
        out_sem=4 * Z + 3,
        e_sem=sh.e_single * E + sh.e_kinds - sh.e_single,
        e_out=sh.e_kinds,
        z_sem=(sh.z_kinds, 2, Z),
        z_extra=(sh.z_kinds - sh.z_heads, 2, Z),
        s_sem=(sh.s_kinds, 2, Z),
        c_sem=(sh.s_kinds, 2, sh.chips),
    )
    scratch = {field: pltpu.VMEM(*shape) for field, shape in shapes.items()}
    for field, shape in sems.items():
        scratch[field] = pltpu.SemaphoreType.DMA(shape if isinstance(shape, tuple) else (shape,))
    return scratch


def outputs_kernel(sh, pieces, *refs):
    given, outs, held, made = refs[:7], refs[7:18], refs[18:25], refs[25:36]
    in_sem, out_sem = refs[36:]
    wout, small = held[5:]
    loads = [
        pltpu.make_async_copy(src, dst, in_sem.at[at])
        for at, (src, dst) in enumerate(zip(given[5:], (wout, small)))
    ]
    steps = []
    for src, through, ready, dst, number in zip(given, held, made, outs, pieces):
        rows = src.shape[0] // number
        for piece in range(number):
            at = pl.ds(piece * rows, rows)
            part = [ref if number == 1 else ref.at[at] for ref in (src, through, ready, dst)]
            load = pltpu.make_async_copy(part[0], part[1], in_sem.at[len(loads) + len(steps)])
            steps.append((load, part))
    for load in loads + [load for load, _ in steps]:
        load.start()
    for load in loads:
        load.wait()
    E, lanes = sh.experts, sh.near_lanes
    me = lax.axis_index("expert")
    begin = me * sh.share - sh.near(me)
    mine = pltpu.roll(small[...], lax.rem(lanes - begin, lanes), 1)[:, 0 : sh.share]
    made[5][...] = wout[...].T
    made[6][...] = mine[0:E]
    for at, gain in enumerate(made[7:]):
        gain[...] = mine[E + at]
    stores = []

    def store(src, dst):
        stores.append(pltpu.make_async_copy(src, dst, out_sem.at[len(stores)]))
        stores[-1].start()

    for src, dst in zip(made[5:], outs[5:]):
        store(src, dst)
    for load, (_, through, ready, dst) in steps:
        load.wait()
        if through.dtype == ready.dtype:
            store(through, dst)
        else:
            ready[...] = through[...].astype(ready.dtype)
            store(ready, dst)
    for copy in stores:
        copy.wait()


def on_device(
    mesh,
    patches,
    first_gain,
    first_bias,
    qkv_weight,
    out_weight,
    second_gain,
    second_bias,
    router_weight,
    up_weight,
    down_weight,
    expert_ids,
    router_noise,
    images_live,
    out_grad,
):
    row_count, model_width = patches.shape
    local_width = out_weight.shape[0]
    sh = Shapes(mesh, row_count, model_width, local_width)
    hidden_width = up_weight.shape[2]
    E, RP, D = sh.experts, sh.padded, sh.width
    anywhere = pl.BlockSpec(memory_space=pl.ANY)
    slots = E * sh.slots
    flops = 2 * (
        6 * slots * D * hidden_width
        + 3 * RP * D * 4 * local_width
        + 4 * slots * RP * D
        + 7 * sh.heads * RP * RP * HEAD_DIM
    )
    inputs = dict(
        gain1=first_gain,
        bias1=first_bias,
        gain2=second_gain,
        bias2=second_bias,
        router_t=router_weight.T,
        ids_row=expert_ids.T,
        noise_row=router_noise.T,
        images_live=images_live,
        wout=out_weight,
        out_grad=out_grad,
        patches=patches,
        wqkv=qkv_weight.transpose(1, 2, 0).reshape(3 * local_width, D),
        up=up_weight[0],
        down=down_weight[0],
    )
    outputs = dict(
        block_out=jax.ShapeDtypeStruct((RP, D), BF16),
        patches_grad=jax.ShapeDtypeStruct((RP, D), BF16),
        qkv_out=jax.ShapeDtypeStruct((3, sh.share, local_width), F32),
        wout_out=jax.ShapeDtypeStruct((sh.share, local_width), F32),
        small_out=jax.ShapeDtypeStruct((sh.small, sh.near_lanes), F32),
        up_out=jax.ShapeDtypeStruct((D, hidden_width), BF16),
        down_out=jax.ShapeDtypeStruct((hidden_width, D), BF16),
    )
    scratch = scratch_of(sh, hidden_width, len(inputs))
    fields = tuple(tuple(group) for group in (inputs, outputs, scratch))
    outs = pl.pallas_call(
        functools.partial(whole_kernel, sh, fields),
        out_shape=tuple(outputs.values()),
        in_specs=[anywhere] * len(inputs),
        out_specs=(anywhere,) * len(outputs),
        scratch_shapes=list(scratch.values()),
        compiler_params=pltpu.CompilerParams(
            collective_id=0, has_side_effects=True, vmem_limit_bytes=62 << 20
        ),
        cost_estimate=pl.CostEstimate(flops=flops, bytes_accessed=16 << 20, transcendentals=0),
        name="block",
    )(*inputs.values())
    block_out, patches_grad, qkv_grad, wout_grad, small, up_grad, down_grad = outs
    pieces = (1, 1, 1, 4, 4)
    wholes = (block_out[:row_count], patches_grad[:row_count], qkv_grad, up_grad, down_grad)
    inputs = wholes + (wout_grad, small)
    kinds = (BF16, F32, F32, F32, F32)
    results = tuple(jax.ShapeDtypeStruct(w.shape, kind) for w, kind in zip(wholes, kinds)) + (
        jax.ShapeDtypeStruct((local_width, sh.share), F32),
        jax.ShapeDtypeStruct((E, sh.share), F32),
    )
    results += (jax.ShapeDtypeStruct((sh.share,), F32),) * 4
    copies = sum(pieces)
    results = pl.pallas_call(
        functools.partial(outputs_kernel, sh, pieces),
        out_shape=results,
        in_specs=[anywhere] * len(inputs),
        out_specs=(anywhere,) * len(results),
        scratch_shapes=[pltpu.VMEM(w.shape, w.dtype) for w in inputs + results]
        + [pltpu.SemaphoreType.DMA((copies + 2,)), pltpu.SemaphoreType.DMA((copies + 6,))],
        compiler_params=pltpu.CompilerParams(vmem_limit_bytes=62 << 20),
        name="outputs",
    )(*inputs)
    block_out, patches_grad, qkv_grad, up_grad, down_grad, wout_grad, router_grad = results[:7]
    gain2_grad, bias2_grad, gain1_grad, bias1_grad = results[7:]
    return (
        block_out,
        patches_grad,
        gain1_grad,
        bias1_grad,
        qkv_grad.transpose(1, 0, 2),
        wout_grad,
        gain2_grad,
        bias2_grad,
        router_grad.T,
        up_grad[None],
        down_grad[None],
    )


def solution(mesh):
    placed = (
        P("expert", None),
        P(),
        P(),
        P(None, None, "tensor"),
        P("tensor", None),
        P(),
        P(),
        P(),
        P("expert", None, "tensor"),
        P("expert", "tensor", None),
        P("expert", None),
        P("expert", None),
        P("expert"),
        P("expert", None),
    )
    return jax.shard_map(
        functools.partial(on_device, mesh),
        mesh=mesh,
        in_specs=placed,
        out_specs=(
            P("expert", None),
            P("expert", None),
            P("expert"),
            P("expert"),
            P("expert", None, "tensor"),
            P("tensor", "expert"),
            P("expert"),
            P("expert"),
            P("expert", None),
            P("expert", None, "tensor"),
            P("expert", "tensor", None),
        ),
        check_vma=False,
    )
```
